32 devices in a mesh: rows: 8 (over z, y), grp: 4 (over x, core).
Axes of the slice: x: 2, y: 2, z: 4, core: 2. Of those that a mesh axis runs over, the one named last changes fastest.
Arguments:
- slab: bfloat16 [18432, 4096], P(('rows', 'grp')), may hold values from -6 to 6
- sketch: bfloat16 [4096, 128], replicated, may hold values from -0.09375 to 0.09375
Outputs:
- basis: float32 [18432, 128], P(('rows', 'grp'))
- projected: bfloat16 [4096, 128], P(('rows', 'grp'))
The draws below stay inside these ranges and needn't reach their ends.
All inputs are finite; a program needn't handle non-finite values.
Results may differ from the reference program's by a relative error of at most 0.0035.
Values sent between devices are 32-bit elements; how exact they have to be, the bound alone decides.
No kernel may reach another device: no remote copies, remote signals or barrier semaphores. Data moves between devices by JAX's collectives and lax.ppermute only.
A program may use at most 64 MiB of HBM per device.

```python
import jax
import jax.numpy as jnp

D = 4096
RANK = 128
ROWS = 18432


def with_spikes(entries, key, source, target, shards_of, factor):
    owner, partner = [(jnp.arange(entries.shape[axis_at]) // (entries.shape[axis_at] // shards_of)).reshape([-1 if axis == axis_at else 1 for axis in range(entries.ndim)]) for axis_at in (source, target)]
    chosen = jax.random.permutation(key, shards_of)[partner]
    strong = (owner == chosen) | (owner == (partner + shards_of // 2) % shards_of)
    return jnp.where(strong, factor * entries, entries)


def steps_of(own_key, shape, pieces, low, high):
    level, own = 1.0, jax.random.fold_in(own_key, 6)
    for dim, shards_of in pieces:
        steps = jnp.exp(jax.random.uniform(jax.random.fold_in(own, dim), (shards_of,), jnp.float32, low / len(pieces), high / len(pieces)))
        level = level * jnp.repeat(steps, shape[dim] // shards_of).reshape([-1 if axis == dim else 1 for axis in range(len(shape))])
    return level


def bell_draw(stream_key, dims, scale, bound, shards=(), dtype=jnp.bfloat16):
    entries = jax.random.normal(stream_key, dims, jnp.float32) * scale
    if len(shards) > 0:
        entries = steps_of(stream_key, dims, shards, -0.22, 0.18) * entries
    return jnp.clip(entries, min=-bound, max=bound).astype(dtype)


def noise_with(own_key, dims, spread, most, shards, heavy, kind=jnp.bfloat16):
    result = spread * jax.random.normal(own_key, dims, jnp.float32)
    if shards:
        result = result * steps_of(own_key, dims, shards, -0.22, 0.18)
    return jnp.clip(with_spikes(result, jax.random.fold_in(own_key, 3), *heavy), -most, most).astype(kind)


def setup_inputs(seed: int = 0) -> dict:
    arg_keys = jax.random.split(jax.random.key(seed), 3)
    return {
        "slab": noise_with(arg_keys[0], (ROWS, D), 1.0, 6.0, ((0, 32),), (0, 1, 32, 2.75)),
        "sketch": bell_draw(arg_keys[1], (D, RANK), D ** -0.5, 0.09375),
    }


def orth(matrix):
    factor_q, factor_r = jnp.linalg.qr(matrix)
    signs = jnp.sign(jnp.diagonal(factor_r))
    return factor_q * signs[None, :]

def reference(slab, sketch):
    first = jnp.dot(slab.astype(jnp.float32), sketch.astype(jnp.float32), preferred_element_type=jnp.float32)
    basis_one = orth(first)
    low_one = basis_one.astype(jnp.bfloat16)
    final = jnp.dot(slab.T.astype(jnp.float32), low_one.astype(jnp.float32), preferred_element_type=jnp.float32)
    basis = basis_one * jnp.sqrt(jnp.float32(ROWS))
    projected = (final * jnp.sqrt(jnp.float32(D) / jnp.float32(ROWS))).astype(jnp.bfloat16)
    return (basis, projected)
```

```python
import functools

import jax
import jax.numpy as jnp
from jax import lax
from jax.experimental import pallas as pl
from jax.experimental.pallas import tpu as pltpu
from jax.sharding import PartitionSpec as P

AXES = ("rows", "grp")
HIGHEST = lax.Precision.HIGHEST
LANES = 128
VMEM_LIMIT = 40 * 1024 * 1024


def sketch_kernel(slab_ref, sketch_ref, first_ref, split_ref, gram_ref, acc_ref):
    step = pl.program_id(0)
    part = jnp.dot(slab_ref[...], sketch_ref[...], preferred_element_type=jnp.float32)

    @pl.when(step == 0)
    def _():
        acc_ref[...] = part

    @pl.when(step > 0)
    def _():
        acc_ref[...] += part

    @pl.when(step == pl.num_programs(0) - 1)
    def _():
        first = acc_ref[...]
        first_ref[...] = first
        gram_ref[...] = lax.dot_general(
            first, first, (((0,), (0,)), ((), ())),
            precision=HIGHEST, preferred_element_type=jnp.float32,
        )
        high = first.astype(jnp.bfloat16)
        low = (first - high.astype(jnp.float32)).astype(jnp.bfloat16)
        split_ref[...] = jnp.concatenate([high.T, low.T], axis=0)


def sketch_call(slab, sketch):
    rows, width = slab.shape
    rank = sketch.shape[1]
    block = 512
    return pl.pallas_call(
        sketch_kernel,
        grid=(width // block,),
        in_specs=[
            pl.BlockSpec((rows, block), lambda k: (0, k)),
            pl.BlockSpec((block, rank), lambda k: (k, 0)),
        ],
        out_specs=[
            pl.BlockSpec((rows, rank), lambda k: (0, 0)),
            pl.BlockSpec((2 * rank, rows), lambda k: (0, 0)),
            pl.BlockSpec((rank, rank), lambda k: (0, 0)),
        ],
        out_shape=[
            jax.ShapeDtypeStruct((rows, rank), jnp.float32),
            jax.ShapeDtypeStruct((2 * rank, rows), jnp.bfloat16),
            jax.ShapeDtypeStruct((rank, rank), jnp.float32),
        ],
        scratch_shapes=[pltpu.VMEM((rows, rank), jnp.float32)],
        compiler_params=pltpu.CompilerParams(vmem_limit_bytes=VMEM_LIMIT),
        cost_estimate=pl.CostEstimate(
            flops=2 * rows * width * rank, bytes_accessed=rows * width * 2, transcendentals=0
        ),
        name="sketch_rows",
    )(slab, sketch)


def project_kernel(me_ref, split_ref, slab_ref, keep_ref, send_ref, block_ref):
    rank = keep_ref.shape[0] * keep_ref.shape[4]
    half = rank // 2
    both = jnp.dot(split_ref[...], slab_ref[...], preferred_element_type=jnp.float32)
    block_ref[...] = both[:rank] + both[rank:]
    low = lax.rem(me_ref[0], 4)
    for x in range(2):
        for core, out in ((0, keep_ref), (1, send_ref)):
            at = pl.multiple_of(lax.bitwise_xor(low, 2 * x + core) * LANES, LANES)
            out[0, x, 0, 0] = block_ref[:half, pl.ds(at, LANES)]
            out[1, x, 0, 0] = block_ref[half:, pl.ds(at, LANES)]


def project_call(owner, split, slab):
    rows, width = slab.shape
    rank = split.shape[0] // 2
    block = 4 * LANES
    steps = width // block
    out_block = pl.BlockSpec((2, 2, 1, 1, rank // 2, LANES), lambda q, me: (0, 0, q % 2, q // 2, 0, 0))
    out_shape = jax.ShapeDtypeStruct((2, 2, 2, steps // 2, rank // 2, LANES), jnp.float32)
    return pl.pallas_call(
        project_kernel,
        grid_spec=pltpu.PrefetchScalarGridSpec(
            num_scalar_prefetch=1,
            grid=(steps,),
            in_specs=[
                pl.BlockSpec((2 * rank, rows), lambda q, me: (0, 0)),
                pl.BlockSpec((rows, block), lambda q, me: (0, lax.bitwise_xor(me[0] // 4, q))),
            ],
            out_specs=[out_block, out_block],
            scratch_shapes=[pltpu.VMEM((rank, block), jnp.float32)],
        ),
        out_shape=[out_shape, out_shape],
        compiler_params=pltpu.CompilerParams(vmem_limit_bytes=VMEM_LIMIT),
        cost_estimate=pl.CostEstimate(
            flops=4 * rows * width * rank, bytes_accessed=rows * width * 2, transcendentals=0
        ),
        name="project_rows",
    )(owner, split, slab)


def lane(block, at):
    return jnp.broadcast_to(block[:, at : at + 1], block.shape)


def sublane(block, at):
    return jnp.broadcast_to(block[at : at + 1, :], block.shape)


def inverse_factor(gram_ref, inverse_ref):
    size = gram_ref.shape[0]
    blocks = size // 8
    left = [gram_ref[8 * i : 8 * i + 8, :] for i in range(blocks)]
    row_at = lax.broadcasted_iota(jnp.int32, (8, size), 0)
    lane_at = lax.broadcasted_iota(jnp.int32, (8, size), 1)
    right = [jnp.where(lane_at == row_at + 8 * i, 1.0, 0.0).astype(jnp.float32) for i in range(blocks)]
    for p in range(blocks):
        column = [lane(left[p], 8 * p + k) for k in range(8)]
        entry = {(r, c): sublane(column[c], r) for c in range(8) for r in range(c, 8)}
        scale, lower = [], {}
        for k in range(8):
            scale.append(lax.rsqrt(entry[k, k]))
            for r in range(k + 1, 8):
                lower[r, k] = entry[r, k] * scale[k]
            for c in range(k + 1, 8):
                for r in range(c, 8):
                    entry[r, c] = entry[r, c] - lower[r, k] * lower[c, k]
        tops, sides = [], []
        for k in range(8):
            top, side = sublane(left[p], k), sublane(right[p], k)
            for j in range(k):
                top = top - lower[k, j] * tops[j]
                side = side - lower[k, j] * sides[j]
            tops.append(top * scale[k])
            sides.append(side * scale[k])
        result = sides[0]
        for k in range(1, 8):
            result = jnp.where(row_at == k, sides[k], result)
        inverse_ref[8 * p : 8 * p + 8, :] = result
        for i in range(p + 1, blocks):
            weights = []
            for k in range(8):
                weight = lane(left[i], 8 * p + k)
                for j in range(k):
                    weight = weight - lower[k, j] * weights[j]
                weights.append(weight * scale[k])
            for k in range(8):
                left[i] = left[i] - weights[k] * tops[k]
                right[i] = right[i] - weights[k] * sides[k]


def basis_kernel(factor, gram_ref, first_ref, inverse_ref, basis_ref):
    inverse_factor(gram_ref, inverse_ref)
    one = lax.dot_general(
        first_ref[...], inverse_ref[...], (((1,), (1,)), ((), ())),
        precision=HIGHEST, preferred_element_type=jnp.float32,
    )
    basis_ref[...] = one * factor


def basis_call(gram, first, total_rows):
    rows, rank = first.shape
    return pl.pallas_call(
        functools.partial(basis_kernel, float(total_rows) ** 0.5),
        out_shape=[
            jax.ShapeDtypeStruct((rank, rank), jnp.float32),
            jax.ShapeDtypeStruct((rows, rank), jnp.float32),
        ],
        compiler_params=pltpu.CompilerParams(vmem_limit_bytes=VMEM_LIMIT),
        cost_estimate=pl.CostEstimate(
            flops=4000000000, bytes_accessed=rows * rank * 8, transcendentals=rank
        ),
        name="basis_rows",
    )(gram, first)


def final_kernel(factor, inverse_ref, sums_ref, out_ref):
    result = jnp.dot(
        inverse_ref[...], sums_ref[...], precision=HIGHEST, preferred_element_type=jnp.float32
    )
    out_ref[...] = (result.T * factor).astype(out_ref.dtype)


def final_call(inverse, sums, factor):
    rank, own = sums.shape
    return pl.pallas_call(
        functools.partial(final_kernel, factor),
        out_shape=jax.ShapeDtypeStruct((own, rank), jnp.bfloat16),
        compiler_params=pltpu.CompilerParams(vmem_limit_bytes=VMEM_LIMIT),
        name="final_rows",
    )(inverse, sums)


def local(slab, sketch):
    rows_loc, width = slab.shape
    devices_all = lax.axis_size(AXES)
    own = width // devices_all
    bits = devices_all.bit_length() - 1
    low_bits = bits - ((width // LANES).bit_length() - 1)
    total_rows = rows_loc * devices_all
    me = lax.axis_index(AXES)

    def swap(array, bit):
        pairs = [(i, i ^ (1 << bit)) for i in range(devices_all)]
        return lax.ppermute(array, AXES, pairs)

    first, split, gram = sketch_call(slab, sketch)
    owner = lax.shift_right_logical(me, low_bits).astype(jnp.int32).reshape(1)
    keep, send = project_call(owner, split, slab)

    for bit in range(bits):
        gram = gram + swap(gram, bit)
    inverse, basis = basis_call(gram, first, total_rows)

    got = swap(send, low_bits)
    got_a = swap(keep[0, 1] + got[0, 1], low_bits + 1)
    got_b = swap(keep[1, :, 1] + got[1, :, 1], low_bits + 2)
    part_a = keep[0, 0] + got[0, 0]
    part_b = keep[1, :, 0] + got[1, :, 0]
    got_a2 = swap(part_a[1] + got_a[1], low_bits + 2)
    got_b2 = swap(part_b[1] + got_b[1], low_bits + 1)
    sums = jnp.concatenate(
        [part_a[0] + got_a[0] + got_a2, part_b[0] + got_b[0] + got_b2], axis=1
    )
    bit = low_bits + 3
    sums = sums.reshape(sums.shape[0] // 2, 2, *sums.shape[1:])
    sums = sums[:, 0] + swap(sums[:, 1], bit)
    sums = sums[0] + swap(sums[1], bit + 1)
    for bit in reversed(range(low_bits)):
        half = sums.shape[1] // 2
        mine = lax.rem(lax.shift_right_logical(me, bit), 2) == 1
        left, right = sums[:, :half], sums[:, half:]
        sums = jnp.where(mine, right, left) + swap(jnp.where(mine, left, right), bit)
    projected = final_call(inverse, sums, (float(width) / float(total_rows)) ** 0.5)
    return (basis, projected)


def solution(mesh):
    return jax.shard_map(
        local,
        mesh=mesh,
        in_specs=(P(AXES, None), P()),
        out_specs=(P(AXES, None), P(AXES, None)),
        check_vma=False,
    )
```

```python
import functools

import jax
import jax.numpy as jnp
from jax import lax
from jax.experimental import pallas as pl
from jax.experimental.pallas import tpu as pltpu
from jax.sharding import PartitionSpec as P

AXES = ("rows", "grp")
HIGHEST = lax.Precision.HIGHEST
LANES = 128
VMEM_LIMIT = 40 * 1024 * 1024
ROWS_VMEM = 40 * 1024 * 1024
GRAM_BITS = 5


CHUNKS = 4


def rows_kernel(
    me_ref, slab_hbm, sketch_hbm, first_ref, gram_ref, keep_ref, send_ref,
    slab_ref, sketch_ref, split_ref, slab_sem, sketch_sem,
):
    rows, width = slab_ref.shape
    rank = sketch_ref.shape[1]
    step = width // CHUNKS
    copies = []
    for k in range(CHUNKS):
        at = pl.ds(k * step, step)
        copies.append((
            pltpu.make_async_copy(sketch_hbm.at[at, :], sketch_ref.at[at, :], sketch_sem.at[k]),
            pltpu.make_async_copy(slab_hbm.at[:, at], slab_ref.at[:, at], slab_sem.at[k]),
        ))
    for pair in copies:
        for copy in pair:
            copy.start()
    for k in range(CHUNKS):
        for copy in copies[k]:
            copy.wait()
        at = pl.ds(k * step, step)
        part = jnp.dot(slab_ref[:, at], sketch_ref[at, :], preferred_element_type=jnp.float32)
        if k == 0:
            first_ref[...] = part
        else:
            first_ref[...] += part
    first = first_ref[...]
    turned = first.T
    high = turned.astype(jnp.bfloat16)
    split_ref[:rank] = high
    split_ref[rank:] = (turned - high.astype(jnp.float32)).astype(jnp.bfloat16)
    gram_ref[...] = jnp.dot(turned, first, precision=HIGHEST, preferred_element_type=jnp.float32)
    odd = lax.rem(me_ref[0], 2) == 1
    for q in range(width // (2 * LANES)):
        at = pl.ds(q * 2 * LANES, 2 * LANES)
        both = jnp.dot(split_ref[...], slab_ref[:, at], preferred_element_type=jnp.float32)
        sums = both[:rank] + both[rank:]
        even_part, odd_part = sums[:, :LANES], sums[:, LANES:]
        keep_ref[q % 4, q // 4] = jnp.where(odd, odd_part, even_part)
        send_ref[q % 4, q // 4] = jnp.where(odd, even_part, odd_part)


def rows_call(owner, slab, sketch):
    rows, width = slab.shape
    rank = sketch.shape[1]
    blocks = (4, width // (8 * LANES), rank, LANES)
    vmem = pl.BlockSpec(memory_space=pltpu.VMEM)
    return pl.pallas_call(
        rows_kernel,
        in_specs=[
            pl.BlockSpec(memory_space=pltpu.SMEM),
            pl.BlockSpec(memory_space=pltpu.HBM),
            pl.BlockSpec(memory_space=pltpu.HBM),
        ],
        out_specs=[vmem] * 4,
        out_shape=[
            jax.ShapeDtypeStruct((rows, rank), jnp.float32),
            jax.ShapeDtypeStruct((rank, rank), jnp.float32),
            jax.ShapeDtypeStruct(blocks, jnp.float32),
            jax.ShapeDtypeStruct(blocks, jnp.float32),
        ],
        scratch_shapes=[
            pltpu.VMEM((rows, width), jnp.bfloat16),
            pltpu.VMEM((width, rank), jnp.bfloat16),
            pltpu.VMEM((2 * rank, rows), jnp.bfloat16),
            pltpu.SemaphoreType.DMA((CHUNKS,)),
            pltpu.SemaphoreType.DMA((CHUNKS,)),
        ],
        compiler_params=pltpu.CompilerParams(vmem_limit_bytes=ROWS_VMEM),
        cost_estimate=pl.CostEstimate(
            flops=6 * rows * width * rank, bytes_accessed=rows * width * 2, transcendentals=0
        ),
        name="project_rows",
    )(
        owner,
        pltpu.with_memory_space_constraint(slab, pltpu.HBM),
        pltpu.with_memory_space_constraint(sketch, pltpu.HBM),
    )


def lane(block, at):
    return jnp.broadcast_to(block[:, at : at + 1], block.shape)


def sublane(block, at):
    return jnp.broadcast_to(block[at : at + 1, :], block.shape)


def inverse_factor(gram_ref, inverse_ref):
    size = gram_ref.shape[0]
    blocks = size // 8
    left = [gram_ref[8 * i : 8 * i + 8, :] for i in range(blocks)]
    row_at = lax.broadcasted_iota(jnp.int32, (8, size), 0)
    lane_at = lax.broadcasted_iota(jnp.int32, (8, size), 1)
    right = [jnp.where(lane_at == row_at + 8 * i, 1.0, 0.0).astype(jnp.float32) for i in range(blocks)]
    for p in range(blocks):
        column = [lane(left[p], 8 * p + k) for k in range(8)]
        entry = {(r, c): sublane(column[c], r) for c in range(8) for r in range(c, 8)}
        scale, lower = [], {}
        for k in range(8):
            scale.append(lax.rsqrt(entry[k, k]))
            for r in range(k + 1, 8):
                lower[r, k] = entry[r, k] * scale[k]
            for c in range(k + 1, 8):
                for r in range(c, 8):
                    entry[r, c] = entry[r, c] - lower[r, k] * lower[c, k]
        tops, sides = [], []
        for k in range(8):
            top, side = sublane(left[p], k), sublane(right[p], k)
            for j in range(k):
                top = top - lower[k, j] * tops[j]
                side = side - lower[k, j] * sides[j]
            tops.append(top * scale[k])
            sides.append(side * scale[k])
        result = sides[0]
        for k in range(1, 8):
            result = jnp.where(row_at == k, sides[k], result)
        inverse_ref[8 * p : 8 * p + 8, :] = result
        for i in range(p + 1, blocks):
            weights = []
            for k in range(8):
                weight = lane(left[i], 8 * p + k)
                for j in range(k):
                    weight = weight - lower[k, j] * weights[j]
                weights.append(weight * scale[k])
            for k in range(8):
                left[i] = left[i] - weights[k] * tops[k]
                right[i] = right[i] - weights[k] * sides[k]


def basis_kernel(factor, gram_ref, first_ref, inverse_ref, basis_ref):
    inverse_factor(gram_ref, inverse_ref)
    one = lax.dot_general(
        first_ref[...], inverse_ref[...], (((1,), (1,)), ((), ())),
        precision=HIGHEST, preferred_element_type=jnp.float32,
    )
    basis_ref[...] = one * factor


def basis_call(gram, first, total_rows):
    rows, rank = first.shape
    return pl.pallas_call(
        functools.partial(basis_kernel, float(total_rows) ** 0.5),
        out_shape=[
            jax.ShapeDtypeStruct((rank, rank), jnp.float32),
            jax.ShapeDtypeStruct((rows, rank), jnp.float32),
        ],
        compiler_params=pltpu.CompilerParams(vmem_limit_bytes=VMEM_LIMIT),
        cost_estimate=pl.CostEstimate(
            flops=4000000000, bytes_accessed=rows * rank * 8, transcendentals=rank
        ),
        name="basis_rows",
    )(gram, first)


def final_kernel(factor, inverse_ref, sums_ref, out_ref):
    result = jnp.dot(
        inverse_ref[...], sums_ref[...], precision=HIGHEST, preferred_element_type=jnp.float32
    )
    out_ref[...] = (result.T * factor).astype(out_ref.dtype)


def final_call(inverse, sums, factor):
    rank, own = sums.shape
    return pl.pallas_call(
        functools.partial(final_kernel, factor),
        out_shape=jax.ShapeDtypeStruct((own, rank), jnp.bfloat16),
        compiler_params=pltpu.CompilerParams(vmem_limit_bytes=VMEM_LIMIT),
        name="final_rows",
    )(inverse, sums)


def local(slab, sketch):
    rows_loc, width = slab.shape
    devices_all = lax.axis_size(AXES)
    own = width // devices_all
    bits = devices_all.bit_length() - 1
    low_bits = bits - ((width // LANES).bit_length() - 1)
    total_rows = rows_loc * devices_all
    me = lax.axis_index(AXES)

    def swap(array, bit):
        pairs = [(i, i ^ (1 << bit)) for i in range(devices_all)]
        return lax.ppermute(array, AXES, pairs)

    def spread(array, shift, count):
        mask = ((1 << count) - 1) << shift
        groups = [
            [base | (i << shift) for i in range(1 << count)]
            for base in range(devices_all) if base & mask == 0
        ]
        return lax.all_to_all(
            array, AXES, split_axis=0, concat_axis=0, axis_index_groups=groups, tiled=True
        )

    owner = lax.shift_right_logical(me, low_bits).astype(jnp.int32).reshape(1)
    first, gram, keep, send = rows_call(owner, slab, sketch)
    rank = first.shape[1]

    parts = 1 << GRAM_BITS
    share = spread(gram, 0, GRAM_BITS).reshape(parts, rank // parts, rank).sum(axis=0)
    for bit in range(GRAM_BITS, bits):
        share = share + swap(share, bit)
    gram = spread(jnp.tile(share, (parts, 1)), 0, GRAM_BITS)
    inverse, basis = basis_call(gram, first, total_rows)

    kept = keep + swap(send, low_bits)
    kept = spread(kept, low_bits + 1, 2).sum(axis=0)
    sums = spread(kept, low_bits + 3, 2).sum(axis=0)
    for bit in reversed(range(low_bits)):
        half = sums.shape[1] // 2
        mine = lax.rem(lax.shift_right_logical(me, bit), 2) == 1
        left, right = sums[:, :half], sums[:, half:]
        sums = jnp.where(mine, right, left) + swap(jnp.where(mine, left, right), bit)
    projected = final_call(inverse, sums, (float(width) / float(total_rows)) ** 0.5)
    return (basis, projected)


def solution(mesh):
    return jax.shard_map(
        local,
        mesh=mesh,
        in_specs=(P(AXES, None), P()),
        out_specs=(P(AXES, None), P(AXES, None)),
        check_vma=False,
    )
```

```python
import functools

import jax
import jax.numpy as jnp
from jax import lax
from jax.experimental import pallas as pl
from jax.experimental.pallas import tpu as pltpu
from jax.sharding import PartitionSpec as P

AXES = ("rows", "grp")
HIGHEST = lax.Precision.HIGHEST
LANES = 128
VMEM_LIMIT = 40 * 1024 * 1024


CHUNKS = 4


def sketch_kernel(
    slab_hbm, sketch_hbm, slab_ref, first_ref, split_ref, gram_ref, sketch_ref, slab_sem, sketch_sem
):
    width, rank = sketch_ref.shape
    step = width // CHUNKS
    copies = []
    for k in range(CHUNKS):
        at = pl.ds(k * step, step)
        copies.append((
            pltpu.make_async_copy(sketch_hbm.at[at, :], sketch_ref.at[at, :], sketch_sem.at[k]),
            pltpu.make_async_copy(slab_hbm.at[:, at], slab_ref.at[:, at], slab_sem.at[k]),
        ))
    for pair in copies:
        for copy in pair:
            copy.start()
    for k in range(CHUNKS):
        for copy in copies[k]:
            copy.wait()
        at = pl.ds(k * step, step)
        part = jnp.dot(slab_ref[:, at], sketch_ref[at, :], preferred_element_type=jnp.float32)
        if k == 0:
            first_ref[...] = part
        else:
            first_ref[...] += part
    first = first_ref[...]
    turned = first.T
    gram_ref[...] = jnp.dot(turned, first, precision=HIGHEST, preferred_element_type=jnp.float32)
    high = turned.astype(jnp.bfloat16)
    split_ref[:rank] = high
    split_ref[rank:] = (turned - high.astype(jnp.float32)).astype(jnp.bfloat16)


def sketch_call(slab, sketch):
    rows, width = slab.shape
    rank = sketch.shape[1]
    return pl.pallas_call(
        sketch_kernel,
        in_specs=[pl.BlockSpec(memory_space=pltpu.HBM)] * 2,
        out_specs=[pl.BlockSpec(memory_space=pltpu.VMEM)] * 4,
        out_shape=[
            jax.ShapeDtypeStruct((rows, width), jnp.bfloat16),
            jax.ShapeDtypeStruct((rows, rank), jnp.float32),
            jax.ShapeDtypeStruct((2 * rank, rows), jnp.bfloat16),
            jax.ShapeDtypeStruct((rank, rank), jnp.float32),
        ],
        scratch_shapes=[
            pltpu.VMEM((width, rank), jnp.bfloat16),
            pltpu.SemaphoreType.DMA((CHUNKS,)),
            pltpu.SemaphoreType.DMA((CHUNKS,)),
        ],
        compiler_params=pltpu.CompilerParams(vmem_limit_bytes=VMEM_LIMIT),
        cost_estimate=pl.CostEstimate(
            flops=2 * rows * width * rank, bytes_accessed=rows * width * 2, transcendentals=0
        ),
        name="sketch_rows",
    )(
        pltpu.with_memory_space_constraint(slab, pltpu.HBM),
        pltpu.with_memory_space_constraint(sketch, pltpu.HBM),
    )


def project_kernel(sibling, owner_ref, split_ref, slab_ref, out_ref):
    rank = out_ref.shape[1]
    owner = owner_ref[0]
    core = lax.bitwise_and(owner, 1)
    wanted = lax.bitwise_xor(core, sibling)
    mine = lax.shift_right_logical(owner, 1)

    def columns(q):
        at = pl.multiple_of((2 * q + wanted) * LANES, LANES)
        return slab_ref[:, pl.ds(at, LANES)]

    def place(q):
        away = lax.bitwise_xor(mine, q)
        bit = [lax.bitwise_and(lax.shift_right_logical(away, i), 1) for i in range(4)]
        straight = 8 * bit[0] + 4 * bit[1] + 2 * bit[2] + bit[3]
        turned = 8 * bit[1] + 4 * bit[0] + 2 * bit[3] + bit[2]
        return jnp.where(wanted == 0, straight, turned)

    for q in range(0, out_ref.shape[0], 2):
        both = jnp.dot(
            split_ref[...], jnp.concatenate([columns(q), columns(q + 1)], axis=1),
            preferred_element_type=jnp.float32,
        )
        sums = both[:rank] + both[rank:]
        out_ref[place(q)] = sums[:, :LANES]
        out_ref[place(q + 1)] = sums[:, LANES:]


def project_call(owner, split, slab, sibling):
    rows, width = slab.shape
    rank = split.shape[0] // 2
    vmem = pl.BlockSpec(memory_space=pltpu.VMEM)
    return pl.pallas_call(
        functools.partial(project_kernel, sibling),
        in_specs=[pl.BlockSpec(memory_space=pltpu.SMEM), vmem, vmem],
        out_specs=vmem,
        out_shape=jax.ShapeDtypeStruct((width // (2 * LANES), rank, LANES), jnp.float32),
        compiler_params=pltpu.CompilerParams(vmem_limit_bytes=VMEM_LIMIT),
        cost_estimate=pl.CostEstimate(
            flops=2 * rows * width * rank, bytes_accessed=rows * width, transcendentals=0
        ),
        name="project_sibling" if sibling else "project_own",
    )(owner, split, slab)


def lane(block, at):
    return jnp.broadcast_to(block[:, at : at + 1], block.shape)


def sublane(block, at):
    return jnp.broadcast_to(block[at : at + 1, :], block.shape)


def inverse_factor(gram_ref, inverse_ref):
    size = gram_ref.shape[0]
    blocks = size // 8
    left = [gram_ref[8 * i : 8 * i + 8, :] for i in range(blocks)]
    row_at = lax.broadcasted_iota(jnp.int32, (8, size), 0)
    lane_at = lax.broadcasted_iota(jnp.int32, (8, size), 1)
    right = [jnp.where(lane_at == row_at + 8 * i, 1.0, 0.0).astype(jnp.float32) for i in range(blocks)]
    for p in range(blocks):
        column = [lane(left[p], 8 * p + k) for k in range(8)]
        entry = {(r, c): sublane(column[c], r) for c in range(8) for r in range(c, 8)}
        scale, lower = [], {}
        for k in range(8):
            scale.append(lax.rsqrt(entry[k, k]))
            for r in range(k + 1, 8):
                lower[r, k] = entry[r, k] * scale[k]
            for c in range(k + 1, 8):
                for r in range(c, 8):
                    entry[r, c] = entry[r, c] - lower[r, k] * lower[c, k]
        tops, sides = [], []
        for k in range(8):
            top, side = sublane(left[p], k), sublane(right[p], k)
            for j in range(k):
                top = top - lower[k, j] * tops[j]
                side = side - lower[k, j] * sides[j]
            tops.append(top * scale[k])
            sides.append(side * scale[k])
        result = sides[0]
        for k in range(1, 8):
            result = jnp.where(row_at == k, sides[k], result)
        inverse_ref[8 * p : 8 * p + 8, :] = result
        for i in range(p + 1, blocks):
            weights = []
            for k in range(8):
                weight = lane(left[i], 8 * p + k)
                for j in range(k):
                    weight = weight - lower[k, j] * weights[j]
                weights.append(weight * scale[k])
            for k in range(8):
                left[i] = left[i] - weights[k] * tops[k]
                right[i] = right[i] - weights[k] * sides[k]


def basis_kernel(factor, gram_ref, first_ref, inverse_ref, basis_ref):
    inverse_factor(gram_ref, inverse_ref)
    one = lax.dot_general(
        first_ref[...], inverse_ref[...], (((1,), (1,)), ((), ())),
        precision=HIGHEST, preferred_element_type=jnp.float32,
    )
    basis_ref[...] = one * factor


def basis_call(gram, first, total_rows):
    rows, rank = first.shape
    return pl.pallas_call(
        functools.partial(basis_kernel, float(total_rows) ** 0.5),
        out_shape=[
            jax.ShapeDtypeStruct((rank, rank), jnp.float32),
            jax.ShapeDtypeStruct((rows, rank), jnp.float32),
        ],
        compiler_params=pltpu.CompilerParams(vmem_limit_bytes=VMEM_LIMIT),
        cost_estimate=pl.CostEstimate(
            flops=4000000000, bytes_accessed=rows * rank * 8, transcendentals=rank
        ),
        name="basis_rows",
    )(gram, first)


def final_kernel(factor, inverse_ref, sums_ref, out_ref):
    result = jnp.dot(
        inverse_ref[...], sums_ref[...], precision=HIGHEST, preferred_element_type=jnp.float32
    )
    out_ref[...] = (result.T * factor).astype(out_ref.dtype)


def final_call(inverse, sums, factor):
    rank, own = sums.shape
    return pl.pallas_call(
        functools.partial(final_kernel, factor),
        out_shape=jax.ShapeDtypeStruct((own, rank), jnp.bfloat16),
        compiler_params=pltpu.CompilerParams(vmem_limit_bytes=VMEM_LIMIT),
        name="final_rows",
    )(inverse, sums)


def local(slab, sketch):
    rows_loc, width = slab.shape
    devices_all = lax.axis_size(AXES)
    own = width // devices_all
    bits = devices_all.bit_length() - 1
    low_bits = bits - ((width // LANES).bit_length() - 1)
    total_rows = rows_loc * devices_all
    me = lax.axis_index(AXES)

    def swap(array, bit):
        pairs = [(i, i ^ (1 << bit)) for i in range(devices_all)]
        return lax.ppermute(array, AXES, pairs)

    def exchange(array, bit, other):
        pairs = [(i, i ^ (1 << (other if (i >> low_bits) & 1 else bit))) for i in range(devices_all)]
        return lax.ppermute(array, AXES, pairs)

    core, x, y, z, zz = range(low_bits, low_bits + 5)
    rounds = [(core, core), (x, y), (y, x), (z, zz), (zz, z)]

    owner = lax.shift_right_logical(me, low_bits).astype(jnp.int32).reshape(1)
    slab_near, first, split, gram = sketch_call(slab, sketch)
    gram = gram + exchange(gram, *rounds[0])
    got = exchange(project_call(owner, split, slab_near, 1), *rounds[0])
    sums = project_call(owner, split, slab_near, 0)
    for pair in rounds[1:]:
        gram = gram + exchange(gram, *pair)
        sums = sums + got
        half = sums.shape[0] // 2
        got = exchange(sums[half:], *pair)
        sums = sums[:half]
    sums = (sums + got)[0]
    for bit in range(low_bits):
        gram = gram + swap(gram, bit)
    inverse, basis = basis_call(gram, first, total_rows)
    for bit in reversed(range(low_bits)):
        half = sums.shape[1] // 2
        mine = lax.rem(lax.shift_right_logical(me, bit), 2) == 1
        left, right = sums[:, :half], sums[:, half:]
        sums = jnp.where(mine, right, left) + swap(jnp.where(mine, left, right), bit)
    projected = final_call(inverse, sums, (float(width) / float(total_rows)) ** 0.5)
    return (basis, projected)


def solution(mesh):
    return jax.shard_map(
        local,
        mesh=mesh,
        in_specs=(P(AXES, None), P()),
        out_specs=(P(AXES, None), P(AXES, None)),
        check_vma=False,
    )
```

```python
import functools

import jax
import jax.numpy as jnp
from jax import lax
from jax.experimental import pallas as pl
from jax.experimental.pallas import tpu as pltpu
from jax.sharding import PartitionSpec as P

AXES = ("rows", "grp")
HIGHEST = lax.Precision.HIGHEST
LANES = 128
VMEM_LIMIT = 40 * 1024 * 1024


CHUNKS = 4


def sketch_kernel(
    slab_hbm, sketch_hbm, slab_ref, first_ref, split_ref, gram_ref, sketch_ref, slab_sem, sketch_sem
):
    width, rank = sketch_ref.shape
    step = width // CHUNKS
    copies = []
    for k in range(CHUNKS):
        at = pl.ds(k * step, step)
        copies.append((
            pltpu.make_async_copy(sketch_hbm.at[at, :], sketch_ref.at[at, :], sketch_sem.at[k]),
            pltpu.make_async_copy(slab_hbm.at[:, at], slab_ref.at[:, at], slab_sem.at[k]),
        ))
    for pair in copies:
        for copy in pair:
            copy.start()
    for k in range(CHUNKS):
        for copy in copies[k]:
            copy.wait()
        at = pl.ds(k * step, step)
        part = jnp.dot(slab_ref[:, at], sketch_ref[at, :], preferred_element_type=jnp.float32)
        if k == 0:
            first_ref[...] = part
        else:
            first_ref[...] += part
    first = first_ref[...]
    turned = first.T
    gram_ref[...] = jnp.dot(turned, first, precision=HIGHEST, preferred_element_type=jnp.float32)
    high = turned.astype(jnp.bfloat16)
    split_ref[:rank] = high
    split_ref[rank:] = (turned - high.astype(jnp.float32)).astype(jnp.bfloat16)


def sketch_call(slab, sketch):
    rows, width = slab.shape
    rank = sketch.shape[1]
    return pl.pallas_call(
        sketch_kernel,
        in_specs=[pl.BlockSpec(memory_space=pltpu.HBM)] * 2,
        out_specs=[pl.BlockSpec(memory_space=pltpu.VMEM)] * 4,
        out_shape=[
            jax.ShapeDtypeStruct((rows, width), jnp.bfloat16),
            jax.ShapeDtypeStruct((rows, rank), jnp.float32),
            jax.ShapeDtypeStruct((2 * rank, rows), jnp.bfloat16),
            jax.ShapeDtypeStruct((rank, rank), jnp.float32),
        ],
        scratch_shapes=[
            pltpu.VMEM((width, rank), jnp.bfloat16),
            pltpu.SemaphoreType.DMA((CHUNKS,)),
            pltpu.SemaphoreType.DMA((CHUNKS,)),
        ],
        compiler_params=pltpu.CompilerParams(vmem_limit_bytes=VMEM_LIMIT),
        cost_estimate=pl.CostEstimate(
            flops=2 * rows * width * rank, bytes_accessed=rows * width * 2, transcendentals=0
        ),
        name="sketch_rows",
    )(
        pltpu.with_memory_space_constraint(slab, pltpu.HBM),
        pltpu.with_memory_space_constraint(sketch, pltpu.HBM),
    )


def project_kernel(sibling, owner_ref, split_ref, slab_ref, out_ref):
    rank = out_ref.shape[1]
    owner = owner_ref[0]
    core = lax.bitwise_and(owner, 1)
    wanted = lax.bitwise_xor(core, sibling)
    mine = lax.shift_right_logical(owner, 1)

    def columns(q):
        at = pl.multiple_of((2 * q + wanted) * LANES, LANES)
        return slab_ref[:, pl.ds(at, LANES)]

    def place(q):
        away = lax.bitwise_xor(mine, q)
        bit = [lax.bitwise_and(lax.shift_right_logical(away, i), 1) for i in range(4)]
        straight = 8 * bit[0] + 4 * bit[1] + 2 * bit[2] + bit[3]
        turned = 8 * bit[1] + 4 * bit[0] + 2 * bit[3] + bit[2]
        return jnp.where(wanted == 0, straight, turned)

    for q in range(0, out_ref.shape[0], 2):
        both = jnp.dot(
            split_ref[...], jnp.concatenate([columns(q), columns(q + 1)], axis=1),
            preferred_element_type=jnp.float32,
        )
        sums = both[:rank] + both[rank:]
        out_ref[place(q)] = sums[:, :LANES]
        out_ref[place(q + 1)] = sums[:, LANES:]


def project_call(owner, split, slab, sibling):
    rows, width = slab.shape
    rank = split.shape[0] // 2
    vmem = pl.BlockSpec(memory_space=pltpu.VMEM)
    return pl.pallas_call(
        functools.partial(project_kernel, sibling),
        in_specs=[pl.BlockSpec(memory_space=pltpu.SMEM), vmem, vmem],
        out_specs=vmem,
        out_shape=jax.ShapeDtypeStruct((width // (2 * LANES), rank, LANES), jnp.float32),
        compiler_params=pltpu.CompilerParams(vmem_limit_bytes=VMEM_LIMIT),
        cost_estimate=pl.CostEstimate(
            flops=2 * rows * width * rank, bytes_accessed=rows * width, transcendentals=0
        ),
        name="project_sibling" if sibling else "project_own",
    )(owner, split, slab)


def lane(block, at):
    return jnp.broadcast_to(block[:, at : at + 1], block.shape)


def sublane(block, at):
    return jnp.broadcast_to(block[at : at + 1, :], block.shape)


def inverse_factor(gram_ref, inverse_ref):
    size = gram_ref.shape[0]
    blocks = size // 8
    left = [gram_ref[8 * i : 8 * i + 8, :] for i in range(blocks)]
    row_at = lax.broadcasted_iota(jnp.int32, (8, size), 0)
    lane_at = lax.broadcasted_iota(jnp.int32, (8, size), 1)
    right = [jnp.where(lane_at == row_at + 8 * i, 1.0, 0.0).astype(jnp.float32) for i in range(blocks)]
    for p in range(blocks):
        column = [lane(left[p], 8 * p + k) for k in range(8)]
        entry = {(r, c): sublane(column[c], r) for c in range(8) for r in range(c, 8)}
        scale, lower = [], {}
        for k in range(8):
            scale.append(lax.rsqrt(entry[k, k]))
            for r in range(k + 1, 8):
                lower[r, k] = entry[r, k] * scale[k]
            for c in range(k + 1, 8):
                for r in range(c, 8):
                    entry[r, c] = entry[r, c] - lower[r, k] * lower[c, k]
        tops, sides = [], []
        for k in range(8):
            top, side = sublane(left[p], k), sublane(right[p], k)
            for j in range(k):
                top = top - lower[k, j] * tops[j]
                side = side - lower[k, j] * sides[j]
            tops.append(top * scale[k])
            sides.append(side * scale[k])
        result = sides[0]
        for k in range(1, 8):
            result = jnp.where(row_at == k, sides[k], result)
        inverse_ref[8 * p : 8 * p + 8, :] = result
        for i in range(p + 1, blocks):
            weights = []
            for k in range(8):
                weight = lane(left[i], 8 * p + k)
                for j in range(k):
                    weight = weight - lower[k, j] * weights[j]
                weights.append(weight * scale[k])
            for k in range(8):
                left[i] = left[i] - weights[k] * tops[k]
                right[i] = right[i] - weights[k] * sides[k]


def factor_kernel(gram_ref, inverse_ref):
    inverse_factor(gram_ref, inverse_ref)


def factor_call(gram):
    return pl.pallas_call(
        factor_kernel,
        in_specs=[pl.BlockSpec(memory_space=pltpu.VMEM)],
        out_specs=pl.BlockSpec(memory_space=pltpu.VMEM),
        out_shape=jax.ShapeDtypeStruct(gram.shape, jnp.float32),
        compiler_params=pltpu.CompilerParams(vmem_limit_bytes=VMEM_LIMIT),
        cost_estimate=pl.CostEstimate(
            flops=4000000000, bytes_accessed=gram.size * 8, transcendentals=gram.shape[0]
        ),
        name="factor",
    )(gram)


def basis_kernel(factor, inverse_ref, first_ref, basis_ref):
    one = lax.dot_general(
        first_ref[...], inverse_ref[...], (((1,), (1,)), ((), ())),
        precision=HIGHEST, preferred_element_type=jnp.float32,
    )
    basis_ref[...] = one * factor


def basis_call(inverse, first, total_rows):
    rows, rank = first.shape
    vmem = pl.BlockSpec(memory_space=pltpu.VMEM)
    return pl.pallas_call(
        functools.partial(basis_kernel, float(total_rows) ** 0.5),
        in_specs=[vmem, vmem],
        out_shape=jax.ShapeDtypeStruct((rows, rank), jnp.float32),
        compiler_params=pltpu.CompilerParams(vmem_limit_bytes=VMEM_LIMIT),
        cost_estimate=pl.CostEstimate(
            flops=12 * rows * rank * rank, bytes_accessed=rows * rank * 8, transcendentals=0
        ),
        name="basis_rows",
    )(inverse, first)


def final_kernel(factor, inverse_ref, sums_ref, out_ref):
    result = jnp.dot(
        inverse_ref[...], sums_ref[...], precision=HIGHEST, preferred_element_type=jnp.float32
    )
    out_ref[...] = (result.T * factor).astype(out_ref.dtype)


def final_call(inverse, sums, factor):
    rank, own = sums.shape
    return pl.pallas_call(
        functools.partial(final_kernel, factor),
        out_shape=jax.ShapeDtypeStruct((own, rank), jnp.bfloat16),
        compiler_params=pltpu.CompilerParams(vmem_limit_bytes=VMEM_LIMIT),
        name="final_rows",
    )(inverse, sums)


def local(slab, sketch):
    rows_loc, width = slab.shape
    devices_all = lax.axis_size(AXES)
    own = width // devices_all
    bits = devices_all.bit_length() - 1
    low_bits = bits - ((width // LANES).bit_length() - 1)
    total_rows = rows_loc * devices_all
    me = lax.axis_index(AXES)

    def swap(array, bit):
        pairs = [(i, i ^ (1 << bit)) for i in range(devices_all)]
        return lax.ppermute(array, AXES, pairs)

    def exchange(array, bit, other):
        pairs = [(i, i ^ (1 << (other if (i >> low_bits) & 1 else bit))) for i in range(devices_all)]
        return lax.ppermute(array, AXES, pairs)

    core, x, y, z, zz = range(low_bits, low_bits + 5)
    tie = lax.optimization_barrier

    owner = lax.shift_right_logical(me, low_bits).astype(jnp.int32).reshape(1)
    slab_near, first, split, gram = sketch_call(slab, sketch)
    gram = gram + exchange(gram, core, core)
    send = project_call(owner, split, slab_near, 1)
    send, split, gram = tie((send, split, gram))
    got = exchange(send, core, core)
    gram = gram + exchange(gram, z, zz)
    got, gram = tie((got, gram))
    sums = project_call(owner, split, slab_near, 0) + got
    got = exchange(sums[8:], x, y)
    gram = gram + exchange(gram, zz, z)
    got, gram = tie((got, gram))
    gram = gram + exchange(gram, x, y)
    sums = sums[:8] + got
    got = exchange(sums[4:], y, x)
    gram = gram + exchange(gram, y, x)
    for bit in range(low_bits):
        gram = gram + swap(gram, bit)
    got, gram = tie((got, gram))
    sums = sums[:4] + got
    got = exchange(sums[2:], z, zz)
    sums, gram = tie((sums, gram))
    inverse = factor_call(gram)
    got, inverse = tie((got, inverse))
    sums = sums[:2] + got
    kept, moved, inverse = tie((sums[0], sums[1], inverse))
    sums = kept + exchange(moved, zz, z)
    basis = basis_call(inverse, first, total_rows)
    for bit in reversed(range(low_bits)):
        half = sums.shape[1] // 2
        mine = lax.rem(lax.shift_right_logical(me, bit), 2) == 1
        left, right = sums[:, :half], sums[:, half:]
        sums = jnp.where(mine, right, left) + swap(jnp.where(mine, left, right), bit)
    projected = final_call(inverse, sums, (float(width) / float(total_rows)) ** 0.5)
    return (basis, projected)


def solution(mesh):
    return jax.shard_map(
        local,
        mesh=mesh,
        in_specs=(P(AXES, None), P()),
        out_specs=(P(AXES, None), P(AXES, None)),
        check_vma=False,
    )
```

```python
import functools

import jax
import jax.numpy as jnp
from jax import lax
from jax.experimental import pallas as pl
from jax.experimental.pallas import tpu as pltpu
from jax.sharding import PartitionSpec as P

AXES = ("rows", "grp")
HIGHEST = lax.Precision.HIGHEST
LANES = 128
VMEM_LIMIT = 24 * 1024 * 1024


CHUNKS = 4


def sketch_kernel(
    slab_hbm, sketch_hbm, slab_ref, first_ref, split_ref, gram_ref, sketch_ref, slab_sem, sketch_sem
):
    width, rank = sketch_ref.shape
    step = width // CHUNKS
    copies = []
    for k in range(CHUNKS):
        at = pl.ds(k * step, step)
        copies.append((
            pltpu.make_async_copy(sketch_hbm.at[at, :], sketch_ref.at[at, :], sketch_sem.at[k]),
            pltpu.make_async_copy(slab_hbm.at[:, at], slab_ref.at[:, at], slab_sem.at[k]),
        ))
    for pair in copies:
        for copy in pair:
            copy.start()
    for k in range(CHUNKS):
        for copy in copies[k]:
            copy.wait()
        at = pl.ds(k * step, step)
        part = jnp.dot(slab_ref[:, at], sketch_ref[at, :], preferred_element_type=jnp.float32)
        if k == 0:
            first_ref[...] = part
        else:
            first_ref[...] += part
    first = first_ref[...]
    turned = first.T
    gram_ref[...] = jnp.dot(turned, first, precision=HIGHEST, preferred_element_type=jnp.float32)
    high = turned.astype(jnp.bfloat16)
    split_ref[:rank] = high
    split_ref[rank:] = (turned - high.astype(jnp.float32)).astype(jnp.bfloat16)


def sketch_call(slab, sketch):
    rows, width = slab.shape
    rank = sketch.shape[1]
    return pl.pallas_call(
        sketch_kernel,
        in_specs=[pl.BlockSpec(memory_space=pltpu.HBM)] * 2,
        out_specs=[pl.BlockSpec(memory_space=pltpu.VMEM)] * 4,
        out_shape=[
            pltpu.VMEM((rows, width), jnp.bfloat16),
            pltpu.VMEM((rows, rank), jnp.float32),
            pltpu.VMEM((2 * rank, rows), jnp.bfloat16),
            pltpu.VMEM((rank, rank), jnp.float32),
        ],
        scratch_shapes=[
            pltpu.VMEM((width, rank), jnp.bfloat16),
            pltpu.SemaphoreType.DMA((CHUNKS,)),
            pltpu.SemaphoreType.DMA((CHUNKS,)),
        ],
        compiler_params=pltpu.CompilerParams(vmem_limit_bytes=VMEM_LIMIT),
        cost_estimate=pl.CostEstimate(
            flops=2 * rows * width * rank, bytes_accessed=rows * width * 2, transcendentals=0
        ),
        name="sketch_rows",
    )(
        pltpu.with_memory_space_constraint(slab, pltpu.HBM),
        pltpu.with_memory_space_constraint(sketch, pltpu.HBM),
    )


def project_kernel(sibling, owner_ref, split_ref, slab_ref, out_ref):
    rank = out_ref.shape[1]
    owner = owner_ref[0]
    core = lax.bitwise_and(owner, 1)
    wanted = lax.bitwise_xor(core, sibling)
    mine = lax.shift_right_logical(owner, 1)

    def columns(q):
        at = pl.multiple_of((2 * q + wanted) * LANES, LANES)
        return slab_ref[:, pl.ds(at, LANES)]

    def place(q):
        away = lax.bitwise_xor(mine, q)
        bit = [lax.bitwise_and(lax.shift_right_logical(away, i), 1) for i in range(4)]
        straight = 8 * bit[0] + 4 * bit[1] + 2 * bit[2] + bit[3]
        turned = 8 * bit[1] + 4 * bit[0] + 2 * bit[3] + bit[2]
        return jnp.where(wanted == 0, straight, turned)

    for q in range(0, out_ref.shape[0], 2):
        both = jnp.dot(
            split_ref[...], jnp.concatenate([columns(q), columns(q + 1)], axis=1),
            preferred_element_type=jnp.float32,
        )
        sums = both[:rank] + both[rank:]
        out_ref[place(q)] = sums[:, :LANES]
        out_ref[place(q + 1)] = sums[:, LANES:]


def project_call(owner, split, slab, sibling):
    rows, width = slab.shape
    rank = split.shape[0] // 2
    vmem = pl.BlockSpec(memory_space=pltpu.VMEM)
    return pl.pallas_call(
        functools.partial(project_kernel, sibling),
        in_specs=[pl.BlockSpec(memory_space=pltpu.SMEM), vmem, vmem],
        out_specs=vmem,
        out_shape=jax.ShapeDtypeStruct((width // (2 * LANES), rank, LANES), jnp.float32),
        compiler_params=pltpu.CompilerParams(vmem_limit_bytes=VMEM_LIMIT),
        cost_estimate=pl.CostEstimate(
            flops=2 * rows * width * rank, bytes_accessed=rows * width, transcendentals=0
        ),
        name="project_sibling" if sibling else "project_own",
    )(owner, split, pltpu.with_memory_space_constraint(slab, pltpu.VMEM))


def lane(block, at):
    return jnp.broadcast_to(block[:, at : at + 1], block.shape)


def sublane(block, at):
    return jnp.broadcast_to(block[at : at + 1, :], block.shape)


def inverse_factor(gram_ref, inverse_ref):
    size = gram_ref.shape[0]
    blocks = size // 8
    left = [gram_ref[8 * i : 8 * i + 8, :] for i in range(blocks)]
    row_at = lax.broadcasted_iota(jnp.int32, (8, size), 0)
    lane_at = lax.broadcasted_iota(jnp.int32, (8, size), 1)
    right = [jnp.where(lane_at == row_at + 8 * i, 1.0, 0.0).astype(jnp.float32) for i in range(blocks)]
    for p in range(blocks):
        column = [lane(left[p], 8 * p + k) for k in range(8)]
        entry = {(r, c): sublane(column[c], r) for c in range(8) for r in range(c, 8)}
        scale, lower = [], {}
        for k in range(8):
            scale.append(lax.rsqrt(entry[k, k]))
            for r in range(k + 1, 8):
                lower[r, k] = entry[r, k] * scale[k]
            for c in range(k + 1, 8):
                for r in range(c, 8):
                    entry[r, c] = entry[r, c] - lower[r, k] * lower[c, k]
        tops, sides = [], []
        for k in range(8):
            top, side = sublane(left[p], k), sublane(right[p], k)
            for j in range(k):
                top = top - lower[k, j] * tops[j]
                side = side - lower[k, j] * sides[j]
            tops.append(top * scale[k])
            sides.append(side * scale[k])
        result = sides[0]
        for k in range(1, 8):
            result = jnp.where(row_at == k, sides[k], result)
        inverse_ref[8 * p : 8 * p + 8, :] = result
        for i in range(p + 1, blocks):
            weights = []
            for k in range(8):
                weight = lane(left[i], 8 * p + k)
                for j in range(k):
                    weight = weight - lower[k, j] * weights[j]
                weights.append(weight * scale[k])
            for k in range(8):
                left[i] = left[i] - weights[k] * tops[k]
                right[i] = right[i] - weights[k] * sides[k]


def factor_kernel(gram_ref, inverse_ref):
    inverse_factor(gram_ref, inverse_ref)


def factor_call(gram):
    return pl.pallas_call(
        factor_kernel,
        in_specs=[pl.BlockSpec(memory_space=pltpu.VMEM)],
        out_specs=pl.BlockSpec(memory_space=pltpu.VMEM),
        out_shape=jax.ShapeDtypeStruct(gram.shape, jnp.float32),
        compiler_params=pltpu.CompilerParams(vmem_limit_bytes=VMEM_LIMIT),
        cost_estimate=pl.CostEstimate(
            flops=4000000000, bytes_accessed=gram.size * 8, transcendentals=gram.shape[0]
        ),
        name="factor",
    )(gram)


def basis_kernel(factor, inverse_ref, first_ref, basis_ref):
    one = lax.dot_general(
        first_ref[...], inverse_ref[...], (((1,), (1,)), ((), ())),
        precision=HIGHEST, preferred_element_type=jnp.float32,
    )
    basis_ref[...] = one * factor


def basis_call(inverse, first, total_rows):
    rows, rank = first.shape
    vmem = pl.BlockSpec(memory_space=pltpu.VMEM)
    return pl.pallas_call(
        functools.partial(basis_kernel, float(total_rows) ** 0.5),
        in_specs=[vmem, vmem],
        out_shape=jax.ShapeDtypeStruct((rows, rank), jnp.float32),
        compiler_params=pltpu.CompilerParams(vmem_limit_bytes=VMEM_LIMIT),
        cost_estimate=pl.CostEstimate(
            flops=12 * rows * rank * rank, bytes_accessed=rows * rank * 8, transcendentals=0
        ),
        name="basis_rows",
    )(inverse, first)


def final_kernel(factor, inverse_ref, sums_ref, out_ref):
    result = jnp.dot(
        inverse_ref[...], sums_ref[...], precision=HIGHEST, preferred_element_type=jnp.float32
    )
    out_ref[...] = (result.T * factor).astype(out_ref.dtype)


def final_call(inverse, sums, factor):
    rank, own = sums.shape
    return pl.pallas_call(
        functools.partial(final_kernel, factor),
        out_shape=jax.ShapeDtypeStruct((own, rank), jnp.bfloat16),
        compiler_params=pltpu.CompilerParams(vmem_limit_bytes=VMEM_LIMIT),
        name="final_rows",
    )(inverse, sums)


def local(slab, sketch):
    rows_loc, width = slab.shape
    devices_all = lax.axis_size(AXES)
    own = width // devices_all
    bits = devices_all.bit_length() - 1
    low_bits = bits - ((width // LANES).bit_length() - 1)
    total_rows = rows_loc * devices_all
    me = lax.axis_index(AXES)

    def swap(array, bit):
        pairs = [(i, i ^ (1 << bit)) for i in range(devices_all)]
        return lax.ppermute(array, AXES, pairs)

    def exchange(array, bit, other):
        pairs = [(i, i ^ (1 << (other if (i >> low_bits) & 1 else bit))) for i in range(devices_all)]
        return lax.ppermute(array, AXES, pairs)

    core, x, y, z, zz = range(low_bits, low_bits + 5)
    tie = lax.optimization_barrier

    owner = lax.shift_right_logical(me, low_bits).astype(jnp.int32).reshape(1)
    slab_near, first, split, gram = sketch_call(slab, sketch)
    gram = gram + exchange(gram, z, zz)
    send = project_call(owner, split, slab_near, 1)
    send, gram = tie((send, gram))
    got = exchange(send, core, core)
    gram = gram + exchange(gram, zz, z)
    sums = project_call(owner, split, slab_near, 0) + got
    got = exchange(sums[8:], x, y)
    gram = gram + exchange(gram, core, core)
    gram = gram + exchange(gram, x, y)
    got, gram = tie((got, gram))
    sums = sums[:8] + got
    got = exchange(sums[4:], y, x)
    gram = gram + exchange(gram, y, x)
    for bit in range(low_bits):
        gram = gram + swap(gram, bit)
    got, gram = tie((got, gram))
    sums = sums[:4] + got
    got = exchange(sums[2:], z, zz)
    sums, gram = tie((sums, gram))
    inverse = factor_call(gram)
    got, inverse = tie((got, inverse))
    sums = sums[:2] + got
    kept, moved, inverse = tie((sums[0], sums[1], inverse))
    sums = kept + exchange(moved, zz, z)
    basis = basis_call(inverse, first, total_rows)
    for bit in reversed(range(low_bits)):
        half = sums.shape[1] // 2
        mine = lax.rem(lax.shift_right_logical(me, bit), 2) == 1
        left, right = sums[:, :half], sums[:, half:]
        sums = jnp.where(mine, right, left) + swap(jnp.where(mine, left, right), bit)
    projected = final_call(inverse, sums, (float(width) / float(total_rows)) ** 0.5)
    return (basis, projected)


def solution(mesh):
    return jax.shard_map(
        local,
        mesh=mesh,
        in_specs=(P(AXES, None), P()),
        out_specs=(P(AXES, None), P(AXES, None)),
        check_vma=False,
    )
```

```python
import functools

import jax
import jax.numpy as jnp
from jax import lax
from jax.experimental import pallas as pl
from jax.experimental.pallas import tpu as pltpu
from jax.sharding import PartitionSpec as P

AXES = ("rows", "grp")
HIGHEST = lax.Precision.HIGHEST
LANES = 128
VMEM_LIMIT = 24 * 1024 * 1024
AHEAD = 2


def project(out_ref, split_ref, columns, mine, wanted):
    rank = out_ref.shape[1]

    def place(q):
        away = lax.bitwise_xor(mine, q)
        bit = [lax.bitwise_and(lax.shift_right_logical(away, i), 1) for i in range(4)]
        straight = 8 * bit[0] + 4 * bit[1] + 2 * bit[2] + bit[3]
        turned = 8 * bit[1] + 4 * bit[0] + 2 * bit[3] + bit[2]
        return jnp.where(wanted == 0, straight, turned)

    for q in range(0, out_ref.shape[0], 2):
        both = jnp.dot(
            split_ref[...], jnp.concatenate([columns(q), columns(q + 1)], axis=1),
            preferred_element_type=jnp.float32,
        )
        sums = both[:rank] + both[rank:]
        out_ref[place(q)] = sums[:, :LANES]
        out_ref[place(q + 1)] = sums[:, LANES:]


def rows_kernel(
    owner_ref, slab_hbm, sketch_hbm, first_ref, gram_ref, split_ref, send_ref,
    slab_ref, sketch_ref, slab_sem, sketch_sem,
):
    rows, width = slab_ref.shape
    rank = sketch_ref.shape[1]
    starts = list(range(0, rows, LANES))
    copies = [
        pltpu.make_async_copy(
            slab_hbm.at[pl.ds(r, min(LANES, rows - r)), :],
            slab_ref.at[pl.ds(r, min(LANES, rows - r)), :],
            slab_sem.at[k],
        )
        for k, r in enumerate(starts)
    ]
    sketch_copy = pltpu.make_async_copy(sketch_hbm, sketch_ref, sketch_sem)
    sketch_copy.start()
    for copy in copies[:AHEAD]:
        copy.start()
    sketch_copy.wait()
    for k, r in enumerate(starts):
        copies[k].wait()
        if k + AHEAD < len(starts):
            copies[k + AHEAD].start()
        at = pl.ds(r, min(LANES, rows - r))
        first = jnp.dot(slab_ref[at, :], sketch_ref[...], preferred_element_type=jnp.float32)
        first_ref[at, :] = first
        turned = first.T
        high = turned.astype(jnp.bfloat16)
        split_ref[:rank, at] = high
        split_ref[rank:, at] = (turned - high.astype(jnp.float32)).astype(jnp.bfloat16)
        gram = jnp.dot(turned, first, precision=HIGHEST, preferred_element_type=jnp.float32)
        if k == 0:
            gram_ref[...] = gram
        else:
            gram_ref[...] += gram

    owner = owner_ref[0]
    other = 1 - lax.bitwise_and(owner, 1)

    def columns(q):
        return slab_ref[:, pl.ds(pl.multiple_of((2 * q + other) * LANES, LANES), LANES)]

    project(send_ref, split_ref, columns, lax.shift_right_logical(owner, 1), other)


def own_kernel(owner_ref, split_ref, slab_hbm, keep_ref, slab_ref, sems):
    owner = owner_ref[0]
    core = lax.bitwise_and(owner, 1)
    copies = []
    for q in range(keep_ref.shape[0]):
        at = pl.multiple_of((2 * q + core) * LANES, LANES)
        copies.append(
            pltpu.make_async_copy(slab_hbm.at[:, pl.ds(at, LANES)], slab_ref.at[q], sems.at[q])
        )
    for copy in copies:
        copy.start()

    def columns(q):
        copies[q].wait()
        return slab_ref[q]

    project(keep_ref, split_ref, columns, lax.shift_right_logical(owner, 1), core)


def own_call(owner, split, slab):
    rows, width = slab.shape
    rank = split.shape[0] // 2
    vmem = pl.BlockSpec(memory_space=pltpu.VMEM)
    chunks = width // (2 * LANES)
    return pl.pallas_call(
        own_kernel,
        in_specs=[
            pl.BlockSpec(memory_space=pltpu.SMEM), vmem, pl.BlockSpec(memory_space=pltpu.HBM)
        ],
        out_specs=vmem,
        out_shape=jax.ShapeDtypeStruct((chunks, rank, LANES), jnp.float32),
        scratch_shapes=[
            pltpu.VMEM((chunks, rows, LANES), jnp.bfloat16),
            pltpu.SemaphoreType.DMA((chunks,)),
        ],
        compiler_params=pltpu.CompilerParams(vmem_limit_bytes=VMEM_LIMIT),
        cost_estimate=pl.CostEstimate(
            flops=2 * rows * width * rank, bytes_accessed=rows * width, transcendentals=0
        ),
        name="project_own",
    )(owner, split, pltpu.with_memory_space_constraint(slab, pltpu.HBM))


def rows_call(owner, slab, sketch):
    rows, width = slab.shape
    rank = sketch.shape[1]
    vmem = pl.BlockSpec(memory_space=pltpu.VMEM)
    chunks = (width // (2 * LANES), rank, LANES)
    return pl.pallas_call(
        rows_kernel,
        in_specs=[
            pl.BlockSpec(memory_space=pltpu.SMEM),
            pl.BlockSpec(memory_space=pltpu.HBM),
            pl.BlockSpec(memory_space=pltpu.HBM),
        ],
        out_specs=[vmem] * 4,
        out_shape=[
            jax.ShapeDtypeStruct((rows, rank), jnp.float32),
            jax.ShapeDtypeStruct((rank, rank), jnp.float32),
            jax.ShapeDtypeStruct((2 * rank, rows), jnp.bfloat16),
            jax.ShapeDtypeStruct(chunks, jnp.float32),
        ],
        scratch_shapes=[
            pltpu.VMEM((rows, width), jnp.bfloat16),
            pltpu.VMEM((width, rank), jnp.bfloat16),
            pltpu.SemaphoreType.DMA((-(-rows // LANES),)),
            pltpu.SemaphoreType.DMA,
        ],
        compiler_params=pltpu.CompilerParams(vmem_limit_bytes=VMEM_LIMIT),
        cost_estimate=pl.CostEstimate(
            flops=4 * rows * width * rank, bytes_accessed=rows * width * 2, transcendentals=0
        ),
        name="sketch_rows",
    )(
        owner,
        pltpu.with_memory_space_constraint(slab, pltpu.HBM),
        pltpu.with_memory_space_constraint(sketch, pltpu.HBM),
    )


def lane(block, at):
    return jnp.broadcast_to(block[:, at : at + 1], block.shape)


def sublane(block, at):
    return jnp.broadcast_to(block[at : at + 1, :], block.shape)


def inverse_factor(gram_ref, inverse_ref):
    size = gram_ref.shape[0]
    blocks = size // 8
    left = [gram_ref[8 * i : 8 * i + 8, :] for i in range(blocks)]
    row_at = lax.broadcasted_iota(jnp.int32, (8, size), 0)
    lane_at = lax.broadcasted_iota(jnp.int32, (8, size), 1)
    right = [jnp.where(lane_at == row_at + 8 * i, 1.0, 0.0).astype(jnp.float32) for i in range(blocks)]
    for p in range(blocks):
        column = [lane(left[p], 8 * p + k) for k in range(8)]
        entry = {(r, c): sublane(column[c], r) for c in range(8) for r in range(c, 8)}
        scale, lower = [], {}
        for k in range(8):
            scale.append(lax.rsqrt(entry[k, k]))
            for r in range(k + 1, 8):
                lower[r, k] = entry[r, k] * scale[k]
            for c in range(k + 1, 8):
                for r in range(c, 8):
                    entry[r, c] = entry[r, c] - lower[r, k] * lower[c, k]
        tops, sides = [], []
        for k in range(8):
            top, side = sublane(left[p], k), sublane(right[p], k)
            for j in range(k):
                top = top - lower[k, j] * tops[j]
                side = side - lower[k, j] * sides[j]
            tops.append(top * scale[k])
            sides.append(side * scale[k])
        result = sides[0]
        for k in range(1, 8):
            result = jnp.where(row_at == k, sides[k], result)
        inverse_ref[8 * p : 8 * p + 8, :] = result
        for i in range(p + 1, blocks):
            weights = []
            for k in range(8):
                weight = lane(left[i], 8 * p + k)
                for j in range(k):
                    weight = weight - lower[k, j] * weights[j]
                weights.append(weight * scale[k])
            for k in range(8):
                left[i] = left[i] - weights[k] * tops[k]
                right[i] = right[i] - weights[k] * sides[k]


def factor_kernel(gram_ref, inverse_ref):
    inverse_factor(gram_ref, inverse_ref)


def factor_call(gram):
    return pl.pallas_call(
        factor_kernel,
        in_specs=[pl.BlockSpec(memory_space=pltpu.VMEM)],
        out_specs=pl.BlockSpec(memory_space=pltpu.VMEM),
        out_shape=jax.ShapeDtypeStruct(gram.shape, jnp.float32),
        compiler_params=pltpu.CompilerParams(vmem_limit_bytes=VMEM_LIMIT),
        cost_estimate=pl.CostEstimate(
            flops=4000000000, bytes_accessed=gram.size * 8, transcendentals=gram.shape[0]
        ),
        name="factor",
    )(gram)


def basis_kernel(factor, inverse_ref, first_ref, basis_ref):
    one = lax.dot_general(
        first_ref[...], inverse_ref[...], (((1,), (1,)), ((), ())),
        precision=HIGHEST, preferred_element_type=jnp.float32,
    )
    basis_ref[...] = one * factor


def basis_call(inverse, first, total_rows):
    rows, rank = first.shape
    vmem = pl.BlockSpec(memory_space=pltpu.VMEM)
    return pl.pallas_call(
        functools.partial(basis_kernel, float(total_rows) ** 0.5),
        in_specs=[vmem, vmem],
        out_shape=jax.ShapeDtypeStruct((rows, rank), jnp.float32),
        compiler_params=pltpu.CompilerParams(vmem_limit_bytes=VMEM_LIMIT),
        cost_estimate=pl.CostEstimate(
            flops=12 * rows * rank * rank, bytes_accessed=rows * rank * 8, transcendentals=0
        ),
        name="basis_rows",
    )(inverse, first)


def final_kernel(factor, inverse_ref, sums_ref, out_ref):
    result = jnp.dot(
        inverse_ref[...], sums_ref[...], precision=HIGHEST, preferred_element_type=jnp.float32
    )
    out_ref[...] = (result.T * factor).astype(out_ref.dtype)


def final_call(inverse, sums, factor):
    rank, own = sums.shape
    return pl.pallas_call(
        functools.partial(final_kernel, factor),
        in_specs=[pl.BlockSpec(memory_space=pltpu.VMEM)] * 2,
        out_shape=jax.ShapeDtypeStruct((own, rank), jnp.bfloat16),
        compiler_params=pltpu.CompilerParams(vmem_limit_bytes=VMEM_LIMIT),
        name="final_rows",
    )(inverse, sums)


def local(slab, sketch):
    rows_loc, width = slab.shape
    devices_all = lax.axis_size(AXES)
    own = width // devices_all
    bits = devices_all.bit_length() - 1
    low_bits = bits - ((width // LANES).bit_length() - 1)
    total_rows = rows_loc * devices_all
    me = lax.axis_index(AXES)

    def swap(array, bit):
        pairs = [(i, i ^ (1 << bit)) for i in range(devices_all)]
        return lax.ppermute(array, AXES, pairs)

    def exchange(array, bit, other):
        pairs = [(i, i ^ (1 << (other if (i >> low_bits) & 1 else bit))) for i in range(devices_all)]
        return lax.ppermute(array, AXES, pairs)

    core, x, y, z, zz = range(low_bits, low_bits + 5)
    tie = lax.optimization_barrier

    owner = lax.shift_right_logical(me, low_bits).astype(jnp.int32).reshape(1)
    first, gram, split, send = rows_call(owner, slab, sketch)
    got = exchange(send, core, core)
    gram = gram + exchange(gram, core, core)
    split, gram = tie((split, gram))
    gram = gram + exchange(gram, x, y)
    got, gram = tie((got, gram))
    sums = own_call(owner, split, slab) + got
    got = exchange(sums[8:], x, y)
    gram = gram + exchange(gram, z, zz)
    gram = gram + exchange(gram, zz, z)
    got, gram = tie((got, gram))
    sums = sums[:8] + got
    got = exchange(jnp.concatenate([sums[4:], gram[None]]), y, x)
    gram = gram + got[4]
    sums = sums[:4] + got[:4]
    got = exchange(sums[2:], z, zz)
    for bit in range(low_bits):
        gram = gram + swap(gram, bit)
    sums, gram = tie((sums, gram))
    inverse = factor_call(gram)
    got, inverse = tie((got, inverse))
    sums = sums[:2] + got
    kept, moved, inverse = tie((sums[0], sums[1], inverse))
    sums = kept + exchange(moved, zz, z)
    basis = basis_call(inverse, first, total_rows)
    for bit in reversed(range(low_bits)):
        half = sums.shape[1] // 2
        mine = lax.rem(lax.shift_right_logical(me, bit), 2) == 1
        left, right = sums[:, :half], sums[:, half:]
        sums = jnp.where(mine, right, left) + swap(jnp.where(mine, left, right), bit)
    projected = final_call(inverse, sums, (float(width) / float(total_rows)) ** 0.5)
    return (basis, projected)


def solution(mesh):
    return jax.shard_map(
        local,
        mesh=mesh,
        in_specs=(P(AXES, None), P()),
        out_specs=(P(AXES, None), P(AXES, None)),
        check_vma=False,
    )
```

```python
import functools

import jax
import jax.numpy as jnp
from jax import lax
from jax.experimental import pallas as pl
from jax.experimental.pallas import tpu as pltpu
from jax.sharding import PartitionSpec as P

AXES = ("rows", "grp")
HIGHEST = lax.Precision.HIGHEST
LANES = 128
VMEM_LIMIT = 24 * 1024 * 1024
AHEAD = 2


def rows_kernel(
    owner_ref, slab_hbm, sketch_hbm, first_ref, gram_ref, send_ref, keep_ref,
    slab_ref, sketch_ref, split_ref, slab_sem, sketch_sem,
):
    rows, width = slab_ref.shape
    rank = sketch_ref.shape[1]
    starts = list(range(0, rows, LANES))
    copies = [
        pltpu.make_async_copy(
            slab_hbm.at[pl.ds(r, min(LANES, rows - r)), :],
            slab_ref.at[pl.ds(r, min(LANES, rows - r)), :],
            slab_sem.at[k],
        )
        for k, r in enumerate(starts)
    ]
    sketch_copy = pltpu.make_async_copy(sketch_hbm, sketch_ref, sketch_sem)
    sketch_copy.start()
    for copy in copies[:AHEAD]:
        copy.start()
    sketch_copy.wait()
    for k, r in enumerate(starts):
        copies[k].wait()
        if k + AHEAD < len(starts):
            copies[k + AHEAD].start()
        at = pl.ds(r, min(LANES, rows - r))
        first = jnp.dot(slab_ref[at, :], sketch_ref[...], preferred_element_type=jnp.float32)
        first_ref[at, :] = first
        turned = first.T
        high = turned.astype(jnp.bfloat16)
        split_ref[:rank, at] = high
        split_ref[rank:, at] = (turned - high.astype(jnp.float32)).astype(jnp.bfloat16)
        gram = jnp.dot(turned, first, precision=HIGHEST, preferred_element_type=jnp.float32)
        if k == 0:
            gram_ref[...] = gram
        else:
            gram_ref[...] += gram

    owner = owner_ref[0]
    core = lax.bitwise_and(owner, 1)
    mine = lax.shift_right_logical(owner, 1)

    def project(out_ref, wanted):
        def columns(q):
            at = pl.multiple_of((2 * q + wanted) * LANES, LANES)
            return slab_ref[:, pl.ds(at, LANES)]

        def place(q):
            away = lax.bitwise_xor(mine, q)
            bit = [lax.bitwise_and(lax.shift_right_logical(away, i), 1) for i in range(4)]
            straight = 8 * bit[0] + 4 * bit[1]
            turned = 8 * bit[1] + 4 * bit[0]
            return jnp.where(wanted == 0, straight, turned) + 2 * bit[3] + bit[2]

        for q in range(0, out_ref.shape[0], 2):
            both = jnp.dot(
                split_ref[...], jnp.concatenate([columns(q), columns(q + 1)], axis=1),
                preferred_element_type=jnp.float32,
            )
            sums = both[:rank] + both[rank:]
            out_ref[place(q)] = sums[:, :LANES]
            out_ref[place(q + 1)] = sums[:, LANES:]

    project(send_ref, 1 - core)
    project(keep_ref, core)


def rows_call(owner, slab, sketch):
    rows, width = slab.shape
    rank = sketch.shape[1]
    vmem = pl.BlockSpec(memory_space=pltpu.VMEM)
    chunks = (width // (2 * LANES), rank, LANES)
    return pl.pallas_call(
        rows_kernel,
        in_specs=[
            pl.BlockSpec(memory_space=pltpu.SMEM),
            pl.BlockSpec(memory_space=pltpu.HBM),
            pl.BlockSpec(memory_space=pltpu.HBM),
        ],
        out_specs=[vmem] * 4,
        out_shape=[
            jax.ShapeDtypeStruct((rows, rank), jnp.float32),
            jax.ShapeDtypeStruct((rank, rank), jnp.float32),
            jax.ShapeDtypeStruct(chunks, jnp.float32),
            jax.ShapeDtypeStruct(chunks, jnp.float32),
        ],
        scratch_shapes=[
            pltpu.VMEM((rows, width), jnp.bfloat16),
            pltpu.VMEM((width, rank), jnp.bfloat16),
            pltpu.VMEM((2 * rank, rows), jnp.bfloat16),
            pltpu.SemaphoreType.DMA((-(-rows // LANES),)),
            pltpu.SemaphoreType.DMA,
        ],
        compiler_params=pltpu.CompilerParams(vmem_limit_bytes=VMEM_LIMIT),
        cost_estimate=pl.CostEstimate(
            flops=6 * rows * width * rank, bytes_accessed=rows * width * 2, transcendentals=0
        ),
        name="project_rows",
    )(
        owner,
        pltpu.with_memory_space_constraint(slab, pltpu.HBM),
        pltpu.with_memory_space_constraint(sketch, pltpu.HBM),
    )


def lane(block, at):
    return jnp.broadcast_to(block[:, at : at + 1], block.shape)


def sublane(block, at):
    return jnp.broadcast_to(block[at : at + 1, :], block.shape)


def inverse_factor(gram_ref, inverse_ref):
    size = gram_ref.shape[0]
    blocks = size // 8
    left = [gram_ref[8 * i : 8 * i + 8, :] for i in range(blocks)]
    row_at = lax.broadcasted_iota(jnp.int32, (8, size), 0)
    lane_at = lax.broadcasted_iota(jnp.int32, (8, size), 1)
    right = [jnp.where(lane_at == row_at + 8 * i, 1.0, 0.0).astype(jnp.float32) for i in range(blocks)]
    for p in range(blocks):
        column = [lane(left[p], 8 * p + k) for k in range(8)]
        entry = {(r, c): sublane(column[c], r) for c in range(8) for r in range(c, 8)}
        scale, lower = [], {}
        for k in range(8):
            scale.append(lax.rsqrt(entry[k, k]))
            for r in range(k + 1, 8):
                lower[r, k] = entry[r, k] * scale[k]
            for c in range(k + 1, 8):
                for r in range(c, 8):
                    entry[r, c] = entry[r, c] - lower[r, k] * lower[c, k]
        tops, sides = [], []
        for k in range(8):
            top, side = sublane(left[p], k), sublane(right[p], k)
            for j in range(k):
                top = top - lower[k, j] * tops[j]
                side = side - lower[k, j] * sides[j]
            tops.append(top * scale[k])
            sides.append(side * scale[k])
        result = sides[0]
        for k in range(1, 8):
            result = jnp.where(row_at == k, sides[k], result)
        inverse_ref[8 * p : 8 * p + 8, :] = result
        for i in range(p + 1, blocks):
            weights = []
            for k in range(8):
                weight = lane(left[i], 8 * p + k)
                for j in range(k):
                    weight = weight - lower[k, j] * weights[j]
                weights.append(weight * scale[k])
            for k in range(8):
                left[i] = left[i] - weights[k] * tops[k]
                right[i] = right[i] - weights[k] * sides[k]


def factor_kernel(gram_ref, inverse_ref):
    inverse_factor(gram_ref, inverse_ref)


def factor_call(gram):
    return pl.pallas_call(
        factor_kernel,
        in_specs=[pl.BlockSpec(memory_space=pltpu.VMEM)],
        out_specs=pl.BlockSpec(memory_space=pltpu.VMEM),
        out_shape=jax.ShapeDtypeStruct(gram.shape, jnp.float32),
        compiler_params=pltpu.CompilerParams(vmem_limit_bytes=VMEM_LIMIT),
        cost_estimate=pl.CostEstimate(
            flops=4000000000, bytes_accessed=gram.size * 8, transcendentals=gram.shape[0]
        ),
        name="factor",
    )(gram)


def finish_kernel(basis_factor, factor, inverse_ref, first_ref, sums_ref, *refs):
    basis_ref, out_ref = refs[-2:]
    inverse = inverse_ref[...]
    one = lax.dot_general(
        first_ref[...], inverse, (((1,), (1,)), ((), ())),
        precision=HIGHEST, preferred_element_type=jnp.float32,
    )
    basis_ref[...] = one * basis_factor
    sums = sums_ref[...]
    for got_ref in refs[:-2]:
        sums = sums + got_ref[...]
    result = jnp.dot(inverse, sums, precision=HIGHEST, preferred_element_type=jnp.float32)
    out_ref[...] = (result.T * factor).astype(out_ref.dtype)


def finish_call(inverse, first, total_rows, factor, sums):
    rows, rank = first.shape
    own = sums[0].shape[1]
    return pl.pallas_call(
        functools.partial(finish_kernel, float(total_rows) ** 0.5, factor),
        in_specs=[pl.BlockSpec(memory_space=pltpu.VMEM)] * (2 + len(sums)),
        out_shape=[
            jax.ShapeDtypeStruct((rows, rank), jnp.float32),
            jax.ShapeDtypeStruct((own, rank), jnp.bfloat16),
        ],
        compiler_params=pltpu.CompilerParams(vmem_limit_bytes=VMEM_LIMIT),
        cost_estimate=pl.CostEstimate(
            flops=12 * rows * rank * rank, bytes_accessed=rows * rank * 8, transcendentals=0
        ),
        name="finish",
    )(inverse, first, *sums)


def local(slab, sketch):
    rows_loc, width = slab.shape
    devices_all = lax.axis_size(AXES)
    own = width // devices_all
    bits = devices_all.bit_length() - 1
    low_bits = bits - ((width // LANES).bit_length() - 1)
    total_rows = rows_loc * devices_all
    me = lax.axis_index(AXES)

    core, x, y, z, zz = [1 << bit for bit in range(low_bits, low_bits + 5)]
    tie = lax.optimization_barrier

    def exchange(array, away, away_odd=None):
        odd = away if away_odd is None else away_odd
        pairs = [(i, i ^ (odd if i & core else away)) for i in range(devices_all)]
        return lax.ppermute(array, AXES, pairs)

    owner = lax.shift_right_logical(me, low_bits).astype(jnp.int32).reshape(1)
    first, gram, send, keep = rows_call(owner, slab, sketch)
    got, gram = tie((exchange(send, core), gram + exchange(gram, core)))
    sums = keep + got
    got = exchange(sums[8:], x, y)
    over_z = [exchange(gram, away) for away in (z | zz, zz, z)]
    gram = (gram + over_z[2]) + (over_z[1] + over_z[0])
    got, gram = tie((got, gram))
    sums = sums[:8] + got
    got = exchange(jnp.concatenate([sums[4:], gram[None]]), y, x)
    sums = sums[:4] + got[:4]
    gram = gram + got[4]
    gram = gram + exchange(gram, x, y)
    over_z = [exchange(sums[i], away) for i, away in ((3, z | zz), (2, zz), (1, z))]
    for bit in range(low_bits):
        gram = gram + exchange(gram, 1 << bit)
    sums, gram = tie((sums, gram))
    inverse = factor_call(gram)
    sums = [sums[0], *over_z]
    if low_bits > 0:
        sums = sum(sums)
        for bit in reversed(range(low_bits)):
            half = sums.shape[1] // 2
            mine = lax.rem(lax.shift_right_logical(me, bit), 2) == 1
            left, right = sums[:, :half], sums[:, half:]
            sums = jnp.where(mine, right, left) + exchange(jnp.where(mine, left, right), 1 << bit)
        sums = [sums]
    factor = (float(width) / float(total_rows)) ** 0.5
    return tuple(finish_call(inverse, first, total_rows, factor, sums))


def solution(mesh):
    return jax.shard_map(
        local,
        mesh=mesh,
        in_specs=(P(AXES, None), P()),
        out_specs=(P(AXES, None), P(AXES, None)),
        check_vma=False,
    )
```

```python
import functools

import jax
import jax.numpy as jnp
from jax import lax
from jax.experimental import pallas as pl
from jax.experimental.pallas import tpu as pltpu
from jax.sharding import PartitionSpec as P

AXES = ("rows", "grp")
HIGHEST = lax.Precision.HIGHEST
LANES = 128
VMEM_LIMIT = 24 * 1024 * 1024
AHEAD = 5


def project(out_ref, split_ref, slab_ref, owner, sibling):
    rank = out_ref.shape[1]
    wanted = lax.bitwise_xor(lax.bitwise_and(owner, 1), sibling)
    mine = lax.shift_right_logical(owner, 1)

    def columns(q):
        at = pl.multiple_of((2 * q + wanted) * LANES, LANES)
        return slab_ref[:, pl.ds(at, LANES)]

    def place(q):
        away = lax.bitwise_xor(mine, q)
        bit = [lax.bitwise_and(lax.shift_right_logical(away, i), 1) for i in range(4)]
        straight = 8 * bit[0] + 4 * bit[1]
        turned = 8 * bit[1] + 4 * bit[0]
        return jnp.where(wanted == 0, straight, turned) + 2 * bit[3] + bit[2]

    for q in range(0, out_ref.shape[0], 2):
        both = jnp.dot(
            split_ref[...], jnp.concatenate([columns(q), columns(q + 1)], axis=1),
            preferred_element_type=jnp.float32,
        )
        sums = both[:rank] + both[rank:]
        out_ref[place(q)] = sums[:, :LANES]
        out_ref[place(q + 1)] = sums[:, LANES:]


def pack(gram):
    half = gram.shape[0] // 2
    top, bottom = gram[:half], gram[half:]
    row = lax.broadcasted_iota(jnp.int32, top.shape, 0)
    column = lax.broadcasted_iota(jnp.int32, top.shape, 1)
    body = jnp.where(column - half < row, jnp.where(column < half, bottom, pltpu.roll(top, half, 1)), bottom)
    diagonal = jnp.sum(jnp.where(row == column, top, 0.0), axis=0, keepdims=True)
    tail = jnp.where(row[:8] == 0, jnp.broadcast_to(diagonal, (8, diagonal.shape[1])), 0.0)
    return jnp.concatenate([body, tail], axis=0)


def unpack(packed):
    half = packed.shape[0] - 8
    body = packed[:half]
    row = lax.broadcasted_iota(jnp.int32, body.shape, 0)
    column = lax.broadcasted_iota(jnp.int32, body.shape, 1)
    diagonal = jnp.broadcast_to(packed[half : half + 1], body.shape)
    top = jnp.where(column < row, pltpu.roll(body, half, 1), jnp.where(column == row, diagonal, 0.0))
    bottom = jnp.where(column - half < row, jnp.where(column < half, body, 0.0), body)
    parts = jnp.concatenate([top, bottom], axis=0)
    row = lax.broadcasted_iota(jnp.int32, parts.shape, 0)
    column = lax.broadcasted_iota(jnp.int32, parts.shape, 1)
    return parts + jnp.where(row == column, 0.0, parts.T)


def rows_kernel(
    owner_ref, slab_hbm, sketch_hbm, slab_ref, first_ref, gram_ref, split_ref, send_ref,
    sketch_ref, sum_ref, slab_sem, sketch_sem,
):
    rows, width = slab_ref.shape
    rank = sketch_ref.shape[1]
    starts = list(range(0, rows, LANES))
    copies = [
        pltpu.make_async_copy(
            slab_hbm.at[pl.ds(r, min(LANES, rows - r)), :],
            slab_ref.at[pl.ds(r, min(LANES, rows - r)), :],
            slab_sem.at[k],
        )
        for k, r in enumerate(starts)
    ]
    sketch_copy = pltpu.make_async_copy(sketch_hbm, sketch_ref, sketch_sem)
    sketch_copy.start()
    for copy in copies[:AHEAD]:
        copy.start()
    sketch_copy.wait()
    for k, r in enumerate(starts):
        copies[k].wait()
        if k + AHEAD < len(starts):
            copies[k + AHEAD].start()
        at = pl.ds(r, min(LANES, rows - r))
        first = jnp.dot(slab_ref[at, :], sketch_ref[...], preferred_element_type=jnp.float32)
        first_ref[at, :] = first
        turned = first.T
        high = turned.astype(jnp.bfloat16)
        split_ref[:rank, at] = high
        split_ref[rank:, at] = (turned - high.astype(jnp.float32)).astype(jnp.bfloat16)
        gram = jnp.dot(turned, first, precision=HIGHEST, preferred_element_type=jnp.float32)
        if k == 0:
            sum_ref[...] = gram
        else:
            sum_ref[...] += gram
    gram_ref[...] = pack(sum_ref[...])

    project(send_ref, split_ref, slab_ref, owner_ref[0], 1)


def own_kernel(owner_ref, split_ref, slab_ref, keep_ref):
    project(keep_ref, split_ref, slab_ref, owner_ref[0], 0)


def own_call(owner, split, slab):
    rows, width = slab.shape
    rank = split.shape[0] // 2
    vmem = pl.BlockSpec(memory_space=pltpu.VMEM)
    return pl.pallas_call(
        own_kernel,
        in_specs=[pl.BlockSpec(memory_space=pltpu.SMEM), vmem, vmem],
        out_specs=vmem,
        out_shape=jax.ShapeDtypeStruct((width // (2 * LANES), rank, LANES), jnp.float32),
        compiler_params=pltpu.CompilerParams(vmem_limit_bytes=VMEM_LIMIT),
        cost_estimate=pl.CostEstimate(
            flops=2 * rows * width * rank, bytes_accessed=rows * width, transcendentals=0
        ),
        name="project_own",
    )(owner, split, slab)


def rows_call(owner, slab, sketch):
    rows, width = slab.shape
    rank = sketch.shape[1]
    vmem = pl.BlockSpec(memory_space=pltpu.VMEM)
    chunks = (width // (2 * LANES), rank, LANES)
    return pl.pallas_call(
        rows_kernel,
        in_specs=[
            pl.BlockSpec(memory_space=pltpu.SMEM),
            pl.BlockSpec(memory_space=pltpu.HBM),
            pl.BlockSpec(memory_space=pltpu.HBM),
        ],
        out_specs=[vmem] * 5,
        out_shape=[
            jax.ShapeDtypeStruct((rows, width), jnp.bfloat16),
            jax.ShapeDtypeStruct((rows, rank), jnp.float32),
            jax.ShapeDtypeStruct((rank // 2 + 8, rank), jnp.float32),
            jax.ShapeDtypeStruct((2 * rank, rows), jnp.bfloat16),
            jax.ShapeDtypeStruct(chunks, jnp.float32),
        ],
        scratch_shapes=[
            pltpu.VMEM((width, rank), jnp.bfloat16),
            pltpu.VMEM((rank, rank), jnp.float32),
            pltpu.SemaphoreType.DMA((-(-rows // LANES),)),
            pltpu.SemaphoreType.DMA,
        ],
        compiler_params=pltpu.CompilerParams(vmem_limit_bytes=VMEM_LIMIT),
        cost_estimate=pl.CostEstimate(
            flops=4 * rows * width * rank, bytes_accessed=rows * width * 2, transcendentals=0
        ),
        name="sketch_rows",
    )(
        owner,
        pltpu.with_memory_space_constraint(slab, pltpu.HBM),
        pltpu.with_memory_space_constraint(sketch, pltpu.HBM),
    )


def lane(block, at):
    return jnp.broadcast_to(block[:, at : at + 1], block.shape)


def sublane(block, at):
    return jnp.broadcast_to(block[at : at + 1, :], block.shape)


def inverse_factor(gram, inverse_ref):
    size = gram.shape[0]
    blocks = size // 8
    left = [gram[8 * i : 8 * i + 8, :] for i in range(blocks)]
    row_at = lax.broadcasted_iota(jnp.int32, (8, size), 0)
    lane_at = lax.broadcasted_iota(jnp.int32, (8, size), 1)
    right = [jnp.where(lane_at == row_at + 8 * i, 1.0, 0.0).astype(jnp.float32) for i in range(blocks)]
    for p in range(blocks):
        column = [lane(left[p], 8 * p + k) for k in range(8)]
        entry = {(r, c): sublane(column[c], r) for c in range(8) for r in range(c, 8)}
        scale, lower = [], {}
        for k in range(8):
            scale.append(lax.rsqrt(entry[k, k]))
            for r in range(k + 1, 8):
                lower[r, k] = entry[r, k] * scale[k]
            for c in range(k + 1, 8):
                for r in range(c, 8):
                    entry[r, c] = entry[r, c] - lower[r, k] * lower[c, k]
        tops, sides = [], []
        for k in range(8):
            top, side = sublane(left[p], k), sublane(right[p], k)
            for j in range(k):
                top = top - lower[k, j] * tops[j]
                side = side - lower[k, j] * sides[j]
            tops.append(top * scale[k])
            sides.append(side * scale[k])
        result = sides[0]
        for k in range(1, 8):
            result = jnp.where(row_at == k, sides[k], result)
        inverse_ref[8 * p : 8 * p + 8, :] = result
        for i in range(p + 1, blocks):
            weights = []
            for k in range(8):
                weight = lane(left[i], 8 * p + k)
                for j in range(k):
                    weight = weight - lower[k, j] * weights[j]
                weights.append(weight * scale[k])
            for k in range(8):
                left[i] = left[i] - weights[k] * tops[k]
                right[i] = right[i] - weights[k] * sides[k]


def factor_kernel(gram_ref, inverse_ref):
    inverse_factor(unpack(gram_ref[...]), inverse_ref)


def factor_call(gram):
    return pl.pallas_call(
        factor_kernel,
        in_specs=[pl.BlockSpec(memory_space=pltpu.VMEM)],
        out_specs=pl.BlockSpec(memory_space=pltpu.VMEM),
        out_shape=jax.ShapeDtypeStruct((gram.shape[1], gram.shape[1]), jnp.float32),
        compiler_params=pltpu.CompilerParams(vmem_limit_bytes=VMEM_LIMIT),
        cost_estimate=pl.CostEstimate(
            flops=4000000000, bytes_accessed=gram.size * 8, transcendentals=gram.shape[0]
        ),
        name="factor",
    )(gram)


def finish_kernel(basis_factor, factor, inverse_ref, first_ref, sums_ref, *refs):
    basis_ref, out_ref = refs[-2:]
    inverse = inverse_ref[...]
    one = lax.dot_general(
        first_ref[...], inverse, (((1,), (1,)), ((), ())),
        precision=HIGHEST, preferred_element_type=jnp.float32,
    )
    basis_ref[...] = one * basis_factor
    sums = sums_ref[...]
    for got_ref in refs[:-2]:
        sums = sums + got_ref[...]
    result = jnp.dot(inverse, sums, precision=HIGHEST, preferred_element_type=jnp.float32)
    out_ref[...] = (result.T * factor).astype(out_ref.dtype)


def finish_call(inverse, first, total_rows, factor, sums):
    rows, rank = first.shape
    own = sums[0].shape[1]
    return pl.pallas_call(
        functools.partial(finish_kernel, float(total_rows) ** 0.5, factor),
        in_specs=[pl.BlockSpec(memory_space=pltpu.VMEM)] * (2 + len(sums)),
        out_shape=[
            jax.ShapeDtypeStruct((rows, rank), jnp.float32),
            jax.ShapeDtypeStruct((own, rank), jnp.bfloat16),
        ],
        compiler_params=pltpu.CompilerParams(vmem_limit_bytes=VMEM_LIMIT),
        cost_estimate=pl.CostEstimate(
            flops=12 * rows * rank * rank, bytes_accessed=rows * rank * 8, transcendentals=0
        ),
        name="finish",
    )(inverse, first, *sums)


def local(slab, sketch):
    rows_loc, width = slab.shape
    devices_all = lax.axis_size(AXES)
    own = width // devices_all
    bits = devices_all.bit_length() - 1
    low_bits = bits - ((width // LANES).bit_length() - 1)
    total_rows = rows_loc * devices_all
    me = lax.axis_index(AXES)

    core, x, y, z, zz = [1 << bit for bit in range(low_bits, low_bits + 5)]
    tie = lax.optimization_barrier

    def exchange(array, away, away_odd=None):
        odd = away if away_odd is None else away_odd
        pairs = [(i, i ^ (odd if i & core else away)) for i in range(devices_all)]
        return lax.ppermute(array, AXES, pairs)

    owner = lax.shift_right_logical(me, low_bits).astype(jnp.int32).reshape(1)
    near, first, gram, split, send = rows_call(owner, slab, sketch)
    got = exchange(send, core)
    keep = own_call(owner, split, near)
    got, gram = tie((got, gram + exchange(gram, core)))
    sums = keep + got
    got = exchange(sums[8:], x, y)
    over_z = [exchange(gram, away) for away in (z | zz, zz, z)]
    gram = (gram + over_z[2]) + (over_z[1] + over_z[0])
    got, gram = tie((got, gram))
    sums = sums[:8] + got
    got = exchange(sums[4:], y, x)
    gram = gram + exchange(gram, x, y)
    got, gram = tie((got, gram))
    sums = sums[:4] + got
    gram = gram + exchange(gram, y, x)
    over_z = [exchange(sums[i], away) for i, away in ((3, z | zz), (2, zz), (1, z))]
    for bit in range(low_bits):
        gram = gram + exchange(gram, 1 << bit)
    sums, gram = tie((sums, gram))
    inverse = factor_call(gram)
    sums = [sums[0], *over_z]
    if low_bits > 0:
        sums = sum(sums)
        for bit in reversed(range(low_bits)):
            half = sums.shape[1] // 2
            mine = lax.rem(lax.shift_right_logical(me, bit), 2) == 1
            left, right = sums[:, :half], sums[:, half:]
            sums = jnp.where(mine, right, left) + exchange(jnp.where(mine, left, right), 1 << bit)
        sums = [sums]
    factor = (float(width) / float(total_rows)) ** 0.5
    return tuple(finish_call(inverse, first, total_rows, factor, sums))


def solution(mesh):
    return jax.shard_map(
        local,
        mesh=mesh,
        in_specs=(P(AXES, None), P()),
        out_specs=(P(AXES, None), P(AXES, None)),
        check_vma=False,
    )
```

```python
import functools

import jax
import jax.numpy as jnp
from jax import lax
from jax.experimental import pallas as pl
from jax.experimental.pallas import tpu as pltpu
from jax.sharding import PartitionSpec as P

AXES = ("rows", "grp")
HIGHEST = lax.Precision.HIGHEST
LANES = 128
VMEM_LIMIT = 24 * 1024 * 1024
AHEAD = 2


def project(out_ref, split_ref, slab_ref, owner, sibling, first_place):
    rank = out_ref.shape[1]
    wanted = lax.bitwise_xor(lax.bitwise_and(owner, 1), sibling)
    mine = lax.shift_right_logical(owner, 1)

    def columns(place):
        one, two = place // 8, place // 4 % 2
        away = jnp.where(wanted == 0, one + 2 * two, two + 2 * one) + 4 * (place % 4)
        at = pl.multiple_of((2 * lax.bitwise_xor(mine, away) + wanted) * LANES, LANES)
        return slab_ref[:, pl.ds(at, LANES)]

    for i in range(0, out_ref.shape[0], 2):
        place = first_place + i
        both = jnp.dot(
            split_ref[...], jnp.concatenate([columns(place), columns(place + 1)], axis=1),
            preferred_element_type=jnp.float32,
        )
        sums = both[:rank] + both[rank:]
        out_ref[i] = sums[:, :LANES]
        out_ref[i + 1] = sums[:, LANES:]


def pack(gram):
    half = gram.shape[0] // 2
    top, bottom = gram[:half], gram[half:]
    row = lax.broadcasted_iota(jnp.int32, top.shape, 0)
    column = lax.broadcasted_iota(jnp.int32, top.shape, 1)
    body = jnp.where(column - half < row, jnp.where(column < half, bottom, pltpu.roll(top, half, 1)), bottom)
    diagonal = jnp.sum(jnp.where(row == column, top, 0.0), axis=0, keepdims=True)
    tail = jnp.where(row[:8] == 0, jnp.broadcast_to(diagonal, (8, diagonal.shape[1])), 0.0)
    return jnp.concatenate([body, tail], axis=0)


def unpack(packed):
    half = packed.shape[0] - 8
    body = packed[:half]
    row = lax.broadcasted_iota(jnp.int32, body.shape, 0)
    column = lax.broadcasted_iota(jnp.int32, body.shape, 1)
    diagonal = jnp.broadcast_to(packed[half : half + 1], body.shape)
    top = jnp.where(column < row, pltpu.roll(body, half, 1), jnp.where(column == row, diagonal, 0.0))
    bottom = jnp.where(column - half < row, jnp.where(column < half, body, 0.0), body)
    parts = jnp.concatenate([top, bottom], axis=0)
    row = lax.broadcasted_iota(jnp.int32, parts.shape, 0)
    column = lax.broadcasted_iota(jnp.int32, parts.shape, 1)
    return parts + jnp.where(row == column, 0.0, parts.T)


def rows_kernel(
    owner_ref, slab_hbm, sketch_hbm, slab_ref, first_ref, gram_ref, split_ref, send_ref,
    sketch_ref, sum_ref, slab_sem, sketch_sem,
):
    rows, width = slab_ref.shape
    rank = sketch_ref.shape[1]
    starts = list(range(0, rows, LANES))
    copies = [
        pltpu.make_async_copy(
            slab_hbm.at[pl.ds(r, min(LANES, rows - r)), :],
            slab_ref.at[pl.ds(r, min(LANES, rows - r)), :],
            slab_sem.at[k],
        )
        for k, r in enumerate(starts)
    ]
    sketch_copy = pltpu.make_async_copy(sketch_hbm, sketch_ref, sketch_sem)
    sketch_copy.start()
    for copy in copies[:AHEAD]:
        copy.start()
    sketch_copy.wait()
    for k, r in enumerate(starts):
        copies[k].wait()
        if k + AHEAD < len(starts):
            copies[k + AHEAD].start()
        at = pl.ds(r, min(LANES, rows - r))
        first = jnp.dot(slab_ref[at, :], sketch_ref[...], preferred_element_type=jnp.float32)
        first_ref[at, :] = first
        turned = first.T
        high = turned.astype(jnp.bfloat16)
        split_ref[:rank, at] = high
        split_ref[rank:, at] = (turned - high.astype(jnp.float32)).astype(jnp.bfloat16)
        gram = jnp.dot(turned, first, precision=HIGHEST, preferred_element_type=jnp.float32)
        if k == 0:
            sum_ref[...] = gram
        else:
            sum_ref[...] += gram
    gram_ref[...] = pack(sum_ref[...])

    project(send_ref, split_ref, slab_ref, owner_ref[0], 1, 8)


def project_kernel(parts, owner_ref, split_ref, slab_ref, *out_refs):
    for (sibling, first_place), out_ref in zip(parts, out_refs):
        project(out_ref, split_ref, slab_ref, owner_ref[0], sibling, first_place)


def project_call(owner, split, slab, parts, name):
    rows, width = slab.shape
    rank = split.shape[0] // 2
    vmem = pl.BlockSpec(memory_space=pltpu.VMEM)
    chunks = jax.ShapeDtypeStruct((width // (4 * LANES), rank, LANES), jnp.float32)
    return pl.pallas_call(
        functools.partial(project_kernel, parts),
        in_specs=[pl.BlockSpec(memory_space=pltpu.SMEM), vmem, vmem],
        out_specs=[vmem] * len(parts),
        out_shape=[chunks] * len(parts),
        compiler_params=pltpu.CompilerParams(vmem_limit_bytes=VMEM_LIMIT),
        cost_estimate=pl.CostEstimate(
            flops=len(parts) * rows * width * rank, bytes_accessed=rows * width, transcendentals=0
        ),
        name=name,
    )(owner, split, slab)


def rows_call(owner, slab, sketch):
    rows, width = slab.shape
    rank = sketch.shape[1]
    vmem = pl.BlockSpec(memory_space=pltpu.VMEM)
    chunks = (width // (4 * LANES), rank, LANES)
    return pl.pallas_call(
        rows_kernel,
        in_specs=[
            pl.BlockSpec(memory_space=pltpu.SMEM),
            pl.BlockSpec(memory_space=pltpu.HBM),
            pl.BlockSpec(memory_space=pltpu.HBM),
        ],
        out_specs=[vmem] * 5,
        out_shape=[
            jax.ShapeDtypeStruct((rows, width), jnp.bfloat16),
            jax.ShapeDtypeStruct((rows, rank), jnp.float32),
            jax.ShapeDtypeStruct((rank // 2 + 8, rank), jnp.float32),
            jax.ShapeDtypeStruct((2 * rank, rows), jnp.bfloat16),
            jax.ShapeDtypeStruct(chunks, jnp.float32),
        ],
        scratch_shapes=[
            pltpu.VMEM((width, rank), jnp.bfloat16),
            pltpu.VMEM((rank, rank), jnp.float32),
            pltpu.SemaphoreType.DMA((-(-rows // LANES),)),
            pltpu.SemaphoreType.DMA,
        ],
        compiler_params=pltpu.CompilerParams(vmem_limit_bytes=VMEM_LIMIT),
        cost_estimate=pl.CostEstimate(
            flops=3 * rows * width * rank, bytes_accessed=rows * width * 2, transcendentals=0
        ),
        name="sketch_rows",
    )(
        owner,
        pltpu.with_memory_space_constraint(slab, pltpu.HBM),
        pltpu.with_memory_space_constraint(sketch, pltpu.HBM),
    )


def lane(block, at):
    return jnp.broadcast_to(block[:, at : at + 1], block.shape)


def sublane(block, at):
    return jnp.broadcast_to(block[at : at + 1, :], block.shape)


def inverse_factor(gram, inverse_ref):
    size = gram.shape[0]
    blocks = size // 8
    left = [gram[8 * i : 8 * i + 8, :] for i in range(blocks)]
    row_at = lax.broadcasted_iota(jnp.int32, (8, size), 0)
    lane_at = lax.broadcasted_iota(jnp.int32, (8, size), 1)
    right = [jnp.where(lane_at == row_at + 8 * i, 1.0, 0.0).astype(jnp.float32) for i in range(blocks)]
    for p in range(blocks):
        column = [lane(left[p], 8 * p + k) for k in range(8)]
        entry = {(r, c): sublane(column[c], r) for c in range(8) for r in range(c, 8)}
        scale, lower = [], {}
        for k in range(8):
            scale.append(lax.rsqrt(entry[k, k]))
            for r in range(k + 1, 8):
                lower[r, k] = entry[r, k] * scale[k]
            for c in range(k + 1, 8):
                for r in range(c, 8):
                    entry[r, c] = entry[r, c] - lower[r, k] * lower[c, k]
        tops, sides = [], []
        for k in range(8):
            top, side = sublane(left[p], k), sublane(right[p], k)
            for j in range(k):
                top = top - lower[k, j] * tops[j]
                side = side - lower[k, j] * sides[j]
            tops.append(top * scale[k])
            sides.append(side * scale[k])
        result = sides[0]
        for k in range(1, 8):
            result = jnp.where(row_at == k, sides[k], result)
        inverse_ref[8 * p : 8 * p + 8, :] = result
        for i in range(p + 1, blocks):
            weights = []
            for k in range(8):
                weight = lane(left[i], 8 * p + k)
                for j in range(k):
                    weight = weight - lower[k, j] * weights[j]
                weights.append(weight * scale[k])
            for k in range(8):
                left[i] = left[i] - weights[k] * tops[k]
                right[i] = right[i] - weights[k] * sides[k]


def factor_kernel(gram_ref, inverse_ref):
    inverse_factor(unpack(gram_ref[...]), inverse_ref)


def factor_call(gram):
    return pl.pallas_call(
        factor_kernel,
        in_specs=[pl.BlockSpec(memory_space=pltpu.VMEM)],
        out_specs=pl.BlockSpec(memory_space=pltpu.VMEM),
        out_shape=jax.ShapeDtypeStruct((gram.shape[1], gram.shape[1]), jnp.float32),
        compiler_params=pltpu.CompilerParams(vmem_limit_bytes=VMEM_LIMIT),
        cost_estimate=pl.CostEstimate(
            flops=4000000000, bytes_accessed=gram.size * 8, transcendentals=gram.shape[0]
        ),
        name="factor",
    )(gram)


def finish_kernel(basis_factor, factor, inverse_ref, first_ref, sums_ref, *refs):
    basis_ref, out_ref = refs[-2:]
    inverse = inverse_ref[...]
    one = lax.dot_general(
        first_ref[...], inverse, (((1,), (1,)), ((), ())),
        precision=HIGHEST, preferred_element_type=jnp.float32,
    )
    basis_ref[...] = one * basis_factor
    sums = sums_ref[...]
    for got_ref in refs[:-2]:
        sums = sums + got_ref[...]
    result = jnp.dot(inverse, sums, precision=HIGHEST, preferred_element_type=jnp.float32)
    out_ref[...] = (result.T * factor).astype(out_ref.dtype)


def finish_call(inverse, first, total_rows, factor, sums):
    rows, rank = first.shape
    own = sums[0].shape[1]
    return pl.pallas_call(
        functools.partial(finish_kernel, float(total_rows) ** 0.5, factor),
        in_specs=[pl.BlockSpec(memory_space=pltpu.VMEM)] * (2 + len(sums)),
        out_shape=[
            jax.ShapeDtypeStruct((rows, rank), jnp.float32),
            jax.ShapeDtypeStruct((own, rank), jnp.bfloat16),
        ],
        compiler_params=pltpu.CompilerParams(vmem_limit_bytes=VMEM_LIMIT),
        cost_estimate=pl.CostEstimate(
            flops=12 * rows * rank * rank, bytes_accessed=rows * rank * 8, transcendentals=0
        ),
        name="finish",
    )(inverse, first, *sums)


def local(slab, sketch):
    rows_loc, width = slab.shape
    devices_all = lax.axis_size(AXES)
    own = width // devices_all
    bits = devices_all.bit_length() - 1
    low_bits = bits - ((width // LANES).bit_length() - 1)
    total_rows = rows_loc * devices_all
    me = lax.axis_index(AXES)

    core, x, y, z, zz = [1 << bit for bit in range(low_bits, low_bits + 5)]
    tie = lax.optimization_barrier

    def exchange(array, away, away_odd=None):
        odd = away if away_odd is None else away_odd
        pairs = [(i, i ^ (odd if i & core else away)) for i in range(devices_all)]
        return lax.ppermute(array, AXES, pairs)

    owner = lax.shift_right_logical(me, low_bits).astype(jnp.int32).reshape(1)
    near, first, gram, split, send = rows_call(owner, slab, sketch)
    got = exchange(send, core)
    keep, = project_call(owner, split, near, ((0, 8),), "project_first")
    got, gram = tie((got, gram + exchange(gram, core)))
    got = exchange(keep + got, x, y)
    send, sums = project_call(owner, split, near, ((1, 0), (0, 0)), "project_rest")
    sums = sums + exchange(send, core)
    over_z = [exchange(gram, away) for away in (z | zz, zz, z)]
    gram = (gram + over_z[2]) + (over_z[1] + over_z[0])
    got, gram = tie((got, gram))
    sums = sums + got
    got = exchange(sums[4:], y, x)
    gram = gram + exchange(gram, x, y)
    got, gram = tie((got, gram))
    sums = sums[:4] + got
    gram = gram + exchange(gram, y, x)
    over_z = [exchange(sums[i], away) for i, away in ((3, z | zz), (2, zz), (1, z))]
    for bit in range(low_bits):
        gram = gram + exchange(gram, 1 << bit)
    sums, gram = tie((sums, gram))
    inverse = factor_call(gram)
    sums = [sums[0], *over_z]
    if low_bits > 0:
        sums = sum(sums)
        for bit in reversed(range(low_bits)):
            half = sums.shape[1] // 2
            mine = lax.rem(lax.shift_right_logical(me, bit), 2) == 1
            left, right = sums[:, :half], sums[:, half:]
            sums = jnp.where(mine, right, left) + exchange(jnp.where(mine, left, right), 1 << bit)
        sums = [sums]
    factor = (float(width) / float(total_rows)) ** 0.5
    return tuple(finish_call(inverse, first, total_rows, factor, sums))


def solution(mesh):
    return jax.shard_map(
        local,
        mesh=mesh,
        in_specs=(P(AXES, None), P()),
        out_specs=(P(AXES, None), P(AXES, None)),
        check_vma=False,
    )
```

```python
import functools

import jax
import jax.numpy as jnp
from jax import lax
from jax.experimental import pallas as pl
from jax.experimental.pallas import tpu as pltpu
from jax.sharding import PartitionSpec as P

AXES = ("rows", "grp")
HIGHEST = lax.Precision.HIGHEST
LANES = 128
VMEM_LIMIT = 24 * 1024 * 1024
AHEAD = 2


def project(out_ref, split_ref, slab_ref, owner, sibling, first_place):
    rank = out_ref.shape[1]
    wanted = lax.bitwise_xor(lax.bitwise_and(owner, 1), sibling)
    mine = lax.shift_right_logical(owner, 1)

    def columns(place):
        one, two = place // 8, place // 4 % 2
        away = jnp.where(wanted == 0, one + 2 * two, two + 2 * one) + 4 * (place % 4)
        at = pl.multiple_of((2 * lax.bitwise_xor(mine, away) + wanted) * LANES, LANES)
        return slab_ref[:, pl.ds(at, LANES)]

    for i in range(0, out_ref.shape[0], 2):
        place = first_place + i
        both = jnp.dot(
            split_ref[...], jnp.concatenate([columns(place), columns(place + 1)], axis=1),
            preferred_element_type=jnp.float32,
        )
        sums = both[:rank] + both[rank:]
        out_ref[i] = sums[:, :LANES]
        out_ref[i + 1] = sums[:, LANES:]


def pack(gram):
    half = gram.shape[0] // 2
    top, bottom = gram[:half], gram[half:]
    row = lax.broadcasted_iota(jnp.int32, top.shape, 0)
    column = lax.broadcasted_iota(jnp.int32, top.shape, 1)
    body = jnp.where(column - half < row, jnp.where(column < half, bottom, pltpu.roll(top, half, 1)), bottom)
    diagonal = jnp.sum(jnp.where(row == column, top, 0.0), axis=0, keepdims=True)
    tail = jnp.where(row[:8] == 0, jnp.broadcast_to(diagonal, (8, diagonal.shape[1])), 0.0)
    return jnp.concatenate([body, tail], axis=0)


def unpack(packed):
    half = packed.shape[0] - 8
    body = packed[:half]
    row = lax.broadcasted_iota(jnp.int32, body.shape, 0)
    column = lax.broadcasted_iota(jnp.int32, body.shape, 1)
    diagonal = jnp.broadcast_to(packed[half : half + 1], body.shape)
    top = jnp.where(column < row, pltpu.roll(body, half, 1), jnp.where(column == row, diagonal, 0.0))
    bottom = jnp.where(column - half < row, jnp.where(column < half, body, 0.0), body)
    parts = jnp.concatenate([top, bottom], axis=0)
    row = lax.broadcasted_iota(jnp.int32, parts.shape, 0)
    column = lax.broadcasted_iota(jnp.int32, parts.shape, 1)
    return parts + jnp.where(row == column, 0.0, parts.T)


def rows_kernel(
    owner_ref, slab_hbm, sketch_hbm, slab_ref, first_ref, gram_ref, split_ref, send_ref,
    sketch_ref, sum_ref, slab_sem, sketch_sem,
):
    rows, width = slab_ref.shape
    rank = sketch_ref.shape[1]
    starts = list(range(0, rows, LANES))
    copies = [
        pltpu.make_async_copy(
            slab_hbm.at[pl.ds(r, min(LANES, rows - r)), :],
            slab_ref.at[pl.ds(r, min(LANES, rows - r)), :],
            slab_sem.at[k],
        )
        for k, r in enumerate(starts)
    ]
    sketch_copy = pltpu.make_async_copy(sketch_hbm, sketch_ref, sketch_sem)
    sketch_copy.start()
    for copy in copies[:AHEAD]:
        copy.start()
    sketch_copy.wait()
    for k, r in enumerate(starts):
        copies[k].wait()
        if k + AHEAD < len(starts):
            copies[k + AHEAD].start()
        at = pl.ds(r, min(LANES, rows - r))
        first = jnp.dot(slab_ref[at, :], sketch_ref[...], preferred_element_type=jnp.float32)
        first_ref[at, :] = first
        turned = first.T
        high = turned.astype(jnp.bfloat16)
        split_ref[:rank, at] = high
        split_ref[rank:, at] = (turned - high.astype(jnp.float32)).astype(jnp.bfloat16)
        gram = jnp.dot(turned, first, precision=HIGHEST, preferred_element_type=jnp.float32)
        if k == 0:
            sum_ref[...] = gram
        else:
            sum_ref[...] += gram
    gram_ref[...] = pack(sum_ref[...])

    project(send_ref, split_ref, slab_ref, owner_ref[0], 1, 8)


def project_kernel(parts, owner_ref, split_ref, slab_ref, *out_refs):
    for (sibling, first_place), out_ref in zip(parts, out_refs):
        project(out_ref, split_ref, slab_ref, owner_ref[0], sibling, first_place)


def project_call(owner, split, slab, parts, name):
    rows, width = slab.shape
    rank = split.shape[0] // 2
    vmem = pl.BlockSpec(memory_space=pltpu.VMEM)
    chunks = jax.ShapeDtypeStruct((width // (4 * LANES), rank, LANES), jnp.float32)
    return pl.pallas_call(
        functools.partial(project_kernel, parts),
        in_specs=[pl.BlockSpec(memory_space=pltpu.SMEM), vmem, vmem],
        out_specs=[vmem] * len(parts),
        out_shape=[chunks] * len(parts),
        compiler_params=pltpu.CompilerParams(vmem_limit_bytes=VMEM_LIMIT),
        cost_estimate=pl.CostEstimate(
            flops=len(parts) * rows * width * rank, bytes_accessed=rows * width, transcendentals=0
        ),
        name=name,
    )(owner, split, slab)


def rows_call(owner, slab, sketch):
    rows, width = slab.shape
    rank = sketch.shape[1]
    vmem = pl.BlockSpec(memory_space=pltpu.VMEM)
    chunks = (width // (4 * LANES), rank, LANES)
    return pl.pallas_call(
        rows_kernel,
        in_specs=[
            pl.BlockSpec(memory_space=pltpu.SMEM),
            pl.BlockSpec(memory_space=pltpu.HBM),
            pl.BlockSpec(memory_space=pltpu.HBM),
        ],
        out_specs=[vmem] * 5,
        out_shape=[
            jax.ShapeDtypeStruct((rows, width), jnp.bfloat16),
            jax.ShapeDtypeStruct((rows, rank), jnp.float32),
            jax.ShapeDtypeStruct((rank // 2 + 8, rank), jnp.float32),
            jax.ShapeDtypeStruct((2 * rank, rows), jnp.bfloat16),
            jax.ShapeDtypeStruct(chunks, jnp.float32),
        ],
        scratch_shapes=[
            pltpu.VMEM((width, rank), jnp.bfloat16),
            pltpu.VMEM((rank, rank), jnp.float32),
            pltpu.SemaphoreType.DMA((-(-rows // LANES),)),
            pltpu.SemaphoreType.DMA,
        ],
        compiler_params=pltpu.CompilerParams(vmem_limit_bytes=VMEM_LIMIT),
        cost_estimate=pl.CostEstimate(
            flops=3 * rows * width * rank, bytes_accessed=rows * width * 2, transcendentals=0
        ),
        name="sketch_rows",
    )(
        owner,
        pltpu.with_memory_space_constraint(slab, pltpu.HBM),
        pltpu.with_memory_space_constraint(sketch, pltpu.HBM),
    )


def lane(block, at):
    return jnp.broadcast_to(block[:, at : at + 1], block.shape)


def sublane(block, at):
    return jnp.broadcast_to(block[at : at + 1, :], block.shape)


def inverse_factor(gram, inverse_ref):
    size = gram.shape[0]
    blocks = size // 8
    left = [gram[8 * i : 8 * i + 8, :] for i in range(blocks)]
    row_at = lax.broadcasted_iota(jnp.int32, (8, size), 0)
    lane_at = lax.broadcasted_iota(jnp.int32, (8, size), 1)
    right = [jnp.where(lane_at == row_at + 8 * i, 1.0, 0.0).astype(jnp.float32) for i in range(blocks)]
    for p in range(blocks):
        column = [lane(left[p], 8 * p + k) for k in range(8)]
        entry = {(r, c): sublane(column[c], r) for c in range(8) for r in range(c, 8)}
        scale, lower = [], {}
        for k in range(8):
            scale.append(lax.rsqrt(entry[k, k]))
            for r in range(k + 1, 8):
                lower[r, k] = entry[r, k] * scale[k]
            for c in range(k + 1, 8):
                for r in range(c, 8):
                    entry[r, c] = entry[r, c] - lower[r, k] * lower[c, k]
        tops, sides = [], []
        for k in range(8):
            top, side = sublane(left[p], k), sublane(right[p], k)
            for j in range(k):
                top = top - lower[k, j] * tops[j]
                side = side - lower[k, j] * sides[j]
            tops.append(top * scale[k])
            sides.append(side * scale[k])
        result = sides[0]
        for k in range(1, 8):
            result = jnp.where(row_at == k, sides[k], result)
        inverse_ref[8 * p : 8 * p + 8, :] = result
        for i in range(p + 1, blocks):
            weights = []
            for k in range(8):
                weight = lane(left[i], 8 * p + k)
                for j in range(k):
                    weight = weight - lower[k, j] * weights[j]
                weights.append(weight * scale[k])
            for k in range(8):
                left[i] = left[i] - weights[k] * tops[k]
                right[i] = right[i] - weights[k] * sides[k]


def factor_kernel(gram_ref, inverse_ref):
    inverse_factor(unpack(gram_ref[...]), inverse_ref)


def factor_call(gram):
    return pl.pallas_call(
        factor_kernel,
        in_specs=[pl.BlockSpec(memory_space=pltpu.VMEM)],
        out_specs=pl.BlockSpec(memory_space=pltpu.VMEM),
        out_shape=jax.ShapeDtypeStruct((gram.shape[1], gram.shape[1]), jnp.float32),
        compiler_params=pltpu.CompilerParams(vmem_limit_bytes=VMEM_LIMIT),
        cost_estimate=pl.CostEstimate(
            flops=4000000000, bytes_accessed=gram.size * 8, transcendentals=gram.shape[0]
        ),
        name="factor",
    )(gram)


def finish_kernel(basis_factor, factor, inverse_ref, first_ref, sums_ref, *refs):
    basis_ref, out_ref = refs[-2:]
    inverse = inverse_ref[...]
    one = lax.dot_general(
        first_ref[...], inverse, (((1,), (1,)), ((), ())),
        precision=HIGHEST, preferred_element_type=jnp.float32,
    )
    basis_ref[...] = one * basis_factor
    sums = sums_ref[...]
    for got_ref in refs[:-2]:
        sums = sums + got_ref[...]
    result = jnp.dot(inverse, sums, precision=HIGHEST, preferred_element_type=jnp.float32)
    out_ref[...] = (result.T * factor).astype(out_ref.dtype)


def finish_call(inverse, first, total_rows, factor, sums):
    rows, rank = first.shape
    own = sums[0].shape[1]
    return pl.pallas_call(
        functools.partial(finish_kernel, float(total_rows) ** 0.5, factor),
        in_specs=[pl.BlockSpec(memory_space=pltpu.VMEM)] * (2 + len(sums)),
        out_shape=[
            jax.ShapeDtypeStruct((rows, rank), jnp.float32),
            jax.ShapeDtypeStruct((own, rank), jnp.bfloat16),
        ],
        compiler_params=pltpu.CompilerParams(vmem_limit_bytes=VMEM_LIMIT),
        cost_estimate=pl.CostEstimate(
            flops=12 * rows * rank * rank, bytes_accessed=rows * rank * 8, transcendentals=0
        ),
        name="finish",
    )(inverse, first, *sums)


def local(slab, sketch):
    rows_loc, width = slab.shape
    devices_all = lax.axis_size(AXES)
    own = width // devices_all
    bits = devices_all.bit_length() - 1
    low_bits = bits - ((width // LANES).bit_length() - 1)
    total_rows = rows_loc * devices_all
    me = lax.axis_index(AXES)

    core, x, y, z, zz = [1 << bit for bit in range(low_bits, low_bits + 5)]
    tie = lax.optimization_barrier

    def exchange(array, away, away_odd=None):
        odd = away if away_odd is None else away_odd
        pairs = [(i, i ^ (odd if i & core else away)) for i in range(devices_all)]
        return lax.ppermute(array, AXES, pairs)

    owner = lax.shift_right_logical(me, low_bits).astype(jnp.int32).reshape(1)
    near, first, gram, split, send = rows_call(owner, slab, sketch)
    got = exchange(send, core)
    keep, = project_call(owner, split, near, ((0, 8),), "project_first")
    got, gram = tie((got, gram + exchange(gram, core)))
    far, split = tie((keep + got, split))
    got = exchange(far, x, y)
    send, sums = project_call(owner, split, near, ((1, 0), (0, 0)), "project_rest")
    sums = sums + exchange(send, core)
    over_z = [exchange(gram, away) for away in (z | zz, zz, z)]
    got, over_z[0] = tie((got, over_z[0]))
    sums, gram = tie((sums + got, gram))
    got = exchange(sums[4:], y, x)
    gram = (gram + over_z[2]) + (over_z[1] + over_z[0])
    gram = gram + exchange(gram, x, y)
    got, gram = tie((got, gram))
    sums = sums[:4] + got
    gram = gram + exchange(gram, y, x)
    over_z = [exchange(sums[i], away) for i, away in ((3, z | zz), (2, zz), (1, z))]
    for bit in range(low_bits):
        gram = gram + exchange(gram, 1 << bit)
    sums, gram = tie((sums, gram))
    inverse = factor_call(gram)
    sums = [sums[0], *over_z]
    if low_bits > 0:
        sums = sum(sums)
        for bit in reversed(range(low_bits)):
            half = sums.shape[1] // 2
            mine = lax.rem(lax.shift_right_logical(me, bit), 2) == 1
            left, right = sums[:, :half], sums[:, half:]
            sums = jnp.where(mine, right, left) + exchange(jnp.where(mine, left, right), 1 << bit)
        sums = [sums]
    factor = (float(width) / float(total_rows)) ** 0.5
    return tuple(finish_call(inverse, first, total_rows, factor, sums))


def solution(mesh):
    return jax.shard_map(
        local,
        mesh=mesh,
        in_specs=(P(AXES, None), P()),
        out_specs=(P(AXES, None), P(AXES, None)),
        check_vma=False,
    )
```

```python
import functools

import jax
import jax.numpy as jnp
from jax import lax
from jax.experimental import pallas as pl
from jax.experimental.pallas import tpu as pltpu
from jax.sharding import PartitionSpec as P

AXES = ("rows", "grp")
HIGHEST = lax.Precision.HIGHEST
LANES = 128
VMEM_LIMIT = 24 * 1024 * 1024
AHEAD = 2


def project(out_ref, split_ref, slab_ref, owner, sibling, first_place):
    rank = out_ref.shape[1]
    wanted = lax.bitwise_xor(lax.bitwise_and(owner, 1), sibling)
    mine = lax.shift_right_logical(owner, 1)

    def columns(place):
        one, rest = place // 8, place % 8
        even = one + 2 * (rest // 4) + 4 * (rest % 4)
        odd = 2 * one + rest % 2 + 4 * (rest // 2)
        away = jnp.where(wanted == 0, even, odd)
        at = pl.multiple_of((2 * lax.bitwise_xor(mine, away) + wanted) * LANES, LANES)
        return slab_ref[:, pl.ds(at, LANES)]

    for i in range(0, out_ref.shape[0], 2):
        place = first_place + i
        both = jnp.dot(
            split_ref[...], jnp.concatenate([columns(place), columns(place + 1)], axis=1),
            preferred_element_type=jnp.float32,
        )
        sums = both[:rank] + both[rank:]
        out_ref[i] = sums[:, :LANES]
        out_ref[i + 1] = sums[:, LANES:]


def pack(gram):
    half = gram.shape[0] // 2
    top, bottom = gram[:half], gram[half:]
    row = lax.broadcasted_iota(jnp.int32, top.shape, 0)
    column = lax.broadcasted_iota(jnp.int32, top.shape, 1)
    body = jnp.where(column - half < row, jnp.where(column < half, bottom, pltpu.roll(top, half, 1)), bottom)
    diagonal = jnp.sum(jnp.where(row == column, top, 0.0), axis=0, keepdims=True)
    tail = jnp.where(row[:8] == 0, jnp.broadcast_to(diagonal, (8, diagonal.shape[1])), 0.0)
    return jnp.concatenate([body, tail], axis=0)


def unpack(packed):
    half = packed.shape[0] - 8
    body = packed[:half]
    row = lax.broadcasted_iota(jnp.int32, body.shape, 0)
    column = lax.broadcasted_iota(jnp.int32, body.shape, 1)
    diagonal = jnp.broadcast_to(packed[half : half + 1], body.shape)
    top = jnp.where(column < row, pltpu.roll(body, half, 1), jnp.where(column == row, diagonal, 0.0))
    bottom = jnp.where(column - half < row, jnp.where(column < half, body, 0.0), body)
    parts = jnp.concatenate([top, bottom], axis=0)
    row = lax.broadcasted_iota(jnp.int32, parts.shape, 0)
    column = lax.broadcasted_iota(jnp.int32, parts.shape, 1)
    return parts + jnp.where(row == column, 0.0, parts.T)


def rows_kernel(
    owner_ref, slab_hbm, sketch_hbm, slab_ref, first_ref, gram_ref, split_ref, send_ref,
    sketch_ref, sum_ref, slab_sem, sketch_sem,
):
    rows, width = slab_ref.shape
    rank = sketch_ref.shape[1]
    starts = list(range(0, rows, LANES))
    copies = [
        pltpu.make_async_copy(
            slab_hbm.at[pl.ds(r, min(LANES, rows - r)), :],
            slab_ref.at[pl.ds(r, min(LANES, rows - r)), :],
            slab_sem.at[k],
        )
        for k, r in enumerate(starts)
    ]
    sketch_copy = pltpu.make_async_copy(sketch_hbm, sketch_ref, sketch_sem)
    sketch_copy.start()
    for copy in copies[:AHEAD]:
        copy.start()
    sketch_copy.wait()
    for k, r in enumerate(starts):
        copies[k].wait()
        if k + AHEAD < len(starts):
            copies[k + AHEAD].start()
        at = pl.ds(r, min(LANES, rows - r))
        first = jnp.dot(slab_ref[at, :], sketch_ref[...], preferred_element_type=jnp.float32)
        first_ref[at, :] = first
        turned = first.T
        high = turned.astype(jnp.bfloat16)
        split_ref[:rank, at] = high
        split_ref[rank:, at] = (turned - high.astype(jnp.float32)).astype(jnp.bfloat16)
        gram = jnp.dot(turned, first, precision=HIGHEST, preferred_element_type=jnp.float32)
        if k == 0:
            sum_ref[...] = gram
        else:
            sum_ref[...] += gram
    gram_ref[...] = pack(sum_ref[...])

    project(send_ref, split_ref, slab_ref, owner_ref[0], 1, 8)


def project_kernel(parts, owner_ref, split_ref, slab_ref, *out_refs):
    for (sibling, first_place), out_ref in zip(parts, out_refs):
        project(out_ref, split_ref, slab_ref, owner_ref[0], sibling, first_place)


def project_call(owner, split, slab, parts, name):
    rows, width = slab.shape
    rank = split.shape[0] // 2
    vmem = pl.BlockSpec(memory_space=pltpu.VMEM)
    chunks = jax.ShapeDtypeStruct((width // (4 * LANES), rank, LANES), jnp.float32)
    return pl.pallas_call(
        functools.partial(project_kernel, parts),
        in_specs=[pl.BlockSpec(memory_space=pltpu.SMEM), vmem, vmem],
        out_specs=[vmem] * len(parts),
        out_shape=[chunks] * len(parts),
        compiler_params=pltpu.CompilerParams(vmem_limit_bytes=VMEM_LIMIT),
        cost_estimate=pl.CostEstimate(
            flops=len(parts) * rows * width * rank, bytes_accessed=rows * width, transcendentals=0
        ),
        name=name,
    )(owner, split, slab)


def rows_call(owner, slab, sketch):
    rows, width = slab.shape
    rank = sketch.shape[1]
    vmem = pl.BlockSpec(memory_space=pltpu.VMEM)
    chunks = (width // (4 * LANES), rank, LANES)
    return pl.pallas_call(
        rows_kernel,
        in_specs=[
            pl.BlockSpec(memory_space=pltpu.SMEM),
            pl.BlockSpec(memory_space=pltpu.HBM),
            pl.BlockSpec(memory_space=pltpu.HBM),
        ],
        out_specs=[vmem] * 5,
        out_shape=[
            jax.ShapeDtypeStruct((rows, width), jnp.bfloat16),
            jax.ShapeDtypeStruct((rows, rank), jnp.float32),
            jax.ShapeDtypeStruct((rank // 2 + 8, rank), jnp.float32),
            jax.ShapeDtypeStruct((2 * rank, rows), jnp.bfloat16),
            jax.ShapeDtypeStruct(chunks, jnp.float32),
        ],
        scratch_shapes=[
            pltpu.VMEM((width, rank), jnp.bfloat16),
            pltpu.VMEM((rank, rank), jnp.float32),
            pltpu.SemaphoreType.DMA((-(-rows // LANES),)),
            pltpu.SemaphoreType.DMA,
        ],
        compiler_params=pltpu.CompilerParams(vmem_limit_bytes=VMEM_LIMIT),
        cost_estimate=pl.CostEstimate(
            flops=3 * rows * width * rank, bytes_accessed=rows * width * 2, transcendentals=0
        ),
        name="sketch_rows",
    )(
        owner,
        pltpu.with_memory_space_constraint(slab, pltpu.HBM),
        pltpu.with_memory_space_constraint(sketch, pltpu.HBM),
    )


def lane(block, at):
    return jnp.broadcast_to(block[:, at : at + 1], block.shape)


def sublane(block, at):
    return jnp.broadcast_to(block[at : at + 1, :], block.shape)


def inverse_factor(gram, inverse_ref):
    size = gram.shape[0]
    blocks = size // 8
    left = [gram[8 * i : 8 * i + 8, :] for i in range(blocks)]
    row_at = lax.broadcasted_iota(jnp.int32, (8, size), 0)
    lane_at = lax.broadcasted_iota(jnp.int32, (8, size), 1)
    right = [jnp.where(lane_at == row_at + 8 * i, 1.0, 0.0).astype(jnp.float32) for i in range(blocks)]
    for p in range(blocks):
        column = [lane(left[p], 8 * p + k) for k in range(8)]
        entry = {(r, c): sublane(column[c], r) for c in range(8) for r in range(c, 8)}
        scale, lower = [], {}
        for k in range(8):
            scale.append(lax.rsqrt(entry[k, k]))
            for r in range(k + 1, 8):
                lower[r, k] = entry[r, k] * scale[k]
            for c in range(k + 1, 8):
                for r in range(c, 8):
                    entry[r, c] = entry[r, c] - lower[r, k] * lower[c, k]
        tops, sides = [], []
        for k in range(8):
            top, side = sublane(left[p], k), sublane(right[p], k)
            for j in range(k):
                top = top - lower[k, j] * tops[j]
                side = side - lower[k, j] * sides[j]
            tops.append(top * scale[k])
            sides.append(side * scale[k])
        result = sides[0]
        for k in range(1, 8):
            result = jnp.where(row_at == k, sides[k], result)
        inverse_ref[8 * p : 8 * p + 8, :] = result
        for i in range(p + 1, blocks):
            weights = []
            for k in range(8):
                weight = lane(left[i], 8 * p + k)
                for j in range(k):
                    weight = weight - lower[k, j] * weights[j]
                weights.append(weight * scale[k])
            for k in range(8):
                left[i] = left[i] - weights[k] * tops[k]
                right[i] = right[i] - weights[k] * sides[k]


def factor_kernel(gram_ref, inverse_ref):
    inverse_factor(unpack(gram_ref[...]), inverse_ref)


def factor_call(gram):
    return pl.pallas_call(
        factor_kernel,
        in_specs=[pl.BlockSpec(memory_space=pltpu.VMEM)],
        out_specs=pl.BlockSpec(memory_space=pltpu.VMEM),
        out_shape=jax.ShapeDtypeStruct((gram.shape[1], gram.shape[1]), jnp.float32),
        compiler_params=pltpu.CompilerParams(vmem_limit_bytes=VMEM_LIMIT),
        cost_estimate=pl.CostEstimate(
            flops=4000000000, bytes_accessed=gram.size * 8, transcendentals=gram.shape[0]
        ),
        name="factor",
    )(gram)


def finish_kernel(basis_factor, factor, inverse_ref, first_ref, sums_ref, *refs):
    basis_ref, out_ref = refs[-2:]
    inverse = inverse_ref[...]
    one = lax.dot_general(
        first_ref[...], inverse, (((1,), (1,)), ((), ())),
        precision=HIGHEST, preferred_element_type=jnp.float32,
    )
    basis_ref[...] = one * basis_factor
    sums = sums_ref[...]
    for got_ref in refs[:-2]:
        sums = sums + got_ref[...]
    result = jnp.dot(inverse, sums, precision=HIGHEST, preferred_element_type=jnp.float32)
    out_ref[...] = (result.T * factor).astype(out_ref.dtype)


def finish_call(inverse, first, total_rows, factor, sums):
    rows, rank = first.shape
    own = sums[0].shape[1]
    return pl.pallas_call(
        functools.partial(finish_kernel, float(total_rows) ** 0.5, factor),
        in_specs=[pl.BlockSpec(memory_space=pltpu.VMEM)] * (2 + len(sums)),
        out_shape=[
            jax.ShapeDtypeStruct((rows, rank), jnp.float32),
            jax.ShapeDtypeStruct((own, rank), jnp.bfloat16),
        ],
        compiler_params=pltpu.CompilerParams(vmem_limit_bytes=VMEM_LIMIT),
        cost_estimate=pl.CostEstimate(
            flops=12 * rows * rank * rank, bytes_accessed=rows * rank * 8, transcendentals=0
        ),
        name="finish",
    )(inverse, first, *sums)


def local(slab, sketch):
    rows_loc, width = slab.shape
    devices_all = lax.axis_size(AXES)
    own = width // devices_all
    bits = devices_all.bit_length() - 1
    low_bits = bits - ((width // LANES).bit_length() - 1)
    total_rows = rows_loc * devices_all
    me = lax.axis_index(AXES)

    core, x, y, z, zz = [1 << bit for bit in range(low_bits, low_bits + 5)]
    tie = lax.optimization_barrier

    def exchange(array, away, away_odd=None):
        odd = away if away_odd is None else away_odd
        pairs = [(i, i ^ (odd if i & core else away)) for i in range(devices_all)]
        return lax.ppermute(array, AXES, [(i, j) for i, j in pairs if i != j])

    owner = lax.shift_right_logical(me, low_bits).astype(jnp.int32).reshape(1)
    near, first, gram, split, send = rows_call(owner, slab, sketch)
    got = exchange(send, core)
    keep, = project_call(owner, split, near, ((0, 8),), "project_first")
    got, gram = tie((got, gram + exchange(gram, core)))
    far, split = tie((keep + got, split))
    got = exchange(far, x, y)
    send, sums = project_call(owner, split, near, ((1, 0), (0, 0)), "project_rest")
    sums = sums + exchange(send, core)
    over_z = [exchange(gram, away) for away in (z | zz, zz, z)]
    got, over_z[0] = tie((got, over_z[0]))
    sums, gram = tie((sums + got, gram))
    got_far = exchange(sums[6:], y, z | zz)
    got_mid = exchange(sums[4:6], y, zz)
    got_near = exchange(sums[2:4], 0, z)
    gram = (gram + over_z[2]) + (over_z[1] + over_z[0])
    got_gram = exchange(gram, x)
    upper, gram = tie((sums[2:4] + got_far, gram))
    over_z = [exchange(upper[1], z | zz, 0), exchange(upper[0], zz, 0)]
    gram = gram + got_gram
    got_gram = exchange(gram, y)
    sums = sums[:2] + got_mid + got_near + jnp.where(lax.bitwise_and(owner[0], 1) == 1, got_far, 0.0)
    sums, gram = tie((sums, gram))
    over_z.append(exchange(sums[1], z, x))
    gram = gram + got_gram
    for bit in range(low_bits):
        gram = gram + exchange(gram, 1 << bit)
    sums, gram = tie((sums, gram))
    inverse = factor_call(gram)
    sums = [sums[0], *over_z]
    if low_bits > 0:
        sums = sum(sums)
        for bit in reversed(range(low_bits)):
            half = sums.shape[1] // 2
            mine = lax.rem(lax.shift_right_logical(me, bit), 2) == 1
            left, right = sums[:, :half], sums[:, half:]
            sums = jnp.where(mine, right, left) + exchange(jnp.where(mine, left, right), 1 << bit)
        sums = [sums]
    factor = (float(width) / float(total_rows)) ** 0.5
    return tuple(finish_call(inverse, first, total_rows, factor, sums))


def solution(mesh):
    return jax.shard_map(
        local,
        mesh=mesh,
        in_specs=(P(AXES, None), P()),
        out_specs=(P(AXES, None), P(AXES, None)),
        check_vma=False,
    )
```

```python
import functools

import jax
import jax.numpy as jnp
from jax import lax
from jax.experimental import pallas as pl
from jax.experimental.pallas import tpu as pltpu
from jax.sharding import PartitionSpec as P

AXES = ("rows", "grp")
HIGHEST = lax.Precision.HIGHEST
LANES = 128
VMEM_LIMIT = 24 * 1024 * 1024
AHEAD = 2
ROWS = 256


def project(out_ref, split_ref, slab_ref, owner, sibling, first_place):
    rank = out_ref.shape[1]
    wanted = lax.bitwise_xor(lax.bitwise_and(owner, 1), sibling)
    mine = lax.shift_right_logical(owner, 1)

    def columns(place):
        one, two = place // 8, place // 4 % 2
        away = jnp.where(wanted == 0, one + 2 * two, two + 2 * one) + 4 * (place % 4)
        at = pl.multiple_of((2 * lax.bitwise_xor(mine, away) + wanted) * LANES, LANES)
        return slab_ref[:, pl.ds(at, LANES)]

    for i in range(0, out_ref.shape[0], 2):
        place = first_place + i
        both = jnp.dot(
            split_ref[...], jnp.concatenate([columns(place), columns(place + 1)], axis=1),
            preferred_element_type=jnp.float32,
        )
        sums = both[:rank] + both[rank:]
        out_ref[i] = sums[:, :LANES]
        out_ref[i + 1] = sums[:, LANES:]


def pack(gram):
    half = gram.shape[0] // 2
    top, bottom = gram[:half], gram[half:]
    row = lax.broadcasted_iota(jnp.int32, top.shape, 0)
    column = lax.broadcasted_iota(jnp.int32, top.shape, 1)
    body = jnp.where(column - half < row, jnp.where(column < half, bottom, pltpu.roll(top, half, 1)), bottom)
    diagonal = jnp.sum(jnp.where(row == column, top, 0.0), axis=0, keepdims=True)
    tail = jnp.where(row[:8] == 0, jnp.broadcast_to(diagonal, (8, diagonal.shape[1])), 0.0)
    return jnp.concatenate([body, tail], axis=0)


def unpack(packed):
    half = packed.shape[0] - 8
    body = packed[:half]
    row = lax.broadcasted_iota(jnp.int32, body.shape, 0)
    column = lax.broadcasted_iota(jnp.int32, body.shape, 1)
    diagonal = jnp.broadcast_to(packed[half : half + 1], body.shape)
    top = jnp.where(column < row, pltpu.roll(body, half, 1), jnp.where(column == row, diagonal, 0.0))
    bottom = jnp.where(column - half < row, jnp.where(column < half, body, 0.0), body)
    parts = jnp.concatenate([top, bottom], axis=0)
    row = lax.broadcasted_iota(jnp.int32, parts.shape, 0)
    column = lax.broadcasted_iota(jnp.int32, parts.shape, 1)
    return parts + jnp.where(row == column, 0.0, parts.T)


def rows_kernel(
    owner_ref, slab_hbm, sketch_hbm, slab_ref, first_ref, gram_ref, split_ref, send_ref,
    sketch_ref, sum_ref, slab_sem, sketch_sem,
):
    rows, width = slab_ref.shape
    rank = sketch_ref.shape[1]
    starts = list(range(0, rows, ROWS))
    copies = [
        pltpu.make_async_copy(
            slab_hbm.at[pl.ds(r, min(ROWS, rows - r)), :],
            slab_ref.at[pl.ds(r, min(ROWS, rows - r)), :],
            slab_sem.at[k],
        )
        for k, r in enumerate(starts)
    ]
    sketch_copy = pltpu.make_async_copy(sketch_hbm, sketch_ref, sketch_sem)
    sketch_copy.start()
    for copy in copies[:AHEAD]:
        copy.start()
    sketch_copy.wait()
    for k, r in enumerate(starts):
        copies[k].wait()
        if k + AHEAD < len(starts):
            copies[k + AHEAD].start()
        at = pl.ds(r, min(ROWS, rows - r))
        first = jnp.dot(slab_ref[at, :], sketch_ref[...], preferred_element_type=jnp.float32)
        first_ref[at, :] = first
        turned = first.T
        high = turned.astype(jnp.bfloat16)
        split_ref[:rank, at] = high
        split_ref[rank:, at] = (turned - high.astype(jnp.float32)).astype(jnp.bfloat16)
        gram = jnp.dot(turned, first, precision=HIGHEST, preferred_element_type=jnp.float32)
        if k == 0:
            sum_ref[...] = gram
        else:
            sum_ref[...] += gram
    gram_ref[...] = pack(sum_ref[...])

    project(send_ref, split_ref, slab_ref, owner_ref[0], 1, 8)


def project_kernel(parts, owner_ref, split_ref, slab_ref, *out_refs):
    for (sibling, first_place), out_ref in zip(parts, out_refs):
        project(out_ref, split_ref, slab_ref, owner_ref[0], sibling, first_place)


def project_call(owner, split, slab, parts, name):
    rows, width = slab.shape
    rank = split.shape[0] // 2
    vmem = pl.BlockSpec(memory_space=pltpu.VMEM)
    chunks = jax.ShapeDtypeStruct((width // (4 * LANES), rank, LANES), jnp.float32)
    return pl.pallas_call(
        functools.partial(project_kernel, parts),
        in_specs=[pl.BlockSpec(memory_space=pltpu.SMEM), vmem, vmem],
        out_specs=[vmem] * len(parts),
        out_shape=[chunks] * len(parts),
        compiler_params=pltpu.CompilerParams(vmem_limit_bytes=VMEM_LIMIT),
        cost_estimate=pl.CostEstimate(
            flops=len(parts) * rows * width * rank, bytes_accessed=rows * width, transcendentals=0
        ),
        name=name,
    )(owner, split, slab)


def rows_call(owner, slab, sketch):
    rows, width = slab.shape
    rank = sketch.shape[1]
    vmem = pl.BlockSpec(memory_space=pltpu.VMEM)
    chunks = (width // (4 * LANES), rank, LANES)
    return pl.pallas_call(
        rows_kernel,
        in_specs=[
            pl.BlockSpec(memory_space=pltpu.SMEM),
            pl.BlockSpec(memory_space=pltpu.HBM),
            pl.BlockSpec(memory_space=pltpu.HBM),
        ],
        out_specs=[vmem] * 5,
        out_shape=[
            jax.ShapeDtypeStruct((rows, width), jnp.bfloat16),
            jax.ShapeDtypeStruct((rows, rank), jnp.float32),
            jax.ShapeDtypeStruct((rank // 2 + 8, rank), jnp.float32),
            jax.ShapeDtypeStruct((2 * rank, rows), jnp.bfloat16),
            jax.ShapeDtypeStruct(chunks, jnp.float32),
        ],
        scratch_shapes=[
            pltpu.VMEM((width, rank), jnp.bfloat16),
            pltpu.VMEM((rank, rank), jnp.float32),
            pltpu.SemaphoreType.DMA((-(-rows // ROWS),)),
            pltpu.SemaphoreType.DMA,
        ],
        compiler_params=pltpu.CompilerParams(vmem_limit_bytes=VMEM_LIMIT),
        cost_estimate=pl.CostEstimate(
            flops=3 * rows * width * rank, bytes_accessed=rows * width * 2, transcendentals=0
        ),
        name="sketch_rows",
    )(
        owner,
        pltpu.with_memory_space_constraint(slab, pltpu.HBM),
        pltpu.with_memory_space_constraint(sketch, pltpu.HBM),
    )


def lane(block, at):
    return jnp.broadcast_to(block[:, at : at + 1], block.shape)


def sublane(block, at):
    return jnp.broadcast_to(block[at : at + 1, :], block.shape)


def inverse_factor(gram, inverse_ref):
    size = gram.shape[0]
    blocks = size // 8
    left = [gram[8 * i : 8 * i + 8, :] for i in range(blocks)]
    row_at = lax.broadcasted_iota(jnp.int32, (8, size), 0)
    lane_at = lax.broadcasted_iota(jnp.int32, (8, size), 1)
    right = [jnp.where(lane_at == row_at + 8 * i, 1.0, 0.0).astype(jnp.float32) for i in range(blocks)]
    for p in range(blocks):
        column = [lane(left[p], 8 * p + k) for k in range(8)]
        entry = {(r, c): sublane(column[c], r) for c in range(8) for r in range(c, 8)}
        scale, lower = [], {}
        for k in range(8):
            scale.append(lax.rsqrt(entry[k, k]))
            for r in range(k + 1, 8):
                lower[r, k] = entry[r, k] * scale[k]
            for c in range(k + 1, 8):
                for r in range(c, 8):
                    entry[r, c] = entry[r, c] - lower[r, k] * lower[c, k]
        tops, sides = [], []
        for k in range(8):
            top, side = sublane(left[p], k), sublane(right[p], k)
            for j in range(k):
                top = top - lower[k, j] * tops[j]
                side = side - lower[k, j] * sides[j]
            tops.append(top * scale[k])
            sides.append(side * scale[k])
        result = sides[0]
        for k in range(1, 8):
            result = jnp.where(row_at == k, sides[k], result)
        inverse_ref[8 * p : 8 * p + 8, :] = result
        for i in range(p + 1, blocks):
            weights = []
            for k in range(8):
                weight = lane(left[i], 8 * p + k)
                for j in range(k):
                    weight = weight - lower[k, j] * weights[j]
                weights.append(weight * scale[k])
            for k in range(8):
                left[i] = left[i] - weights[k] * tops[k]
                right[i] = right[i] - weights[k] * sides[k]


def factor_kernel(gram_ref, inverse_ref):
    inverse_factor(unpack(gram_ref[...]), inverse_ref)


def factor_call(gram):
    return pl.pallas_call(
        factor_kernel,
        in_specs=[pl.BlockSpec(memory_space=pltpu.VMEM)],
        out_specs=pl.BlockSpec(memory_space=pltpu.VMEM),
        out_shape=jax.ShapeDtypeStruct((gram.shape[1], gram.shape[1]), jnp.float32),
        compiler_params=pltpu.CompilerParams(vmem_limit_bytes=VMEM_LIMIT),
        cost_estimate=pl.CostEstimate(
            flops=4000000000, bytes_accessed=gram.size * 8, transcendentals=gram.shape[0]
        ),
        name="factor",
    )(gram)


def finish_kernel(basis_factor, factor, inverse_ref, first_ref, sums_ref, *refs):
    basis_ref, out_ref = refs[-2:]
    inverse = inverse_ref[...]
    one = lax.dot_general(
        first_ref[...], inverse, (((1,), (1,)), ((), ())),
        precision=HIGHEST, preferred_element_type=jnp.float32,
    )
    basis_ref[...] = one * basis_factor
    sums = sums_ref[...]
    for got_ref in refs[:-2]:
        sums = sums + got_ref[...]
    result = jnp.dot(inverse, sums, precision=HIGHEST, preferred_element_type=jnp.float32)
    out_ref[...] = (result.T * factor).astype(out_ref.dtype)


def finish_call(inverse, first, total_rows, factor, sums):
    rows, rank = first.shape
    own = sums[0].shape[1]
    return pl.pallas_call(
        functools.partial(finish_kernel, float(total_rows) ** 0.5, factor),
        in_specs=[pl.BlockSpec(memory_space=pltpu.VMEM)] * (2 + len(sums)),
        out_shape=[
            jax.ShapeDtypeStruct((rows, rank), jnp.float32),
            jax.ShapeDtypeStruct((own, rank), jnp.bfloat16),
        ],
        compiler_params=pltpu.CompilerParams(vmem_limit_bytes=VMEM_LIMIT),
        cost_estimate=pl.CostEstimate(
            flops=12 * rows * rank * rank, bytes_accessed=rows * rank * 8, transcendentals=0
        ),
        name="finish",
    )(inverse, first, *sums)


def local(slab, sketch):
    rows_loc, width = slab.shape
    devices_all = lax.axis_size(AXES)
    own = width // devices_all
    bits = devices_all.bit_length() - 1
    low_bits = bits - ((width // LANES).bit_length() - 1)
    total_rows = rows_loc * devices_all
    me = lax.axis_index(AXES)

    core, x, y, z, zz = [1 << bit for bit in range(low_bits, low_bits + 5)]
    tie = lax.optimization_barrier

    def exchange(array, away, away_odd=None):
        odd = away if away_odd is None else away_odd
        pairs = [(i, i ^ (odd if i & core else away)) for i in range(devices_all)]
        return lax.ppermute(array, AXES, pairs)

    owner = lax.shift_right_logical(me, low_bits).astype(jnp.int32).reshape(1)
    near, first, gram, split, send = rows_call(owner, slab, sketch)
    got = exchange(send, core)
    keep, = project_call(owner, split, near, ((0, 8),), "project_first")
    got, gram = tie((got, gram + exchange(gram, core)))
    far, split = tie((keep + got, split))
    got = exchange(far, x, y)
    send, sums = project_call(owner, split, near, ((1, 0), (0, 0)), "project_rest")
    sums = sums + exchange(send, core)
    over_z = [exchange(gram, away) for away in (z | zz, zz, z)]
    got, over_z[0] = tie((got, over_z[0]))
    sums, gram = tie((sums + got, gram))
    got = exchange(sums[4:], y, x)
    gram = (gram + over_z[2]) + (over_z[1] + over_z[0])
    gram = gram + exchange(gram, x, y)
    got, gram = tie((got, gram))
    sums = sums[:4] + got
    gram = gram + exchange(gram, y, x)
    over_z = [exchange(sums[i], away) for i, away in ((1, z), (2, zz), (3, z | zz))]
    for bit in range(low_bits):
        gram = gram + exchange(gram, 1 << bit)
    sums, gram = tie((sums, gram))
    inverse = factor_call(gram)
    sums = [sums[0], *over_z]
    if low_bits > 0:
        sums = sum(sums)
        for bit in reversed(range(low_bits)):
            half = sums.shape[1] // 2
            mine = lax.rem(lax.shift_right_logical(me, bit), 2) == 1
            left, right = sums[:, :half], sums[:, half:]
            sums = jnp.where(mine, right, left) + exchange(jnp.where(mine, left, right), 1 << bit)
        sums = [sums]
    factor = (float(width) / float(total_rows)) ** 0.5
    return tuple(finish_call(inverse, first, total_rows, factor, sums))


def solution(mesh):
    return jax.shard_map(
        local,
        mesh=mesh,
        in_specs=(P(AXES, None), P()),
        out_specs=(P(AXES, None), P(AXES, None)),
        check_vma=False,
    )
```

```python
import functools

import jax
import jax.numpy as jnp
from jax import lax
from jax.experimental import pallas as pl
from jax.experimental.pallas import tpu as pltpu
from jax.sharding import PartitionSpec as P

AXES = ("rows", "grp")
HIGHEST = lax.Precision.HIGHEST
LANES = 128
VMEM_LIMIT = 24 * 1024 * 1024
AHEAD = 2
ROWS = 256


def project(out_ref, split_ref, slab_ref, owner, sibling, first_place):
    rank = out_ref.shape[1]
    wanted = lax.bitwise_xor(lax.bitwise_and(owner, 1), sibling)
    mine = lax.shift_right_logical(owner, 1)

    def columns(place):
        one, two = place // 8, place // 4 % 2
        away = jnp.where(wanted == 0, one + 2 * two, two + 2 * one) + 4 * (place % 4)
        at = pl.multiple_of((2 * lax.bitwise_xor(mine, away) + wanted) * LANES, LANES)
        return slab_ref[:, pl.ds(at, LANES)]

    for i in range(0, out_ref.shape[0], 2):
        place = first_place + i
        both = jnp.dot(
            split_ref[...], jnp.concatenate([columns(place), columns(place + 1)], axis=1),
            preferred_element_type=jnp.float32,
        )
        sums = both[:rank] + both[rank:]
        out_ref[i] = sums[:, :LANES]
        out_ref[i + 1] = sums[:, LANES:]


def pack(gram):
    half = gram.shape[0] // 2
    top, bottom = gram[:half], gram[half:]
    row = lax.broadcasted_iota(jnp.int32, top.shape, 0)
    column = lax.broadcasted_iota(jnp.int32, top.shape, 1)
    body = jnp.where(column - half < row, jnp.where(column < half, bottom, pltpu.roll(top, half, 1)), bottom)
    diagonal = jnp.sum(jnp.where(row == column, top, 0.0), axis=0, keepdims=True)
    tail = jnp.where(row[:8] == 0, jnp.broadcast_to(diagonal, (8, diagonal.shape[1])), 0.0)
    return jnp.concatenate([body, tail], axis=0)


def unpack(packed):
    half = packed.shape[0] - 8
    body = packed[:half]
    row = lax.broadcasted_iota(jnp.int32, body.shape, 0)
    column = lax.broadcasted_iota(jnp.int32, body.shape, 1)
    diagonal = jnp.broadcast_to(packed[half : half + 1], body.shape)
    top = jnp.where(column < row, pltpu.roll(body, half, 1), jnp.where(column == row, diagonal, 0.0))
    bottom = jnp.where(column - half < row, jnp.where(column < half, body, 0.0), body)
    parts = jnp.concatenate([top, bottom], axis=0)
    row = lax.broadcasted_iota(jnp.int32, parts.shape, 0)
    column = lax.broadcasted_iota(jnp.int32, parts.shape, 1)
    return parts + jnp.where(row == column, 0.0, parts.T)


def rows_kernel(
    owner_ref, slab_hbm, sketch_hbm, slab_ref, first_ref, gram_ref, split_ref, send_ref,
    sketch_ref, sum_ref, slab_sem, sketch_sem,
):
    rows, width = slab_ref.shape
    rank = sketch_ref.shape[1]
    starts = list(range(0, rows, ROWS))
    copies = [
        pltpu.make_async_copy(
            slab_hbm.at[pl.ds(r, min(ROWS, rows - r)), :],
            slab_ref.at[pl.ds(r, min(ROWS, rows - r)), :],
            slab_sem.at[k],
        )
        for k, r in enumerate(starts)
    ]
    sketch_copy = pltpu.make_async_copy(sketch_hbm, sketch_ref, sketch_sem)
    sketch_copy.start()
    for copy in copies[:AHEAD]:
        copy.start()
    sketch_copy.wait()
    for k, r in enumerate(starts):
        copies[k].wait()
        if k + AHEAD < len(starts):
            copies[k + AHEAD].start()
        at = pl.ds(r, min(ROWS, rows - r))
        first = jnp.dot(slab_ref[at, :], sketch_ref[...], preferred_element_type=jnp.float32)
        first_ref[at, :] = first
        turned = first.T
        high = turned.astype(jnp.bfloat16)
        split_ref[:rank, at] = high
        split_ref[rank:, at] = (turned - high.astype(jnp.float32)).astype(jnp.bfloat16)
        gram = jnp.dot(turned, first, precision=HIGHEST, preferred_element_type=jnp.float32)
        if k == 0:
            sum_ref[...] = gram
        else:
            sum_ref[...] += gram
    gram_ref[...] = pack(sum_ref[...])

    project(send_ref, split_ref, slab_ref, owner_ref[0], 1, 8)


def project_kernel(parts, owner_ref, split_ref, slab_ref, *out_refs):
    for (sibling, first_place), out_ref in zip(parts, out_refs):
        project(out_ref, split_ref, slab_ref, owner_ref[0], sibling, first_place)


def project_call(owner, split, slab, parts, name):
    rows, width = slab.shape
    rank = split.shape[0] // 2
    vmem = pl.BlockSpec(memory_space=pltpu.VMEM)
    chunks = jax.ShapeDtypeStruct((width // (4 * LANES), rank, LANES), jnp.float32)
    return pl.pallas_call(
        functools.partial(project_kernel, parts),
        in_specs=[pl.BlockSpec(memory_space=pltpu.SMEM), vmem, vmem],
        out_specs=[vmem] * len(parts),
        out_shape=[chunks] * len(parts),
        compiler_params=pltpu.CompilerParams(vmem_limit_bytes=VMEM_LIMIT),
        cost_estimate=pl.CostEstimate(
            flops=len(parts) * rows * width * rank, bytes_accessed=rows * width, transcendentals=0
        ),
        name=name,
    )(owner, split, slab)


def rows_call(owner, slab, sketch):
    rows, width = slab.shape
    rank = sketch.shape[1]
    vmem = pl.BlockSpec(memory_space=pltpu.VMEM)
    chunks = (width // (4 * LANES), rank, LANES)
    return pl.pallas_call(
        rows_kernel,
        in_specs=[
            pl.BlockSpec(memory_space=pltpu.SMEM),
            pl.BlockSpec(memory_space=pltpu.HBM),
            pl.BlockSpec(memory_space=pltpu.HBM),
        ],
        out_specs=[vmem] * 5,
        out_shape=[
            jax.ShapeDtypeStruct((rows, width), jnp.bfloat16),
            jax.ShapeDtypeStruct((rows, rank), jnp.float32),
            jax.ShapeDtypeStruct((rank // 2 + 8, rank), jnp.float32),
            jax.ShapeDtypeStruct((2 * rank, rows), jnp.bfloat16),
            jax.ShapeDtypeStruct(chunks, jnp.float32),
        ],
        scratch_shapes=[
            pltpu.VMEM((width, rank), jnp.bfloat16),
            pltpu.VMEM((rank, rank), jnp.float32),
            pltpu.SemaphoreType.DMA((-(-rows // ROWS),)),
            pltpu.SemaphoreType.DMA,
        ],
        compiler_params=pltpu.CompilerParams(vmem_limit_bytes=VMEM_LIMIT),
        cost_estimate=pl.CostEstimate(
            flops=3 * rows * width * rank, bytes_accessed=rows * width * 2, transcendentals=0
        ),
        name="sketch_rows",
    )(
        owner,
        pltpu.with_memory_space_constraint(slab, pltpu.HBM),
        pltpu.with_memory_space_constraint(sketch, pltpu.HBM),
    )


def lane(block, at):
    return jnp.broadcast_to(block[:, at : at + 1], block.shape)


def sublane(block, at):
    return jnp.broadcast_to(block[at : at + 1, :], block.shape)


def inverse_factor(gram, inverse_ref):
    size = gram.shape[0]
    blocks = [gram[i : i + 8, :] for i in range(0, size, 8)]
    row_at = lax.broadcasted_iota(jnp.int32, (8, size), 0)
    lane_at = lax.broadcasted_iota(jnp.int32, (8, size), 1)
    for p in range(len(blocks)):
        start = 8 * p
        column = [lane(blocks[p], start + k) for k in range(8)]
        entry = {(r, c): sublane(column[c], r) for c in range(8) for r in range(c, 8)}
        root, inverse, lower = [], [], {}
        for k in range(8):
            root.append(lax.rsqrt(entry[k, k]))
            inverse.append(root[k] * root[k])
            for r in range(k + 1, 8):
                lower[r, k] = entry[r, k] * inverse[k]
            for c in range(k + 1, 8):
                for r in range(c, 8):
                    entry[r, c] = entry[r, c] - lower[r, k] * entry[c, k]
        in_panel = (lane_at >= start) & (lane_at < start + 8)
        unit = jnp.where(lane_at - start == row_at, 1.0, 0.0)
        panel = jnp.where(in_panel, unit, blocks[p])
        tops = []
        for k in range(8):
            top = sublane(panel, k)
            for j in range(k):
                top = top - lower[k, j] * tops[j]
            tops.append(top)
        result, scale = tops[0], root[0]
        for k in range(1, 8):
            result = jnp.where(row_at == k, tops[k], result)
            scale = jnp.where(row_at == k, root[k], scale)
        inverse_ref[start : start + 8, :] = jnp.where(lane_at < start + 8, result * scale, 0.0)
        scaled = [tops[k] * inverse[k] for k in range(8)]
        for i in range(p + 1, len(blocks)):
            block = jnp.where(in_panel, 0.0, blocks[i])
            weights = []
            for k in range(8):
                weight = lane(blocks[i], start + k)
                for j in range(k):
                    weight = weight - lower[k, j] * weights[j]
                weights.append(weight)
                block = block - weight * scaled[k]
            blocks[i] = block


def factor_kernel(gram_ref, inverse_ref):
    inverse_factor(unpack(gram_ref[...]), inverse_ref)


def factor_call(gram):
    return pl.pallas_call(
        factor_kernel,
        in_specs=[pl.BlockSpec(memory_space=pltpu.VMEM)],
        out_specs=pl.BlockSpec(memory_space=pltpu.VMEM),
        out_shape=jax.ShapeDtypeStruct((gram.shape[1], gram.shape[1]), jnp.float32),
        compiler_params=pltpu.CompilerParams(vmem_limit_bytes=VMEM_LIMIT),
        cost_estimate=pl.CostEstimate(
            flops=4000000000, bytes_accessed=gram.size * 8, transcendentals=gram.shape[0]
        ),
        name="factor",
    )(gram)


def two_parts(array):
    high = array.astype(jnp.bfloat16)
    return high, (array - high.astype(jnp.float32)).astype(jnp.bfloat16)


def finish_kernel(basis_factor, factor, inverse_ref, first_ref, sums_ref, *refs):
    basis_ref, out_ref = refs[-2:]
    inverse = inverse_ref[...]
    high, low = two_parts(first_ref[...])
    inverse_high, inverse_low = two_parts(inverse.T * basis_factor)
    basis_ref[...] = jnp.dot(
        jnp.concatenate([high, high, low, low], axis=1),
        jnp.concatenate([inverse_high, inverse_low, inverse_high, inverse_low], axis=0),
        preferred_element_type=jnp.float32,
    )
    sums = sums_ref[...]
    for got_ref in refs[:-2]:
        sums = sums + got_ref[...]
    result = jnp.dot(inverse, sums, precision=HIGHEST, preferred_element_type=jnp.float32)
    out_ref[...] = (result.T * factor).astype(out_ref.dtype)


def finish_call(inverse, first, total_rows, factor, sums):
    rows, rank = first.shape
    own = sums[0].shape[1]
    return pl.pallas_call(
        functools.partial(finish_kernel, float(total_rows) ** 0.5, factor),
        in_specs=[pl.BlockSpec(memory_space=pltpu.VMEM)] * (2 + len(sums)),
        out_shape=[
            jax.ShapeDtypeStruct((rows, rank), jnp.float32),
            jax.ShapeDtypeStruct((own, rank), jnp.bfloat16),
        ],
        compiler_params=pltpu.CompilerParams(vmem_limit_bytes=VMEM_LIMIT),
        cost_estimate=pl.CostEstimate(
            flops=12 * rows * rank * rank, bytes_accessed=rows * rank * 8, transcendentals=0
        ),
        name="finish",
    )(inverse, first, *sums)


def local(slab, sketch):
    rows_loc, width = slab.shape
    devices_all = lax.axis_size(AXES)
    own = width // devices_all
    bits = devices_all.bit_length() - 1
    low_bits = bits - ((width // LANES).bit_length() - 1)
    total_rows = rows_loc * devices_all
    me = lax.axis_index(AXES)

    core, x, y, z, zz = [1 << bit for bit in range(low_bits, low_bits + 5)]
    tie = lax.optimization_barrier

    def exchange(array, away, away_odd=None):
        odd = away if away_odd is None else away_odd
        pairs = [(i, i ^ (odd if i & core else away)) for i in range(devices_all)]
        return lax.ppermute(array, AXES, pairs)

    owner = lax.shift_right_logical(me, low_bits).astype(jnp.int32).reshape(1)
    near, first, gram, split, send = rows_call(owner, slab, sketch)
    got = exchange(send, core)
    keep, = project_call(owner, split, near, ((0, 8),), "project_first")
    got, gram = tie((got, gram + exchange(gram, core)))
    far, split = tie((keep + got, split))
    got = exchange(far, x, y)
    send, sums = project_call(owner, split, near, ((1, 0), (0, 0)), "project_rest")
    sums = sums + exchange(send, core)
    over_z = [exchange(gram, away) for away in (z | zz, zz, z)]
    got, over_z[0] = tie((got, over_z[0]))
    sums, gram = tie((sums + got, gram))
    got = exchange(sums[4:], y, x)
    gram = (gram + over_z[2]) + (over_z[1] + over_z[0])
    gram = gram + exchange(gram, x, y)
    got, gram = tie((got, gram))
    sums = sums[:4] + got
    gram = gram + exchange(gram, y, x)
    over_z = [exchange(sums[i], away) for i, away in ((1, z), (2, zz), (3, z | zz))]
    for bit in range(low_bits):
        gram = gram + exchange(gram, 1 << bit)
    sums, gram = tie((sums, gram))
    inverse = factor_call(gram)
    sums = [sums[0], *over_z]
    if low_bits > 0:
        sums = sum(sums)
        for bit in reversed(range(low_bits)):
            half = sums.shape[1] // 2
            mine = lax.rem(lax.shift_right_logical(me, bit), 2) == 1
            left, right = sums[:, :half], sums[:, half:]
            sums = jnp.where(mine, right, left) + exchange(jnp.where(mine, left, right), 1 << bit)
        sums = [sums]
    factor = (float(width) / float(total_rows)) ** 0.5
    return tuple(finish_call(inverse, first, total_rows, factor, sums))


def solution(mesh):
    return jax.shard_map(
        local,
        mesh=mesh,
        in_specs=(P(AXES, None), P()),
        out_specs=(P(AXES, None), P(AXES, None)),
        check_vma=False,
    )
```

```python
import functools

import jax
import jax.numpy as jnp
from jax import lax
from jax.experimental import pallas as pl
from jax.experimental.pallas import tpu as pltpu
from jax.sharding import PartitionSpec as P

AXES = ("rows", "grp")
HIGHEST = lax.Precision.HIGHEST
LANES = 128
VMEM_LIMIT = 24 * 1024 * 1024
AHEAD = 1
ROWS = 256


def project(out_ref, split_ref, slab_ref, owner, sibling, first_place):
    rank = out_ref.shape[1]
    wanted = lax.bitwise_xor(lax.bitwise_and(owner, 1), sibling)
    mine = lax.shift_right_logical(owner, 1)

    def columns(place):
        one, two = place // 8, place // 4 % 2
        away = jnp.where(wanted == 0, one + 2 * two, two + 2 * one) + 4 * (place % 4)
        at = pl.multiple_of((2 * lax.bitwise_xor(mine, away) + wanted) * LANES, LANES)
        return slab_ref[:, pl.ds(at, LANES)]

    for i in range(0, out_ref.shape[0], 2):
        place = first_place + i
        both = jnp.dot(
            split_ref[...], jnp.concatenate([columns(place), columns(place + 1)], axis=1),
            preferred_element_type=jnp.float32,
        )
        sums = both[:rank] + both[rank:]
        out_ref[i] = sums[:, :LANES]
        out_ref[i + 1] = sums[:, LANES:]


def pack(gram):
    half = gram.shape[0] // 2
    top, bottom = gram[:half], gram[half:]
    row = lax.broadcasted_iota(jnp.int32, top.shape, 0)
    column = lax.broadcasted_iota(jnp.int32, top.shape, 1)
    body = jnp.where(column - half < row, jnp.where(column < half, bottom, pltpu.roll(top, half, 1)), bottom)
    diagonal = jnp.sum(jnp.where(row == column, top, 0.0), axis=0, keepdims=True)
    tail = jnp.where(row[:8] == 0, jnp.broadcast_to(diagonal, (8, diagonal.shape[1])), 0.0)
    return jnp.concatenate([body, tail], axis=0)


def unpack(packed):
    half = packed.shape[0] - 8
    body = packed[:half]
    row = lax.broadcasted_iota(jnp.int32, body.shape, 0)
    column = lax.broadcasted_iota(jnp.int32, body.shape, 1)
    diagonal = jnp.broadcast_to(packed[half : half + 1], body.shape)
    top = jnp.where(column < row, pltpu.roll(body, half, 1), jnp.where(column == row, diagonal, 0.0))
    bottom = jnp.where(column - half < row, jnp.where(column < half, body, 0.0), body)
    parts = jnp.concatenate([top, bottom], axis=0)
    row = lax.broadcasted_iota(jnp.int32, parts.shape, 0)
    column = lax.broadcasted_iota(jnp.int32, parts.shape, 1)
    return parts + jnp.where(row == column, 0.0, parts.T)


def rows_kernel(
    owner_ref, slab_hbm, sketch_hbm, slab_ref, first_ref, gram_ref, split_ref, send_ref,
    sketch_ref, sum_ref, slab_sem, sketch_sem,
):
    rows, width = slab_ref.shape
    rank = sketch_ref.shape[1]
    starts = list(range(0, rows, ROWS))
    copies = [
        pltpu.make_async_copy(
            slab_hbm.at[pl.ds(r, min(ROWS, rows - r)), :],
            slab_ref.at[pl.ds(r, min(ROWS, rows - r)), :],
            slab_sem.at[k],
        )
        for k, r in enumerate(starts)
    ]
    sketch_copy = pltpu.make_async_copy(sketch_hbm, sketch_ref, sketch_sem)
    sketch_copy.start()
    for copy in copies[:AHEAD]:
        copy.start()
    sketch_copy.wait()
    for k, r in enumerate(starts):
        copies[k].wait()
        if k + AHEAD < len(starts):
            copies[k + AHEAD].start()
        at = pl.ds(r, min(ROWS, rows - r))
        first = jnp.dot(slab_ref[at, :], sketch_ref[...], preferred_element_type=jnp.float32)
        first_ref[at, :] = first
        turned = first.T
        high = turned.astype(jnp.bfloat16)
        split_ref[:rank, at] = high
        split_ref[rank:, at] = (turned - high.astype(jnp.float32)).astype(jnp.bfloat16)
        gram = jnp.dot(turned, first, precision=HIGHEST, preferred_element_type=jnp.float32)
        if k == 0:
            sum_ref[...] = gram
        else:
            sum_ref[...] += gram
    gram_ref[...] = pack(sum_ref[...])

    project(send_ref, split_ref, slab_ref, owner_ref[0], 1, 8)


def project_kernel(parts, owner_ref, split_ref, slab_ref, *out_refs):
    for (sibling, first_place), out_ref in zip(parts, out_refs):
        project(out_ref, split_ref, slab_ref, owner_ref[0], sibling, first_place)


def project_call(owner, split, slab, parts, name):
    rows, width = slab.shape
    rank = split.shape[0] // 2
    vmem = pl.BlockSpec(memory_space=pltpu.VMEM)
    chunks = jax.ShapeDtypeStruct((width // (4 * LANES), rank, LANES), jnp.float32)
    return pl.pallas_call(
        functools.partial(project_kernel, parts),
        in_specs=[pl.BlockSpec(memory_space=pltpu.SMEM), vmem, vmem],
        out_specs=[vmem] * len(parts),
        out_shape=[chunks] * len(parts),
        compiler_params=pltpu.CompilerParams(vmem_limit_bytes=VMEM_LIMIT),
        cost_estimate=pl.CostEstimate(
            flops=len(parts) * rows * width * rank, bytes_accessed=rows * width, transcendentals=0
        ),
        name=name,
    )(owner, split, slab)


def rows_call(owner, slab, sketch):
    rows, width = slab.shape
    rank = sketch.shape[1]
    vmem = pl.BlockSpec(memory_space=pltpu.VMEM)
    chunks = (width // (4 * LANES), rank, LANES)
    return pl.pallas_call(
        rows_kernel,
        in_specs=[
            pl.BlockSpec(memory_space=pltpu.SMEM),
            pl.BlockSpec(memory_space=pltpu.HBM),
            pl.BlockSpec(memory_space=pltpu.HBM),
        ],
        out_specs=[vmem] * 5,
        out_shape=[
            jax.ShapeDtypeStruct((rows, width), jnp.bfloat16),
            jax.ShapeDtypeStruct((rows, rank), jnp.float32),
            jax.ShapeDtypeStruct((rank // 2 + 8, rank), jnp.float32),
            jax.ShapeDtypeStruct((2 * rank, rows), jnp.bfloat16),
            jax.ShapeDtypeStruct(chunks, jnp.float32),
        ],
        scratch_shapes=[
            pltpu.VMEM((width, rank), jnp.bfloat16),
            pltpu.VMEM((rank, rank), jnp.float32),
            pltpu.SemaphoreType.DMA((-(-rows // ROWS),)),
            pltpu.SemaphoreType.DMA,
        ],
        compiler_params=pltpu.CompilerParams(vmem_limit_bytes=VMEM_LIMIT),
        cost_estimate=pl.CostEstimate(
            flops=3 * rows * width * rank, bytes_accessed=rows * width * 2, transcendentals=0
        ),
        name="sketch_rows",
    )(
        owner,
        pltpu.with_memory_space_constraint(slab, pltpu.HBM),
        pltpu.with_memory_space_constraint(sketch, pltpu.HBM),
    )


def lane(block, at):
    return jnp.broadcast_to(block[:, at : at + 1], block.shape)


def sublane(block, at):
    return jnp.broadcast_to(block[at : at + 1, :], block.shape)


def inverse_factor(gram, inverse_ref):
    size = gram.shape[0]
    blocks = [gram[i : i + 8, :] for i in range(0, size, 8)]
    row_at = lax.broadcasted_iota(jnp.int32, (8, size), 0)
    lane_at = lax.broadcasted_iota(jnp.int32, (8, size), 1)
    for p in range(len(blocks)):
        start = 8 * p
        column = [lane(blocks[p], start + k) for k in range(8)]
        entry = {(r, c): sublane(column[c], r) for c in range(8) for r in range(c, 8)}
        root, lower = [], {}
        for k in range(0, 8, 2):
            first, side, second = entry[k, k], entry[k + 1, k], entry[k + 1, k + 1]
            one = lax.rsqrt(first)
            two = lax.rsqrt(first * second - side * side) * (first * one)
            root += [one, two]
            lower[k + 1, k] = side * one
            for r in range(k + 2, 8):
                lower[r, k] = entry[r, k] * one
                lower[r, k + 1] = (entry[r, k + 1] - lower[r, k] * lower[k + 1, k]) * two
            for c in range(k + 2, 8):
                for r in range(c, 8):
                    pair = lower[r, k] * lower[c, k] + lower[r, k + 1] * lower[c, k + 1]
                    entry[r, c] = entry[r, c] - pair
        in_panel = (lane_at >= start) & (lane_at < start + 8)
        unit = jnp.where(lane_at - start == row_at, 1.0, 0.0)
        panel = jnp.where(in_panel, unit, blocks[p])
        tops = []
        for k in range(8):
            top = sublane(panel, k)
            for j in range(k):
                top = top - lower[k, j] * tops[j]
            tops.append(top * root[k])
        result = tops[0]
        for k in range(1, 8):
            result = jnp.where(row_at == k, tops[k], result)
        inverse_ref[start : start + 8, :] = jnp.where(lane_at < start + 8, result, 0.0)
        for i in range(p + 1, len(blocks)):
            block = jnp.where(in_panel, 0.0, blocks[i])
            weights = []
            for k in range(8):
                weight = lane(blocks[i], start + k)
                for j in range(k):
                    weight = weight - lower[k, j] * weights[j]
                weights.append(weight * root[k])
                block = block - weights[k] * tops[k]
            blocks[i] = block


def factor_kernel(gram_ref, inverse_ref):
    inverse_factor(unpack(gram_ref[...]), inverse_ref)


def factor_call(gram):
    return pl.pallas_call(
        factor_kernel,
        in_specs=[pl.BlockSpec(memory_space=pltpu.VMEM)],
        out_specs=pl.BlockSpec(memory_space=pltpu.VMEM),
        out_shape=jax.ShapeDtypeStruct((gram.shape[1], gram.shape[1]), jnp.float32),
        compiler_params=pltpu.CompilerParams(vmem_limit_bytes=VMEM_LIMIT),
        cost_estimate=pl.CostEstimate(
            flops=4000000000, bytes_accessed=gram.size * 8, transcendentals=gram.shape[0]
        ),
        name="factor",
    )(gram)


def two_parts(array):
    high = array.astype(jnp.bfloat16)
    return high, (array - high.astype(jnp.float32)).astype(jnp.bfloat16)


def finish_kernel(basis_factor, factor, inverse_ref, first_ref, sums_ref, *refs):
    basis_ref, out_ref = refs[-2:]
    inverse = inverse_ref[...]
    high, low = two_parts(first_ref[...])
    inverse_high, inverse_low = two_parts(inverse.T * basis_factor)
    basis_ref[...] = jnp.dot(
        jnp.concatenate([high, high, low, low], axis=1),
        jnp.concatenate([inverse_high, inverse_low, inverse_high, inverse_low], axis=0),
        preferred_element_type=jnp.float32,
    )
    sums = sums_ref[...]
    for got_ref in refs[:-2]:
        sums = sums + got_ref[...]
    result = jnp.dot(inverse, sums, precision=HIGHEST, preferred_element_type=jnp.float32)
    out_ref[...] = (result.T * factor).astype(out_ref.dtype)


def finish_call(inverse, first, total_rows, factor, sums):
    rows, rank = first.shape
    own = sums[0].shape[1]
    return pl.pallas_call(
        functools.partial(finish_kernel, float(total_rows) ** 0.5, factor),
        in_specs=[pl.BlockSpec(memory_space=pltpu.VMEM)] * (2 + len(sums)),
        out_shape=[
            jax.ShapeDtypeStruct((rows, rank), jnp.float32),
            jax.ShapeDtypeStruct((own, rank), jnp.bfloat16),
        ],
        compiler_params=pltpu.CompilerParams(vmem_limit_bytes=VMEM_LIMIT),
        cost_estimate=pl.CostEstimate(
            flops=12 * rows * rank * rank, bytes_accessed=rows * rank * 8, transcendentals=0
        ),
        name="finish",
    )(inverse, first, *sums)


def local(slab, sketch):
    rows_loc, width = slab.shape
    devices_all = lax.axis_size(AXES)
    own = width // devices_all
    bits = devices_all.bit_length() - 1
    low_bits = bits - ((width // LANES).bit_length() - 1)
    total_rows = rows_loc * devices_all
    me = lax.axis_index(AXES)

    core, x, y, z, zz = [1 << bit for bit in range(low_bits, low_bits + 5)]
    tie = lax.optimization_barrier

    def exchange(array, away, away_odd=None):
        odd = away if away_odd is None else away_odd
        pairs = [(i, i ^ (odd if i & core else away)) for i in range(devices_all)]
        return lax.ppermute(array, AXES, pairs)

    owner = lax.shift_right_logical(me, low_bits).astype(jnp.int32).reshape(1)
    near, first, gram, split, send = rows_call(owner, slab, sketch)
    got = exchange(send, core)
    keep, = project_call(owner, split, near, ((0, 8),), "project_first")
    got, gram = tie((got, gram + exchange(gram, core)))
    far, split = tie((keep + got, split))
    got = exchange(far, x, y)
    send, sums = project_call(owner, split, near, ((1, 0), (0, 0)), "project_rest")
    sums = sums + exchange(send, core)
    over_z = [exchange(gram, away) for away in (z | zz, zz, z)]
    got, over_z[0] = tie((got, over_z[0]))
    sums, gram = tie((sums + got, gram))
    got = exchange(sums[4:], y, x)
    gram = (gram + over_z[2]) + (over_z[1] + over_z[0])
    gram = gram + exchange(gram, x, y)
    got, gram = tie((got, gram))
    sums = sums[:4] + got
    gram = gram + exchange(gram, y, x)
    over_z = [exchange(sums[i], away) for i, away in ((1, z), (2, zz), (3, z | zz))]
    for bit in range(low_bits):
        gram = gram + exchange(gram, 1 << bit)
    sums, gram = tie((sums, gram))
    inverse = factor_call(gram)
    sums = [sums[0], *over_z]
    if low_bits > 0:
        sums = sum(sums)
        for bit in reversed(range(low_bits)):
            half = sums.shape[1] // 2
            mine = lax.rem(lax.shift_right_logical(me, bit), 2) == 1
            left, right = sums[:, :half], sums[:, half:]
            sums = jnp.where(mine, right, left) + exchange(jnp.where(mine, left, right), 1 << bit)
        sums = [sums]
    factor = (float(width) / float(total_rows)) ** 0.5
    return tuple(finish_call(inverse, first, total_rows, factor, sums))


def solution(mesh):
    return jax.shard_map(
        local,
        mesh=mesh,
        in_specs=(P(AXES, None), P()),
        out_specs=(P(AXES, None), P(AXES, None)),
        check_vma=False,
    )
```

```python
import functools

import jax
import jax.numpy as jnp
from jax import lax
from jax.experimental import pallas as pl
from jax.experimental.pallas import tpu as pltpu
from jax.sharding import PartitionSpec as P

AXES = ("rows", "grp")
HIGHEST = lax.Precision.HIGHEST
LANES = 128
VMEM_LIMIT = 24 * 1024 * 1024
AHEAD = 2


def project(out_ref, split_ref, slab_ref, owner, sibling, first_place):
    rank = out_ref.shape[1]
    wanted = lax.bitwise_xor(lax.bitwise_and(owner, 1), sibling)
    mine = lax.shift_right_logical(owner, 1)

    def columns(place):
        one, two = place // 8, place // 4 % 2
        away = jnp.where(wanted == 0, one + 2 * two, two + 2 * one) + 4 * (place % 4)
        at = pl.multiple_of((2 * lax.bitwise_xor(mine, away) + wanted) * LANES, LANES)
        return slab_ref[:, pl.ds(at, LANES)]

    for i in range(0, out_ref.shape[0], 2):
        place = first_place + i
        both = jnp.dot(
            split_ref[...], jnp.concatenate([columns(place), columns(place + 1)], axis=1),
            preferred_element_type=jnp.float32,
        )
        sums = both[:rank] + both[rank:]
        out_ref[i] = sums[:, :LANES]
        out_ref[i + 1] = sums[:, LANES:]


def pack(gram):
    half = gram.shape[0] // 2
    top, bottom = gram[:half], gram[half:]
    row = lax.broadcasted_iota(jnp.int32, top.shape, 0)
    column = lax.broadcasted_iota(jnp.int32, top.shape, 1)
    body = jnp.where(column - half < row, jnp.where(column < half, bottom, pltpu.roll(top, half, 1)), bottom)
    diagonal = jnp.sum(jnp.where(row == column, top, 0.0), axis=0, keepdims=True)
    tail = jnp.where(row[:8] == 0, jnp.broadcast_to(diagonal, (8, diagonal.shape[1])), 0.0)
    return jnp.concatenate([body, tail], axis=0)


def unpack(packed):
    half = packed.shape[0] - 8
    body = packed[:half]
    row = lax.broadcasted_iota(jnp.int32, body.shape, 0)
    column = lax.broadcasted_iota(jnp.int32, body.shape, 1)
    diagonal = jnp.broadcast_to(packed[half : half + 1], body.shape)
    top = jnp.where(column < row, pltpu.roll(body, half, 1), jnp.where(column == row, diagonal, 0.0))
    bottom = jnp.where(column - half < row, jnp.where(column < half, body, 0.0), body)
    parts = jnp.concatenate([top, bottom], axis=0)
    row = lax.broadcasted_iota(jnp.int32, parts.shape, 0)
    column = lax.broadcasted_iota(jnp.int32, parts.shape, 1)
    return parts + jnp.where(row == column, 0.0, parts.T)


def row_chunks(rows):
    sizes, left = [], rows
    while left > 0:
        sizes.append(min(LANES if len(sizes) < 2 else 2 * LANES, left))
        left -= sizes[-1]
    return [(sum(sizes[:k]), size) for k, size in enumerate(sizes)]


def rows_kernel(
    owner_ref, slab_hbm, sketch_hbm, slab_ref, first_ref, gram_ref, split_ref, send_ref,
    sketch_ref, sum_ref, slab_sem, sketch_sem,
):
    rows, width = slab_ref.shape
    rank = sketch_ref.shape[1]
    chunks = [pl.ds(r, size) for r, size in row_chunks(rows)]
    copies = [
        pltpu.make_async_copy(slab_hbm.at[at, :], slab_ref.at[at, :], slab_sem.at[k])
        for k, at in enumerate(chunks)
    ]
    half = slab_ref.shape[1] // 2
    sketch_copies = [
        pltpu.make_async_copy(sketch_hbm.at[at, :], sketch_ref.at[at, :], sketch_sem.at[k])
        for k, at in enumerate((pl.ds(0, half), pl.ds(half, half)))
    ]
    for copy in sketch_copies + copies[:AHEAD]:
        copy.start()
    for copy in sketch_copies:
        copy.wait()
    for k, at in enumerate(chunks):
        copies[k].wait()
        if k + AHEAD < len(chunks):
            copies[k + AHEAD].start()
        first = jnp.dot(slab_ref[at, :], sketch_ref[...], preferred_element_type=jnp.float32)
        first_ref[at, :] = first
        turned = first.T
        high = turned.astype(jnp.bfloat16)
        split_ref[:rank, at] = high
        split_ref[rank:, at] = (turned - high.astype(jnp.float32)).astype(jnp.bfloat16)
        gram = jnp.dot(turned, first, precision=HIGHEST, preferred_element_type=jnp.float32)
        if k == 0:
            sum_ref[...] = gram
        else:
            sum_ref[...] += gram
    gram_ref[...] = pack(sum_ref[...])

    project(send_ref, split_ref, slab_ref, owner_ref[0], 1, 8)


def project_kernel(parts, owner_ref, split_ref, slab_ref, *out_refs):
    for (sibling, first_place), out_ref in zip(parts, out_refs):
        project(out_ref, split_ref, slab_ref, owner_ref[0], sibling, first_place)


def project_call(owner, split, slab, parts, name):
    rows, width = slab.shape
    rank = split.shape[0] // 2
    vmem = pl.BlockSpec(memory_space=pltpu.VMEM)
    chunks = jax.ShapeDtypeStruct((width // (4 * LANES), rank, LANES), jnp.float32)
    return pl.pallas_call(
        functools.partial(project_kernel, parts),
        in_specs=[pl.BlockSpec(memory_space=pltpu.SMEM), vmem, vmem],
        out_specs=[vmem] * len(parts),
        out_shape=[chunks] * len(parts),
        compiler_params=pltpu.CompilerParams(vmem_limit_bytes=VMEM_LIMIT),
        cost_estimate=pl.CostEstimate(
            flops=len(parts) * rows * width * rank, bytes_accessed=rows * width, transcendentals=0
        ),
        name=name,
    )(owner, split, slab)


def rows_call(owner, slab, sketch):
    rows, width = slab.shape
    rank = sketch.shape[1]
    vmem = pl.BlockSpec(memory_space=pltpu.VMEM)
    chunks = (width // (4 * LANES), rank, LANES)
    return pl.pallas_call(
        rows_kernel,
        in_specs=[
            pl.BlockSpec(memory_space=pltpu.SMEM),
            pl.BlockSpec(memory_space=pltpu.HBM),
            pl.BlockSpec(memory_space=pltpu.HBM),
        ],
        out_specs=[vmem] * 5,
        out_shape=[
            jax.ShapeDtypeStruct((rows, width), jnp.bfloat16),
            jax.ShapeDtypeStruct((rows, rank), jnp.float32),
            jax.ShapeDtypeStruct((rank // 2 + 8, rank), jnp.float32),
            jax.ShapeDtypeStruct((2 * rank, rows), jnp.bfloat16),
            jax.ShapeDtypeStruct(chunks, jnp.float32),
        ],
        scratch_shapes=[
            pltpu.VMEM((width, rank), jnp.bfloat16),
            pltpu.VMEM((rank, rank), jnp.float32),
            pltpu.SemaphoreType.DMA((len(row_chunks(rows)),)),
            pltpu.SemaphoreType.DMA((2,)),
        ],
        compiler_params=pltpu.CompilerParams(vmem_limit_bytes=VMEM_LIMIT),
        cost_estimate=pl.CostEstimate(
            flops=3 * rows * width * rank, bytes_accessed=rows * width * 2, transcendentals=0
        ),
        name="sketch_rows",
    )(
        owner,
        pltpu.with_memory_space_constraint(slab, pltpu.HBM),
        pltpu.with_memory_space_constraint(sketch, pltpu.HBM),
    )


def lane(block, at):
    return jnp.broadcast_to(block[:, at : at + 1], block.shape)


def sublane(block, at):
    return jnp.broadcast_to(block[at : at + 1, :], block.shape)


def inverse_factor(gram, inverse_ref):
    size = gram.shape[0]
    blocks = [gram[i : i + 8, :] for i in range(0, size, 8)]
    row_at = lax.broadcasted_iota(jnp.int32, (8, size), 0)
    lane_at = lax.broadcasted_iota(jnp.int32, (8, size), 1)
    for p in range(len(blocks)):
        start = 8 * p
        column = [lane(blocks[p], start + k) for k in range(8)]
        entry = {(r, c): sublane(column[c], r) for c in range(8) for r in range(c, 8)}
        root, lower = [], {}
        for k in range(0, 8, 2):
            first, side, second = entry[k, k], entry[k + 1, k], entry[k + 1, k + 1]
            one = lax.rsqrt(first)
            two = lax.rsqrt(first * second - side * side) * (first * one)
            root += [one, two]
            lower[k + 1, k] = side * one
            for r in range(k + 2, 8):
                lower[r, k] = entry[r, k] * one
                lower[r, k + 1] = (entry[r, k + 1] - lower[r, k] * lower[k + 1, k]) * two
            for c in range(k + 2, 8):
                for r in range(c, 8):
                    pair = lower[r, k] * lower[c, k] + lower[r, k + 1] * lower[c, k + 1]
                    entry[r, c] = entry[r, c] - pair
        in_panel = (lane_at >= start) & (lane_at < start + 8)
        unit = jnp.where(lane_at - start == row_at, 1.0, 0.0)
        panel = jnp.where(in_panel, unit, blocks[p])
        tops = []
        for k in range(8):
            top = sublane(panel, k)
            for j in range(k):
                top = top - lower[k, j] * tops[j]
            tops.append(top * root[k])
        result = tops[0]
        for k in range(1, 8):
            result = jnp.where(row_at == k, tops[k], result)
        inverse_ref[start : start + 8, :] = jnp.where(lane_at < start + 8, result, 0.0)
        for i in range(p + 1, len(blocks)):
            block = jnp.where(in_panel, 0.0, blocks[i])
            weights = []
            for k in range(8):
                weight = lane(blocks[i], start + k)
                for j in range(k):
                    weight = weight - lower[k, j] * weights[j]
                weights.append(weight * root[k])
                block = block - weights[k] * tops[k]
            blocks[i] = block


def factor_kernel(gram_ref, inverse_ref):
    inverse_factor(unpack(gram_ref[...]), inverse_ref)


def factor_call(gram):
    return pl.pallas_call(
        factor_kernel,
        in_specs=[pl.BlockSpec(memory_space=pltpu.VMEM)],
        out_specs=pl.BlockSpec(memory_space=pltpu.VMEM),
        out_shape=jax.ShapeDtypeStruct((gram.shape[1], gram.shape[1]), jnp.float32),
        compiler_params=pltpu.CompilerParams(vmem_limit_bytes=VMEM_LIMIT),
        cost_estimate=pl.CostEstimate(
            flops=4000000000, bytes_accessed=gram.size * 8, transcendentals=gram.shape[0]
        ),
        name="factor",
    )(gram)


def two_parts(array):
    high = array.astype(jnp.bfloat16)
    return high, (array - high.astype(jnp.float32)).astype(jnp.bfloat16)


def finish_kernel(basis_factor, factor, inverse_ref, first_ref, *refs):
    *sums_refs, basis_hbm, out_hbm, basis_ref, out_ref, sems = refs
    inverse = inverse_ref[...]
    inverse_high, inverse_low = two_parts(inverse.T * basis_factor)
    factors = jnp.concatenate([inverse_high, inverse_low, inverse_high, inverse_low], axis=0)
    half = basis_ref.shape[0] // 2
    copies = []
    for k in range(2):
        at = pl.ds(k * half, half)
        high, low = two_parts(first_ref[at, :])
        basis_ref[at, :] = jnp.dot(
            jnp.concatenate([high, high, low, low], axis=1), factors,
            preferred_element_type=jnp.float32,
        )
        copies.append(pltpu.make_async_copy(basis_ref.at[at, :], basis_hbm.at[at, :], sems.at[k]))
        copies[k].start()
    sums = sums_refs[0][...]
    for got_ref in sums_refs[1:]:
        sums = sums + got_ref[...]
    result = jnp.dot(inverse, sums, precision=HIGHEST, preferred_element_type=jnp.float32)
    out_ref[...] = (result.T * factor).astype(out_ref.dtype)
    copies.append(pltpu.make_async_copy(out_ref, out_hbm, sems.at[2]))
    copies[2].start()
    for copy in copies:
        copy.wait()


def finish_call(inverse, first, total_rows, factor, sums):
    rows, rank = first.shape
    own = sums[0].shape[1]
    return pl.pallas_call(
        functools.partial(finish_kernel, float(total_rows) ** 0.5, factor),
        in_specs=[pl.BlockSpec(memory_space=pltpu.VMEM)] * (2 + len(sums)),
        out_specs=[pl.BlockSpec(memory_space=pltpu.HBM)] * 2,
        out_shape=[
            jax.ShapeDtypeStruct((rows, rank), jnp.float32),
            jax.ShapeDtypeStruct((own, rank), jnp.bfloat16),
        ],
        scratch_shapes=[
            pltpu.VMEM((rows, rank), jnp.float32),
            pltpu.VMEM((own, rank), jnp.bfloat16),
            pltpu.SemaphoreType.DMA((3,)),
        ],
        compiler_params=pltpu.CompilerParams(vmem_limit_bytes=VMEM_LIMIT),
        cost_estimate=pl.CostEstimate(
            flops=12 * rows * rank * rank, bytes_accessed=rows * rank * 8, transcendentals=0
        ),
        name="finish",
    )(inverse, first, *sums)


def local(slab, sketch):
    rows_loc, width = slab.shape
    devices_all = lax.axis_size(AXES)
    own = width // devices_all
    bits = devices_all.bit_length() - 1
    low_bits = bits - ((width // LANES).bit_length() - 1)
    total_rows = rows_loc * devices_all
    me = lax.axis_index(AXES)

    core, x, y, z, zz = [1 << bit for bit in range(low_bits, low_bits + 5)]
    tie = lax.optimization_barrier

    def exchange(array, away, away_odd=None):
        odd = away if away_odd is None else away_odd
        pairs = [(i, i ^ (odd if i & core else away)) for i in range(devices_all)]
        return lax.ppermute(array, AXES, pairs)

    owner = lax.shift_right_logical(me, low_bits).astype(jnp.int32).reshape(1)
    near, first, gram, split, send = rows_call(owner, slab, sketch)
    got = exchange(send, core)
    keep, = project_call(owner, split, near, ((0, 8),), "project_first")
    got, gram = tie((got, gram + exchange(gram, core)))
    far, split = tie((keep + got, split))
    got = exchange(far, x, y)
    send, sums = project_call(owner, split, near, ((1, 0), (0, 0)), "project_rest")
    sums = sums + exchange(send, core)
    over_z = [exchange(gram, away) for away in (z | zz, zz, z)]
    got, over_z[0] = tie((got, over_z[0]))
    sums, gram = tie((sums + got, gram))
    got = exchange(sums[4:], y, x)
    gram = (gram + over_z[2]) + (over_z[1] + over_z[0])
    gram = gram + exchange(gram, x, y)
    got, gram = tie((got, gram))
    sums = sums[:4] + got
    gram = gram + exchange(gram, y, x)
    over_z = [exchange(sums[i], away) for i, away in ((1, z), (2, zz), (3, z | zz))]
    for bit in range(low_bits):
        gram = gram + exchange(gram, 1 << bit)
    sums, gram = tie((sums, gram))
    inverse = factor_call(gram)
    sums = [sums[0], *over_z]
    if low_bits > 0:
        sums = sum(sums)
        for bit in reversed(range(low_bits)):
            half = sums.shape[1] // 2
            mine = lax.rem(lax.shift_right_logical(me, bit), 2) == 1
            left, right = sums[:, :half], sums[:, half:]
            sums = jnp.where(mine, right, left) + exchange(jnp.where(mine, left, right), 1 << bit)
        sums = [sums]
    factor = (float(width) / float(total_rows)) ** 0.5
    return tuple(finish_call(inverse, first, total_rows, factor, sums))


def solution(mesh):
    return jax.shard_map(
        local,
        mesh=mesh,
        in_specs=(P(AXES, None), P()),
        out_specs=(P(AXES, None), P(AXES, None)),
        check_vma=False,
    )
```

```python
import functools

import jax
import jax.numpy as jnp
from jax import lax
from jax.experimental import pallas as pl
from jax.experimental.pallas import tpu as pltpu
from jax.sharding import PartitionSpec as P

AXES = ("rows", "grp")
HIGHEST = lax.Precision.HIGHEST
LANES = 128
VMEM_LIMIT = 24 * 1024 * 1024
CUT = 256


def project(out_ref, split_ref, slab_ref, owner, sibling, first_place):
    rank = out_ref.shape[1]
    wanted = lax.bitwise_xor(lax.bitwise_and(owner, 1), sibling)
    mine = lax.shift_right_logical(owner, 1)

    def columns(place):
        one, two = place // 8, place // 4 % 2
        away = jnp.where(wanted == 0, one + 2 * two, two + 2 * one) + 4 * (place % 4)
        at = pl.multiple_of((2 * lax.bitwise_xor(mine, away) + wanted) * LANES, LANES)
        return slab_ref[:, pl.ds(at, LANES)]

    for i in range(0, out_ref.shape[0], 2):
        place = first_place + i
        both = jnp.dot(
            split_ref[...], jnp.concatenate([columns(place), columns(place + 1)], axis=1),
            preferred_element_type=jnp.float32,
        )
        sums = both[:rank] + both[rank:]
        out_ref[i] = sums[:, :LANES]
        out_ref[i + 1] = sums[:, LANES:]


def pack(gram):
    half = gram.shape[0] // 2
    top, bottom = gram[:half], gram[half:]
    row = lax.broadcasted_iota(jnp.int32, top.shape, 0)
    column = lax.broadcasted_iota(jnp.int32, top.shape, 1)
    body = jnp.where(column - half < row, jnp.where(column < half, bottom, pltpu.roll(top, half, 1)), bottom)
    diagonal = jnp.sum(jnp.where(row == column, top, 0.0), axis=0, keepdims=True)
    tail = jnp.where(row[:8] == 0, jnp.broadcast_to(diagonal, (8, diagonal.shape[1])), 0.0)
    return jnp.concatenate([body, tail], axis=0)


def unpack(packed):
    half = packed.shape[0] - 8
    body = packed[:half]
    row = lax.broadcasted_iota(jnp.int32, body.shape, 0)
    column = lax.broadcasted_iota(jnp.int32, body.shape, 1)
    diagonal = jnp.broadcast_to(packed[half : half + 1], body.shape)
    top = jnp.where(column < row, pltpu.roll(body, half, 1), jnp.where(column == row, diagonal, 0.0))
    bottom = jnp.where(column - half < row, jnp.where(column < half, body, 0.0), body)
    parts = jnp.concatenate([top, bottom], axis=0)
    row = lax.broadcasted_iota(jnp.int32, parts.shape, 0)
    column = lax.broadcasted_iota(jnp.int32, parts.shape, 1)
    return parts + jnp.where(row == column, 0.0, parts.T)


def rows_kernel(
    owner_ref, slab_hbm, sketch_hbm, slab_ref, first_ref, gram_ref, split_ref, send_ref,
    sketch_ref, sum_ref, slab_sem, sketch_sem,
):
    rows, width = slab_ref.shape
    rank = sketch_ref.shape[1]
    chunks = [pl.ds(0, CUT), pl.ds(CUT, rows - CUT)]
    copies = [
        pltpu.make_async_copy(slab_hbm.at[at, :], slab_ref.at[at, :], slab_sem.at[k])
        for k, at in enumerate(chunks)
    ]
    sketch_copy = pltpu.make_async_copy(sketch_hbm, sketch_ref, sketch_sem)
    for copy in (sketch_copy, *copies):
        copy.start()
    sketch_copy.wait()
    for k, at in enumerate(chunks):
        copies[k].wait()
        first = jnp.dot(slab_ref[at, :], sketch_ref[...], preferred_element_type=jnp.float32)
        first_ref[at, :] = first
        turned = first.T
        high = turned.astype(jnp.bfloat16)
        split_ref[:rank, at] = high
        split_ref[rank:, at] = (turned - high.astype(jnp.float32)).astype(jnp.bfloat16)
        gram = jnp.dot(turned, first, precision=HIGHEST, preferred_element_type=jnp.float32)
        if k == 0:
            sum_ref[...] = gram
        else:
            sum_ref[...] += gram
    gram_ref[...] = pack(sum_ref[...])

    project(send_ref, split_ref, slab_ref, owner_ref[0], 1, 8)


def project_kernel(parts, owner_ref, split_ref, slab_ref, *out_refs):
    for (sibling, first_place), out_ref in zip(parts, out_refs):
        project(out_ref, split_ref, slab_ref, owner_ref[0], sibling, first_place)


def project_call(owner, split, slab, parts, name):
    rows, width = slab.shape
    rank = split.shape[0] // 2
    vmem = pl.BlockSpec(memory_space=pltpu.VMEM)
    chunks = jax.ShapeDtypeStruct((width // (4 * LANES), rank, LANES), jnp.float32)
    return pl.pallas_call(
        functools.partial(project_kernel, parts),
        in_specs=[pl.BlockSpec(memory_space=pltpu.SMEM), vmem, vmem],
        out_specs=[vmem] * len(parts),
        out_shape=[chunks] * len(parts),
        compiler_params=pltpu.CompilerParams(vmem_limit_bytes=VMEM_LIMIT),
        cost_estimate=pl.CostEstimate(
            flops=len(parts) * rows * width * rank, bytes_accessed=rows * width, transcendentals=0
        ),
        name=name,
    )(owner, split, slab)


def rows_call(owner, slab, sketch):
    rows, width = slab.shape
    rank = sketch.shape[1]
    vmem = pl.BlockSpec(memory_space=pltpu.VMEM)
    chunks = (width // (4 * LANES), rank, LANES)
    return pl.pallas_call(
        rows_kernel,
        in_specs=[
            pl.BlockSpec(memory_space=pltpu.SMEM),
            pl.BlockSpec(memory_space=pltpu.HBM),
            pl.BlockSpec(memory_space=pltpu.HBM),
        ],
        out_specs=[vmem] * 5,
        out_shape=[
            jax.ShapeDtypeStruct((rows, width), jnp.bfloat16),
            jax.ShapeDtypeStruct((rows, rank), jnp.float32),
            jax.ShapeDtypeStruct((rank // 2 + 8, rank), jnp.float32),
            jax.ShapeDtypeStruct((2 * rank, rows), jnp.bfloat16),
            jax.ShapeDtypeStruct(chunks, jnp.float32),
        ],
        scratch_shapes=[
            pltpu.VMEM((width, rank), jnp.bfloat16),
            pltpu.VMEM((rank, rank), jnp.float32),
            pltpu.SemaphoreType.DMA((2,)),
            pltpu.SemaphoreType.DMA,
        ],
        compiler_params=pltpu.CompilerParams(vmem_limit_bytes=VMEM_LIMIT),
        cost_estimate=pl.CostEstimate(
            flops=3 * rows * width * rank, bytes_accessed=rows * width * 2, transcendentals=0
        ),
        name="sketch_rows",
    )(
        owner,
        pltpu.with_memory_space_constraint(slab, pltpu.HBM),
        pltpu.with_memory_space_constraint(sketch, pltpu.HBM),
    )


def lane(block, at):
    return jnp.broadcast_to(block[:, at : at + 1], block.shape)


def sublane(block, at):
    return jnp.broadcast_to(block[at : at + 1, :], block.shape)


def inverse_factor(gram, inverse_ref):
    size = gram.shape[0]
    blocks = [gram[i : i + 8, :] for i in range(0, size, 8)]
    row_at = lax.broadcasted_iota(jnp.int32, (8, size), 0)
    lane_at = lax.broadcasted_iota(jnp.int32, (8, size), 1)
    for p in range(len(blocks)):
        start = 8 * p
        column = [lane(blocks[p], start + k) for k in range(8)]
        entry = {(r, c): sublane(column[c], r) for c in range(8) for r in range(c, 8)}
        root, lower = [], {}
        for k in range(0, 8, 2):
            first, side, second = entry[k, k], entry[k + 1, k], entry[k + 1, k + 1]
            one = lax.rsqrt(first)
            two = lax.rsqrt(first * second - side * side) * (first * one)
            root += [one, two]
            lower[k + 1, k] = side * one
            for r in range(k + 2, 8):
                lower[r, k] = entry[r, k] * one
                lower[r, k + 1] = (entry[r, k + 1] - lower[r, k] * lower[k + 1, k]) * two
            for c in range(k + 2, 8):
                for r in range(c, 8):
                    pair = lower[r, k] * lower[c, k] + lower[r, k + 1] * lower[c, k + 1]
                    entry[r, c] = entry[r, c] - pair
        in_panel = (lane_at >= start) & (lane_at < start + 8)
        unit = jnp.where(lane_at - start == row_at, 1.0, 0.0)
        panel = jnp.where(in_panel, unit, blocks[p])
        tops = []
        for k in range(8):
            top = sublane(panel, k)
            for j in range(k):
                top = top - lower[k, j] * tops[j]
            tops.append(top * root[k])
        result = tops[0]
        for k in range(1, 8):
            result = jnp.where(row_at == k, tops[k], result)
        inverse_ref[start : start + 8, :] = jnp.where(lane_at < start + 8, result, 0.0)
        for i in range(p + 1, len(blocks)):
            block = jnp.where(in_panel, 0.0, blocks[i])
            weights = []
            for k in range(8):
                weight = lane(blocks[i], start + k)
                for j in range(k):
                    weight = weight - lower[k, j] * weights[j]
                weights.append(weight * root[k])
                block = block - weights[k] * tops[k]
            blocks[i] = block


def factor_kernel(gram_ref, inverse_ref):
    inverse_factor(unpack(gram_ref[...]), inverse_ref)


def factor_call(gram):
    return pl.pallas_call(
        factor_kernel,
        in_specs=[pl.BlockSpec(memory_space=pltpu.VMEM)],
        out_specs=pl.BlockSpec(memory_space=pltpu.VMEM),
        out_shape=jax.ShapeDtypeStruct((gram.shape[1], gram.shape[1]), jnp.float32),
        compiler_params=pltpu.CompilerParams(vmem_limit_bytes=VMEM_LIMIT),
        cost_estimate=pl.CostEstimate(
            flops=4000000000, bytes_accessed=gram.size * 8, transcendentals=gram.shape[0]
        ),
        name="factor",
    )(gram)


def two_parts(array):
    high = array.astype(jnp.bfloat16)
    return high, (array - high.astype(jnp.float32)).astype(jnp.bfloat16)


def finish_kernel(basis_factor, factor, inverse_ref, first_ref, sums_ref, *refs):
    basis_ref, out_ref = refs[-2:]
    inverse = inverse_ref[...]
    high, low = two_parts(first_ref[...])
    inverse_high, inverse_low = two_parts(inverse.T * basis_factor)
    basis_ref[...] = jnp.dot(
        jnp.concatenate([high, high, low, low], axis=1),
        jnp.concatenate([inverse_high, inverse_low, inverse_high, inverse_low], axis=0),
        preferred_element_type=jnp.float32,
    )
    sums = sums_ref[...]
    for got_ref in refs[:-2]:
        sums = sums + got_ref[...]
    result = jnp.dot(inverse, sums, precision=HIGHEST, preferred_element_type=jnp.float32)
    out_ref[...] = (result.T * factor).astype(out_ref.dtype)


def finish_call(inverse, first, total_rows, factor, sums):
    rows, rank = first.shape
    own = sums[0].shape[1]
    return pl.pallas_call(
        functools.partial(finish_kernel, float(total_rows) ** 0.5, factor),
        in_specs=[pl.BlockSpec(memory_space=pltpu.VMEM)] * (2 + len(sums)),
        out_shape=[
            jax.ShapeDtypeStruct((rows, rank), jnp.float32),
            jax.ShapeDtypeStruct((own, rank), jnp.bfloat16),
        ],
        compiler_params=pltpu.CompilerParams(vmem_limit_bytes=VMEM_LIMIT),
        cost_estimate=pl.CostEstimate(
            flops=12 * rows * rank * rank, bytes_accessed=rows * rank * 8, transcendentals=0
        ),
        name="finish",
    )(inverse, first, *sums)


def local(slab, sketch):
    rows_loc, width = slab.shape
    devices_all = lax.axis_size(AXES)
    own = width // devices_all
    bits = devices_all.bit_length() - 1
    low_bits = bits - ((width // LANES).bit_length() - 1)
    total_rows = rows_loc * devices_all
    me = lax.axis_index(AXES)

    core, x, y, z, zz = [1 << bit for bit in range(low_bits, low_bits + 5)]
    tie = lax.optimization_barrier

    def exchange(array, away, away_odd=None):
        odd = away if away_odd is None else away_odd
        pairs = [(i, i ^ (odd if i & core else away)) for i in range(devices_all)]
        return lax.ppermute(array, AXES, pairs)

    owner = lax.shift_right_logical(me, low_bits).astype(jnp.int32).reshape(1)
    near, first, gram, split, send = rows_call(owner, slab, sketch)
    got = exchange(send, core)
    keep, = project_call(owner, split, near, ((0, 8),), "project_first")
    got, gram = tie((got, gram + exchange(gram, core)))
    far, split = tie((keep + got, split))
    got = exchange(far, x, y)
    send, sums = project_call(owner, split, near, ((1, 0), (0, 0)), "project_rest")
    sums = sums + exchange(send, core)
    over_z = [exchange(gram, away) for away in (z | zz, zz, z)]
    got, over_z[0] = tie((got, over_z[0]))
    sums, gram = tie((sums + got, gram))
    got = exchange(sums[4:], y, x)
    gram = (gram + over_z[2]) + (over_z[1] + over_z[0])
    gram = gram + exchange(gram, x, y)
    got, gram = tie((got, gram))
    sums = sums[:4] + got
    gram = gram + exchange(gram, y, x)
    over_z = [exchange(sums[i], away) for i, away in ((1, z), (2, zz), (3, z | zz))]
    for bit in range(low_bits):
        gram = gram + exchange(gram, 1 << bit)
    sums, gram = tie((sums, gram))
    inverse = factor_call(gram)
    sums = [sums[0], *over_z]
    if low_bits > 0:
        sums = sum(sums)
        for bit in reversed(range(low_bits)):
            half = sums.shape[1] // 2
            mine = lax.rem(lax.shift_right_logical(me, bit), 2) == 1
            left, right = sums[:, :half], sums[:, half:]
            sums = jnp.where(mine, right, left) + exchange(jnp.where(mine, left, right), 1 << bit)
        sums = [sums]
    factor = (float(width) / float(total_rows)) ** 0.5
    return tuple(finish_call(inverse, first, total_rows, factor, sums))


def solution(mesh):
    return jax.shard_map(
        local,
        mesh=mesh,
        in_specs=(P(AXES, None), P()),
        out_specs=(P(AXES, None), P(AXES, None)),
        check_vma=False,
    )
```

```python
import functools

import jax
import jax.numpy as jnp
from jax import lax
from jax.experimental import pallas as pl
from jax.experimental.pallas import tpu as pltpu
from jax.sharding import PartitionSpec as P

AXES = ("rows", "grp")
HIGHEST = lax.Precision.HIGHEST
LANES = 128
VMEM_LIMIT = 24 * 1024 * 1024
AHEAD = 2
CHUNKS = 4


def project(out_ref, split_ref, slab_ref, owner, sibling, first_place):
    rank = out_ref.shape[1]
    wanted = lax.bitwise_xor(lax.bitwise_and(owner, 1), sibling)
    mine = lax.shift_right_logical(owner, 1)

    def columns(place):
        one, two = place // 8, place // 4 % 2
        away = jnp.where(wanted == 0, one + 2 * two, two + 2 * one) + 4 * (place % 4)
        at = pl.multiple_of((2 * lax.bitwise_xor(mine, away) + wanted) * LANES, LANES)
        return slab_ref[:, pl.ds(at, LANES)]

    for i in range(0, out_ref.shape[0], 2):
        place = first_place + i
        both = jnp.dot(
            split_ref[...], jnp.concatenate([columns(place), columns(place + 1)], axis=1),
            preferred_element_type=jnp.float32,
        )
        sums = both[:rank] + both[rank:]
        out_ref[i] = sums[:, :LANES]
        out_ref[i + 1] = sums[:, LANES:]


def pack(gram):
    half = gram.shape[0] // 2
    top, bottom = gram[:half], gram[half:]
    row = lax.broadcasted_iota(jnp.int32, top.shape, 0)
    column = lax.broadcasted_iota(jnp.int32, top.shape, 1)
    body = jnp.where(column - half < row, jnp.where(column < half, bottom, pltpu.roll(top, half, 1)), bottom)
    diagonal = jnp.sum(jnp.where(row == column, top, 0.0), axis=0, keepdims=True)
    tail = jnp.where(row[:8] == 0, jnp.broadcast_to(diagonal, (8, diagonal.shape[1])), 0.0)
    return jnp.concatenate([body, tail], axis=0)


def unpack(packed):
    half = packed.shape[0] - 8
    body = packed[:half]
    row = lax.broadcasted_iota(jnp.int32, body.shape, 0)
    column = lax.broadcasted_iota(jnp.int32, body.shape, 1)
    diagonal = jnp.broadcast_to(packed[half : half + 1], body.shape)
    top = jnp.where(column < row, pltpu.roll(body, half, 1), jnp.where(column == row, diagonal, 0.0))
    bottom = jnp.where(column - half < row, jnp.where(column < half, body, 0.0), body)
    parts = jnp.concatenate([top, bottom], axis=0)
    row = lax.broadcasted_iota(jnp.int32, parts.shape, 0)
    column = lax.broadcasted_iota(jnp.int32, parts.shape, 1)
    return parts + jnp.where(row == column, 0.0, parts.T)


def rows_kernel(
    owner_ref, slab_hbm, sketch_hbm, slab_ref, first_ref, gram_ref, split_ref, send_ref,
    sketch_ref, slab_sem, sketch_sem,
):
    rows, width = slab_ref.shape
    rank = sketch_ref.shape[1]
    step = width // CHUNKS
    chunks = [pl.ds(k * step, step) for k in range(CHUNKS)]
    copies = [
        (
            pltpu.make_async_copy(sketch_hbm.at[at, :], sketch_ref.at[at, :], sketch_sem.at[k]),
            pltpu.make_async_copy(slab_hbm.at[:, at], slab_ref.at[:, at], slab_sem.at[k]),
        )
        for k, at in enumerate(chunks)
    ]
    for pair in copies[:AHEAD]:
        for copy in pair:
            copy.start()
    for k, at in enumerate(chunks):
        for copy in copies[k]:
            copy.wait()
        if k + AHEAD < CHUNKS:
            for copy in copies[k + AHEAD]:
                copy.start()
        part = jnp.dot(slab_ref[:, at], sketch_ref[at, :], preferred_element_type=jnp.float32)
        if k == 0:
            first_ref[...] = part
        else:
            first_ref[...] += part
    first = first_ref[...]
    turned = first.T
    high = turned.astype(jnp.bfloat16)
    split_ref[:rank] = high
    split_ref[rank:] = (turned - high.astype(jnp.float32)).astype(jnp.bfloat16)
    gram = jnp.dot(turned, first, precision=HIGHEST, preferred_element_type=jnp.float32)
    gram_ref[...] = pack(gram)
    project(send_ref, split_ref, slab_ref, owner_ref[0], 1, 8)


def project_kernel(parts, owner_ref, split_ref, slab_ref, *out_refs):
    for (sibling, first_place), out_ref in zip(parts, out_refs):
        project(out_ref, split_ref, slab_ref, owner_ref[0], sibling, first_place)


def project_call(owner, split, slab, parts, name):
    rows, width = slab.shape
    rank = split.shape[0] // 2
    vmem = pl.BlockSpec(memory_space=pltpu.VMEM)
    chunks = jax.ShapeDtypeStruct((width // (4 * LANES), rank, LANES), jnp.float32)
    return pl.pallas_call(
        functools.partial(project_kernel, parts),
        in_specs=[pl.BlockSpec(memory_space=pltpu.SMEM), vmem, vmem],
        out_specs=[vmem] * len(parts),
        out_shape=[chunks] * len(parts),
        compiler_params=pltpu.CompilerParams(vmem_limit_bytes=VMEM_LIMIT),
        cost_estimate=pl.CostEstimate(
            flops=len(parts) * rows * width * rank, bytes_accessed=rows * width, transcendentals=0
        ),
        name=name,
    )(owner, split, slab)


def rows_call(owner, slab, sketch):
    rows, width = slab.shape
    rank = sketch.shape[1]
    vmem = pl.BlockSpec(memory_space=pltpu.VMEM)
    chunks = (width // (4 * LANES), rank, LANES)
    return pl.pallas_call(
        rows_kernel,
        in_specs=[
            pl.BlockSpec(memory_space=pltpu.SMEM),
            pl.BlockSpec(memory_space=pltpu.HBM),
            pl.BlockSpec(memory_space=pltpu.HBM),
        ],
        out_specs=[vmem] * 5,
        out_shape=[
            jax.ShapeDtypeStruct((rows, width), jnp.bfloat16),
            jax.ShapeDtypeStruct((rows, rank), jnp.float32),
            jax.ShapeDtypeStruct((rank // 2 + 8, rank), jnp.float32),
            jax.ShapeDtypeStruct((2 * rank, rows), jnp.bfloat16),
            jax.ShapeDtypeStruct(chunks, jnp.float32),
        ],
        scratch_shapes=[
            pltpu.VMEM((width, rank), jnp.bfloat16),
            pltpu.SemaphoreType.DMA((CHUNKS,)),
            pltpu.SemaphoreType.DMA((CHUNKS,)),
        ],
        compiler_params=pltpu.CompilerParams(vmem_limit_bytes=VMEM_LIMIT),
        cost_estimate=pl.CostEstimate(
            flops=3 * rows * width * rank, bytes_accessed=rows * width * 2, transcendentals=0
        ),
        name="sketch_rows",
    )(
        owner,
        pltpu.with_memory_space_constraint(slab, pltpu.HBM),
        pltpu.with_memory_space_constraint(sketch, pltpu.HBM),
    )


def lane(block, at):
    return jnp.broadcast_to(block[:, at : at + 1], block.shape)


def sublane(block, at):
    return jnp.broadcast_to(block[at : at + 1, :], block.shape)


def inverse_factor(gram, inverse_ref):
    size = gram.shape[0]
    blocks = [gram[i : i + 8, :] for i in range(0, size, 8)]
    row_at = lax.broadcasted_iota(jnp.int32, (8, size), 0)
    lane_at = lax.broadcasted_iota(jnp.int32, (8, size), 1)
    for p in range(len(blocks)):
        start = 8 * p
        column = [lane(blocks[p], start + k) for k in range(8)]
        entry = {(r, c): sublane(column[c], r) for c in range(8) for r in range(c, 8)}
        root, lower = [], {}
        for k in range(0, 8, 2):
            first, side, second = entry[k, k], entry[k + 1, k], entry[k + 1, k + 1]
            one = lax.rsqrt(first)
            two = lax.rsqrt(first * second - side * side) * (first * one)
            root += [one, two]
            lower[k + 1, k] = side * one
            for r in range(k + 2, 8):
                lower[r, k] = entry[r, k] * one
                lower[r, k + 1] = (entry[r, k + 1] - lower[r, k] * lower[k + 1, k]) * two
            for c in range(k + 2, 8):
                for r in range(c, 8):
                    pair = lower[r, k] * lower[c, k] + lower[r, k + 1] * lower[c, k + 1]
                    entry[r, c] = entry[r, c] - pair
        in_panel = (lane_at >= start) & (lane_at < start + 8)
        unit = jnp.where(lane_at - start == row_at, 1.0, 0.0)
        panel = jnp.where(in_panel, unit, blocks[p])
        tops = []
        for k in range(8):
            top = sublane(panel, k)
            for j in range(k):
                top = top - lower[k, j] * tops[j]
            tops.append(top * root[k])
        result = tops[0]
        for k in range(1, 8):
            result = jnp.where(row_at == k, tops[k], result)
        inverse_ref[start : start + 8, :] = jnp.where(lane_at < start + 8, result, 0.0)
        for i in range(p + 1, len(blocks)):
            block = jnp.where(in_panel, 0.0, blocks[i])
            weights = []
            for k in range(8):
                weight = lane(blocks[i], start + k)
                for j in range(k):
                    weight = weight - lower[k, j] * weights[j]
                weights.append(weight * root[k])
                block = block - weights[k] * tops[k]
            blocks[i] = block


def factor_kernel(gram_ref, inverse_ref):
    inverse_factor(unpack(gram_ref[...]), inverse_ref)


def factor_call(gram):
    return pl.pallas_call(
        factor_kernel,
        in_specs=[pl.BlockSpec(memory_space=pltpu.VMEM)],
        out_specs=pl.BlockSpec(memory_space=pltpu.VMEM),
        out_shape=jax.ShapeDtypeStruct((gram.shape[1], gram.shape[1]), jnp.float32),
        compiler_params=pltpu.CompilerParams(vmem_limit_bytes=VMEM_LIMIT),
        cost_estimate=pl.CostEstimate(
            flops=4000000000, bytes_accessed=gram.size * 8, transcendentals=gram.shape[0]
        ),
        name="factor",
    )(gram)


def two_parts(array):
    high = array.astype(jnp.bfloat16)
    return high, (array - high.astype(jnp.float32)).astype(jnp.bfloat16)


def finish_kernel(basis_factor, factor, inverse_ref, first_ref, sums_ref, *refs):
    basis_ref, out_ref = refs[-2:]
    inverse = inverse_ref[...]
    high, low = two_parts(first_ref[...])
    inverse_high, inverse_low = two_parts(inverse.T * basis_factor)
    basis_ref[...] = jnp.dot(
        jnp.concatenate([high, high, low, low], axis=1),
        jnp.concatenate([inverse_high, inverse_low, inverse_high, inverse_low], axis=0),
        preferred_element_type=jnp.float32,
    )
    sums = sums_ref[...]
    for got_ref in refs[:-2]:
        sums = sums + got_ref[...]
    result = jnp.dot(inverse, sums, precision=HIGHEST, preferred_element_type=jnp.float32)
    out_ref[...] = (result.T * factor).astype(out_ref.dtype)


def finish_call(inverse, first, total_rows, factor, sums):
    rows, rank = first.shape
    own = sums[0].shape[1]
    return pl.pallas_call(
        functools.partial(finish_kernel, float(total_rows) ** 0.5, factor),
        in_specs=[pl.BlockSpec(memory_space=pltpu.VMEM)] * (2 + len(sums)),
        out_shape=[
            jax.ShapeDtypeStruct((rows, rank), jnp.float32),
            jax.ShapeDtypeStruct((own, rank), jnp.bfloat16),
        ],
        compiler_params=pltpu.CompilerParams(vmem_limit_bytes=VMEM_LIMIT),
        cost_estimate=pl.CostEstimate(
            flops=12 * rows * rank * rank, bytes_accessed=rows * rank * 8, transcendentals=0
        ),
        name="finish",
    )(inverse, first, *sums)


def local(slab, sketch):
    rows_loc, width = slab.shape
    devices_all = lax.axis_size(AXES)
    own = width // devices_all
    bits = devices_all.bit_length() - 1
    low_bits = bits - ((width // LANES).bit_length() - 1)
    total_rows = rows_loc * devices_all
    me = lax.axis_index(AXES)

    core, x, y, z, zz = [1 << bit for bit in range(low_bits, low_bits + 5)]
    tie = lax.optimization_barrier

    def exchange(array, away, away_odd=None):
        odd = away if away_odd is None else away_odd
        pairs = [(i, i ^ (odd if i & core else away)) for i in range(devices_all)]
        return lax.ppermute(array, AXES, pairs)

    owner = lax.shift_right_logical(me, low_bits).astype(jnp.int32).reshape(1)
    near, first, gram, split, send = rows_call(owner, slab, sketch)
    got = exchange(send, core)
    keep, = project_call(owner, split, near, ((0, 8),), "project_first")
    got, gram = tie((got, gram + exchange(gram, core)))
    far, split = tie((keep + got, split))
    got = exchange(far, x, y)
    send, sums = project_call(owner, split, near, ((1, 0), (0, 0)), "project_rest")
    sums = sums + exchange(send, core)
    over_z = [exchange(gram, away) for away in (z | zz, zz, z)]
    got, over_z[0] = tie((got, over_z[0]))
    sums, gram = tie((sums + got, gram))
    got = exchange(sums[4:], y, x)
    gram = (gram + over_z[2]) + (over_z[1] + over_z[0])
    gram = gram + exchange(gram, x, y)
    got, gram = tie((got, gram))
    sums = sums[:4] + got
    gram = gram + exchange(gram, y, x)
    over_z = [exchange(sums[i], away) for i, away in ((1, z), (2, zz), (3, z | zz))]
    for bit in range(low_bits):
        gram = gram + exchange(gram, 1 << bit)
    sums, gram = tie((sums, gram))
    inverse = factor_call(gram)
    sums = [sums[0], *over_z]
    if low_bits > 0:
        sums = sum(sums)
        for bit in reversed(range(low_bits)):
            half = sums.shape[1] // 2
            mine = lax.rem(lax.shift_right_logical(me, bit), 2) == 1
            left, right = sums[:, :half], sums[:, half:]
            sums = jnp.where(mine, right, left) + exchange(jnp.where(mine, left, right), 1 << bit)
        sums = [sums]
    factor = (float(width) / float(total_rows)) ** 0.5
    return tuple(finish_call(inverse, first, total_rows, factor, sums))


def solution(mesh):
    return jax.shard_map(
        local,
        mesh=mesh,
        in_specs=(P(AXES, None), P()),
        out_specs=(P(AXES, None), P(AXES, None)),
        check_vma=False,
    )
```

```python
import functools

import jax
import jax.numpy as jnp
from jax import lax
from jax.experimental import pallas as pl
from jax.experimental.pallas import tpu as pltpu
from jax.sharding import PartitionSpec as P

AXES = ("rows", "grp")
HIGHEST = lax.Precision.HIGHEST
LANES = 128
VMEM_LIMIT = 24 * 1024 * 1024
AHEAD = 2
ROWS = 256


def project(out_ref, split_ref, slab_ref, owner, sibling, first_place):
    rank = out_ref.shape[1]
    wanted = lax.bitwise_xor(lax.bitwise_and(owner, 1), sibling)
    mine = lax.shift_right_logical(owner, 1)

    def columns(place):
        one, two = place // 8, place // 4 % 2
        away = jnp.where(wanted == 0, one + 2 * two, two + 2 * one) + 4 * (place % 4)
        at = pl.multiple_of((2 * lax.bitwise_xor(mine, away) + wanted) * LANES, LANES)
        return slab_ref[:, pl.ds(at, LANES)]

    for i in range(0, out_ref.shape[0], 2):
        place = first_place + i
        both = jnp.dot(
            split_ref[...], jnp.concatenate([columns(place), columns(place + 1)], axis=1),
            preferred_element_type=jnp.float32,
        )
        sums = both[:rank] + both[rank:]
        out_ref[i] = sums[:, :LANES]
        out_ref[i + 1] = sums[:, LANES:]


def pack(gram):
    half = gram.shape[0] // 2
    top, bottom = gram[:half], gram[half:]
    row = lax.broadcasted_iota(jnp.int32, top.shape, 0)
    column = lax.broadcasted_iota(jnp.int32, top.shape, 1)
    body = jnp.where(column - half < row, jnp.where(column < half, bottom, pltpu.roll(top, half, 1)), bottom)
    diagonal = jnp.sum(jnp.where(row == column, top, 0.0), axis=0, keepdims=True)
    tail = jnp.where(row[:8] == 0, jnp.broadcast_to(diagonal, (8, diagonal.shape[1])), 0.0)
    return jnp.concatenate([body, tail], axis=0)


def unpack(packed):
    half = packed.shape[0] - 8
    body = packed[:half]
    row = lax.broadcasted_iota(jnp.int32, body.shape, 0)
    column = lax.broadcasted_iota(jnp.int32, body.shape, 1)
    diagonal = jnp.broadcast_to(packed[half : half + 1], body.shape)
    top = jnp.where(column < row, pltpu.roll(body, half, 1), jnp.where(column == row, diagonal, 0.0))
    bottom = jnp.where(column - half < row, jnp.where(column < half, body, 0.0), body)
    parts = jnp.concatenate([top, bottom], axis=0)
    row = lax.broadcasted_iota(jnp.int32, parts.shape, 0)
    column = lax.broadcasted_iota(jnp.int32, parts.shape, 1)
    return parts + jnp.where(row == column, 0.0, parts.T)


def rows_kernel(
    owner_ref, slab_hbm, sketch_hbm, slab_ref, first_ref, gram_ref, split_ref, send_ref,
    sketch_ref, sum_ref, slab_sem, sketch_sem,
):
    rows, width = slab_ref.shape
    rank = sketch_ref.shape[1]
    starts = list(range(0, rows, ROWS))
    copies = [
        pltpu.make_async_copy(
            slab_hbm.at[pl.ds(r, min(ROWS, rows - r)), :],
            slab_ref.at[pl.ds(r, min(ROWS, rows - r)), :],
            slab_sem.at[k],
        )
        for k, r in enumerate(starts)
    ]
    sketch_copy = pltpu.make_async_copy(sketch_hbm, sketch_ref, sketch_sem)
    sketch_copy.start()
    for copy in copies[:AHEAD]:
        copy.start()
    sketch_copy.wait()
    for k, r in enumerate(starts):
        copies[k].wait()
        if k + AHEAD < len(starts):
            copies[k + AHEAD].start()
        at = pl.ds(r, min(ROWS, rows - r))
        first = jnp.dot(slab_ref[at, :], sketch_ref[...], preferred_element_type=jnp.float32)
        first_ref[at, :] = first
        turned = first.T
        high = turned.astype(jnp.bfloat16)
        split_ref[:rank, at] = high
        split_ref[rank:, at] = (turned - high.astype(jnp.float32)).astype(jnp.bfloat16)
        gram = jnp.dot(turned, first, precision=HIGHEST, preferred_element_type=jnp.float32)
        if k == 0:
            sum_ref[...] = gram
        else:
            sum_ref[...] += gram
    gram_ref[...] = pack(sum_ref[...])

    project(send_ref, split_ref, slab_ref, owner_ref[0], 1, 8)


def project_kernel(parts, owner_ref, split_ref, slab_ref, *out_refs):
    for (sibling, first_place), out_ref in zip(parts, out_refs):
        project(out_ref, split_ref, slab_ref, owner_ref[0], sibling, first_place)


def project_call(owner, split, slab, parts, name):
    rows, width = slab.shape
    rank = split.shape[0] // 2
    vmem = pl.BlockSpec(memory_space=pltpu.VMEM)
    chunks = jax.ShapeDtypeStruct((width // (4 * LANES), rank, LANES), jnp.float32)
    return pl.pallas_call(
        functools.partial(project_kernel, parts),
        in_specs=[pl.BlockSpec(memory_space=pltpu.SMEM), vmem, vmem],
        out_specs=[vmem] * len(parts),
        out_shape=[chunks] * len(parts),
        compiler_params=pltpu.CompilerParams(vmem_limit_bytes=VMEM_LIMIT),
        cost_estimate=pl.CostEstimate(
            flops=len(parts) * rows * width * rank, bytes_accessed=rows * width, transcendentals=0
        ),
        name=name,
    )(owner, split, slab)


def rows_call(owner, slab, sketch):
    rows, width = slab.shape
    rank = sketch.shape[1]
    vmem = pl.BlockSpec(memory_space=pltpu.VMEM)
    chunks = (width // (4 * LANES), rank, LANES)
    return pl.pallas_call(
        rows_kernel,
        in_specs=[
            pl.BlockSpec(memory_space=pltpu.SMEM),
            pl.BlockSpec(memory_space=pltpu.HBM),
            pl.BlockSpec(memory_space=pltpu.HBM),
        ],
        out_specs=[vmem] * 5,
        out_shape=[
            jax.ShapeDtypeStruct((rows, width), jnp.bfloat16),
            jax.ShapeDtypeStruct((rows, rank), jnp.float32),
            jax.ShapeDtypeStruct((rank // 2 + 8, rank), jnp.float32),
            jax.ShapeDtypeStruct((2 * rank, rows), jnp.bfloat16),
            jax.ShapeDtypeStruct(chunks, jnp.float32),
        ],
        scratch_shapes=[
            pltpu.VMEM((width, rank), jnp.bfloat16),
            pltpu.VMEM((rank, rank), jnp.float32),
            pltpu.SemaphoreType.DMA((-(-rows // ROWS),)),
            pltpu.SemaphoreType.DMA,
        ],
        compiler_params=pltpu.CompilerParams(vmem_limit_bytes=VMEM_LIMIT),
        cost_estimate=pl.CostEstimate(
            flops=3 * rows * width * rank, bytes_accessed=rows * width * 2, transcendentals=0
        ),
        name="sketch_rows",
    )(
        owner,
        pltpu.with_memory_space_constraint(slab, pltpu.HBM),
        pltpu.with_memory_space_constraint(sketch, pltpu.HBM),
    )


def lane(block, at):
    return jnp.broadcast_to(block[:, at : at + 1], block.shape)


def sublane(block, at):
    return jnp.broadcast_to(block[at : at + 1, :], block.shape)


def inverse_factor(gram, inverse_ref):
    size = gram.shape[0]
    blocks = [gram[i : i + 8, :] for i in range(0, size, 8)]
    row_at = lax.broadcasted_iota(jnp.int32, (8, size), 0)
    lane_at = lax.broadcasted_iota(jnp.int32, (8, size), 1)
    for p in range(len(blocks)):
        start = 8 * p
        column = [lane(blocks[p], start + k) for k in range(8)]
        entry = {(r, c): sublane(column[c], r) for c in range(8) for r in range(c, 8)}
        root, lower = [], {}
        for k in range(0, 8, 2):
            first, side, second = entry[k, k], entry[k + 1, k], entry[k + 1, k + 1]
            one = lax.rsqrt(first)
            two = lax.rsqrt(first * second - side * side) * (first * one)
            root += [one, two]
            lower[k + 1, k] = side * one
            for r in range(k + 2, 8):
                lower[r, k] = entry[r, k] * one
                lower[r, k + 1] = (entry[r, k + 1] - lower[r, k] * lower[k + 1, k]) * two
            for c in range(k + 2, 8):
                for r in range(c, 8):
                    pair = lower[r, k] * lower[c, k] + lower[r, k + 1] * lower[c, k + 1]
                    entry[r, c] = entry[r, c] - pair
        in_panel = (lane_at >= start) & (lane_at < start + 8)
        unit = jnp.where(lane_at - start == row_at, 1.0, 0.0)
        panel = jnp.where(in_panel, unit, blocks[p])
        tops = []
        for k in range(8):
            top = sublane(panel, k)
            for j in range(k):
                top = top - lower[k, j] * tops[j]
            tops.append(top * root[k])
        result = tops[0]
        for k in range(1, 8):
            result = jnp.where(row_at == k, tops[k], result)
        inverse_ref[start : start + 8, :] = jnp.where(lane_at < start + 8, result, 0.0)
        for i in range(p + 1, len(blocks)):
            block = jnp.where(in_panel, 0.0, blocks[i])
            weights = []
            for k in range(8):
                weight = lane(blocks[i], start + k)
                for j in range(k):
                    weight = weight - lower[k, j] * weights[j]
                weights.append(weight * root[k])
                block = block - weights[k] * tops[k]
            blocks[i] = block


def factor_kernel(gram_ref, inverse_ref):
    inverse_factor(unpack(gram_ref[...]), inverse_ref)


def factor_call(gram):
    return pl.pallas_call(
        factor_kernel,
        in_specs=[pl.BlockSpec(memory_space=pltpu.VMEM)],
        out_specs=pl.BlockSpec(memory_space=pltpu.VMEM),
        out_shape=jax.ShapeDtypeStruct((gram.shape[1], gram.shape[1]), jnp.float32),
        compiler_params=pltpu.CompilerParams(vmem_limit_bytes=VMEM_LIMIT),
        cost_estimate=pl.CostEstimate(
            flops=4000000000, bytes_accessed=gram.size * 8, transcendentals=gram.shape[0]
        ),
        name="factor",
    )(gram)


def two_parts(array):
    high = array.astype(jnp.bfloat16)
    return high, (array - high.astype(jnp.float32)).astype(jnp.bfloat16)


def finish_kernel(basis_factor, factor, inverse_ref, first_ref, sums_ref, *refs):
    basis_ref, out_ref = refs[-2:]
    inverse = inverse_ref[...]
    high, low = two_parts(first_ref[...])
    inverse_high, inverse_low = two_parts(inverse.T * basis_factor)
    basis_ref[...] = jnp.dot(
        jnp.concatenate([high, high, low, low], axis=1),
        jnp.concatenate([inverse_high, inverse_low, inverse_high, inverse_low], axis=0),
        preferred_element_type=jnp.float32,
    )
    sums = sums_ref[...]
    for got_ref in refs[:-2]:
        sums = sums + got_ref[...]
    result = jnp.dot(inverse, sums, precision=HIGHEST, preferred_element_type=jnp.float32)
    out_ref[...] = (result.T * factor).astype(out_ref.dtype)


def finish_call(inverse, first, total_rows, factor, sums):
    rows, rank = first.shape
    own = sums[0].shape[1]
    return pl.pallas_call(
        functools.partial(finish_kernel, float(total_rows) ** 0.5, factor),
        in_specs=[pl.BlockSpec(memory_space=pltpu.VMEM)] * (2 + len(sums)),
        out_shape=[
            jax.ShapeDtypeStruct((rows, rank), jnp.float32),
            jax.ShapeDtypeStruct((own, rank), jnp.bfloat16),
        ],
        compiler_params=pltpu.CompilerParams(vmem_limit_bytes=VMEM_LIMIT),
        cost_estimate=pl.CostEstimate(
            flops=12 * rows * rank * rank, bytes_accessed=rows * rank * 8, transcendentals=0
        ),
        name="finish",
    )(inverse, first, *sums)


def local(slab, sketch):
    rows_loc, width = slab.shape
    devices_all = lax.axis_size(AXES)
    own = width // devices_all
    bits = devices_all.bit_length() - 1
    low_bits = bits - ((width // LANES).bit_length() - 1)
    total_rows = rows_loc * devices_all
    me = lax.axis_index(AXES)

    core, x, y, z, zz = [1 << bit for bit in range(low_bits, low_bits + 5)]
    tie = lax.optimization_barrier

    def exchange(array, away, away_odd=None):
        odd = away if away_odd is None else away_odd
        pairs = [(i, i ^ (odd if i & core else away)) for i in range(devices_all)]
        return lax.ppermute(array, AXES, pairs)

    owner = lax.shift_right_logical(me, low_bits).astype(jnp.int32).reshape(1)
    near, first, gram, split, send = rows_call(owner, slab, sketch)
    got = exchange(send, core)
    keep, = project_call(owner, split, near, ((0, 8),), "project_first")
    got, gram = tie((got, gram + exchange(gram, core)))
    far, split = tie((keep + got, split))
    got = exchange(far, x, y)
    send, sums = project_call(owner, split, near, ((1, 0), (0, 0)), "project_rest")
    sums = sums + exchange(send, core)
    over_z = [exchange(gram, away) for away in (z | zz, zz, z)]
    got, over_z[0] = tie((got, over_z[0]))
    sums, gram = tie((sums + got, gram))
    got = exchange(sums[4:], y, x)
    gram = (gram + over_z[2]) + (over_z[1] + over_z[0])
    gram = gram + exchange(gram, x, y)
    got, gram = tie((got, gram))
    sums = sums[:4] + got
    gram = gram + exchange(gram, y, x)
    over_z = [exchange(sums[i], away) for i, away in ((1, z), (2, zz), (3, z | zz))]
    for bit in range(low_bits):
        gram = gram + exchange(gram, 1 << bit)
    sums, gram = tie((sums, gram))
    inverse = factor_call(gram)
    sums = [sums[0], *over_z]
    if low_bits > 0:
        sums = sum(sums)
        for bit in reversed(range(low_bits)):
            half = sums.shape[1] // 2
            mine = lax.rem(lax.shift_right_logical(me, bit), 2) == 1
            left, right = sums[:, :half], sums[:, half:]
            sums = jnp.where(mine, right, left) + exchange(jnp.where(mine, left, right), 1 << bit)
        sums = [sums]
    factor = (float(width) / float(total_rows)) ** 0.5
    return tuple(finish_call(inverse, first, total_rows, factor, sums))


def solution(mesh):
    return jax.shard_map(
        local,
        mesh=mesh,
        in_specs=(P(AXES, None), P()),
        out_specs=(P(AXES, None), P(AXES, None)),
        check_vma=False,
    )
```

```python
import functools

import jax
import jax.numpy as jnp
from jax import lax
from jax.experimental import pallas as pl
from jax.experimental.pallas import tpu as pltpu
from jax.sharding import PartitionSpec as P

AXES = ("rows", "grp")
HIGHEST = lax.Precision.HIGHEST
LANES = 128
VMEM_LIMIT = 24 * 1024 * 1024
AHEAD = 2
ROWS = 256


def project(out_ref, split_ref, slab_ref, owner, sibling, first_place):
    rank = out_ref.shape[1]
    wanted = lax.bitwise_xor(lax.bitwise_and(owner, 1), sibling)
    mine = lax.shift_right_logical(owner, 1)

    def columns(place):
        one, two = place // 8, place // 4 % 2
        away = jnp.where(wanted == 0, one + 2 * two, two + 2 * one) + 4 * (place % 4)
        at = pl.multiple_of((2 * lax.bitwise_xor(mine, away) + wanted) * LANES, LANES)
        return slab_ref[:, pl.ds(at, LANES)]

    for i in range(0, out_ref.shape[0], 2):
        place = first_place + i
        both = jnp.dot(
            split_ref[...], jnp.concatenate([columns(place), columns(place + 1)], axis=1),
            preferred_element_type=jnp.float32,
        )
        sums = both[:rank] + both[rank:]
        out_ref[i] = sums[:, :LANES]
        out_ref[i + 1] = sums[:, LANES:]


def pack(gram):
    half = gram.shape[0] // 2
    top, bottom = gram[:half], gram[half:]
    row = lax.broadcasted_iota(jnp.int32, top.shape, 0)
    column = lax.broadcasted_iota(jnp.int32, top.shape, 1)
    body = jnp.where(column - half < row, jnp.where(column < half, bottom, pltpu.roll(top, half, 1)), bottom)
    diagonal = jnp.sum(jnp.where(row == column, top, 0.0), axis=0, keepdims=True)
    tail = jnp.where(row[:8] == 0, jnp.broadcast_to(diagonal, (8, diagonal.shape[1])), 0.0)
    return jnp.concatenate([body, tail], axis=0)


def unpack(packed):
    half = packed.shape[0] - 8
    body = packed[:half]
    row = lax.broadcasted_iota(jnp.int32, body.shape, 0)
    column = lax.broadcasted_iota(jnp.int32, body.shape, 1)
    diagonal = jnp.broadcast_to(packed[half : half + 1], body.shape)
    top = jnp.where(column < row, pltpu.roll(body, half, 1), jnp.where(column == row, diagonal, 0.0))
    bottom = jnp.where(column - half < row, jnp.where(column < half, body, 0.0), body)
    parts = jnp.concatenate([top, bottom], axis=0)
    row = lax.broadcasted_iota(jnp.int32, parts.shape, 0)
    column = lax.broadcasted_iota(jnp.int32, parts.shape, 1)
    return parts + jnp.where(row == column, 0.0, parts.T)


def rows_kernel(
    owner_ref, slab_hbm, sketch_hbm, slab_ref, first_ref, gram_ref, split_ref, send_ref,
    sketch_ref, sum_ref, slab_sem, sketch_sem,
):
    rows, width = slab_ref.shape
    rank = sketch_ref.shape[1]
    starts = list(range(0, rows, ROWS))
    copies = [
        pltpu.make_async_copy(
            slab_hbm.at[pl.ds(r, min(ROWS, rows - r)), :],
            slab_ref.at[pl.ds(r, min(ROWS, rows - r)), :],
            slab_sem.at[k],
        )
        for k, r in enumerate(starts)
    ]
    sketch_copy = pltpu.make_async_copy(sketch_hbm, sketch_ref, sketch_sem)
    sketch_copy.start()
    for copy in copies[:AHEAD]:
        copy.start()
    sketch_copy.wait()
    for k, r in enumerate(starts):
        copies[k].wait()
        if k + AHEAD < len(starts):
            copies[k + AHEAD].start()
        at = pl.ds(r, min(ROWS, rows - r))
        first = jnp.dot(slab_ref[at, :], sketch_ref[...], preferred_element_type=jnp.float32)
        first_ref[at, :] = first
        turned = first.T
        high = turned.astype(jnp.bfloat16)
        split_ref[:rank, at] = high
        split_ref[rank:, at] = (turned - high.astype(jnp.float32)).astype(jnp.bfloat16)
        gram = jnp.dot(turned, first, precision=HIGHEST, preferred_element_type=jnp.float32)
        if k == 0:
            sum_ref[...] = gram
        else:
            sum_ref[...] += gram
    gram_ref[...] = pack(sum_ref[...])

    project(send_ref, split_ref, slab_ref, owner_ref[0], 1, 8)


def project_kernel(parts, owner_ref, split_ref, slab_ref, *out_refs):
    for (sibling, first_place), out_ref in zip(parts, out_refs):
        project(out_ref, split_ref, slab_ref, owner_ref[0], sibling, first_place)


def project_call(owner, split, slab, parts, name):
    rows, width = slab.shape
    rank = split.shape[0] // 2
    vmem = pl.BlockSpec(memory_space=pltpu.VMEM)
    chunks = jax.ShapeDtypeStruct((width // (4 * LANES), rank, LANES), jnp.float32)
    return pl.pallas_call(
        functools.partial(project_kernel, parts),
        in_specs=[pl.BlockSpec(memory_space=pltpu.SMEM), vmem, vmem],
        out_specs=[vmem] * len(parts),
        out_shape=[chunks] * len(parts),
        compiler_params=pltpu.CompilerParams(vmem_limit_bytes=VMEM_LIMIT),
        cost_estimate=pl.CostEstimate(
            flops=len(parts) * rows * width * rank, bytes_accessed=rows * width, transcendentals=0
        ),
        name=name,
    )(owner, split, slab)


def rows_call(owner, slab, sketch):
    rows, width = slab.shape
    rank = sketch.shape[1]
    vmem = pl.BlockSpec(memory_space=pltpu.VMEM)
    chunks = (width // (4 * LANES), rank, LANES)
    return pl.pallas_call(
        rows_kernel,
        in_specs=[
            pl.BlockSpec(memory_space=pltpu.SMEM),
            pl.BlockSpec(memory_space=pltpu.HBM),
            pl.BlockSpec(memory_space=pltpu.HBM),
        ],
        out_specs=[vmem] * 5,
        out_shape=[
            jax.ShapeDtypeStruct((rows, width), jnp.bfloat16),
            jax.ShapeDtypeStruct((rows, rank), jnp.float32),
            jax.ShapeDtypeStruct((rank // 2 + 8, rank), jnp.float32),
            jax.ShapeDtypeStruct((2 * rank, rows), jnp.bfloat16),
            jax.ShapeDtypeStruct(chunks, jnp.float32),
        ],
        scratch_shapes=[
            pltpu.VMEM((width, rank), jnp.bfloat16),
            pltpu.VMEM((rank, rank), jnp.float32),
            pltpu.SemaphoreType.DMA((-(-rows // ROWS),)),
            pltpu.SemaphoreType.DMA,
        ],
        compiler_params=pltpu.CompilerParams(vmem_limit_bytes=VMEM_LIMIT),
        cost_estimate=pl.CostEstimate(
            flops=3 * rows * width * rank, bytes_accessed=rows * width * 2, transcendentals=0
        ),
        name="sketch_rows",
    )(
        owner,
        pltpu.with_memory_space_constraint(slab, pltpu.HBM),
        pltpu.with_memory_space_constraint(sketch, pltpu.HBM),
    )


def lane(block, at):
    return jnp.broadcast_to(block[:, at : at + 1], block.shape)


def sublane(block, at):
    return jnp.broadcast_to(block[at : at + 1, :], block.shape)


def inverse_factor(gram, inverse_ref):
    size = gram.shape[0]
    blocks = [gram[i : i + 8, :] for i in range(0, size, 8)]
    row_at = lax.broadcasted_iota(jnp.int32, (8, size), 0)
    lane_at = lax.broadcasted_iota(jnp.int32, (8, size), 1)
    for p in range(len(blocks)):
        start = 8 * p
        column = [lane(blocks[p], start + k) for k in range(8)]
        entry = {(r, c): sublane(column[c], r) for c in range(8) for r in range(c, 8)}
        root, lower = [], {}
        for k in range(0, 8, 2):
            first, side, second = entry[k, k], entry[k + 1, k], entry[k + 1, k + 1]
            one = lax.rsqrt(first)
            two = lax.rsqrt(first * second - side * side) * (first * one)
            root += [one, two]
            lower[k + 1, k] = side * one
            for r in range(k + 2, 8):
                lower[r, k] = entry[r, k] * one
                lower[r, k + 1] = (entry[r, k + 1] - lower[r, k] * lower[k + 1, k]) * two
            for c in range(k + 2, 8):
                for r in range(c, 8):
                    pair = lower[r, k] * lower[c, k] + lower[r, k + 1] * lower[c, k + 1]
                    entry[r, c] = entry[r, c] - pair
        in_panel = (lane_at >= start) & (lane_at < start + 8)
        unit = jnp.where(lane_at - start == row_at, 1.0, 0.0)
        panel = jnp.where(in_panel, unit, blocks[p])
        tops = []
        for k in range(8):
            top = sublane(panel, k)
            for j in range(k):
                top = top - lower[k, j] * tops[j]
            tops.append(top * root[k])
        result = tops[0]
        for k in range(1, 8):
            result = jnp.where(row_at == k, tops[k], result)
        inverse_ref[start : start + 8, :] = jnp.where(lane_at < start + 8, result, 0.0)
        for i in range(p + 1, len(blocks)):
            block = jnp.where(in_panel, 0.0, blocks[i])
            weights = []
            for k in range(8):
                weight = lane(blocks[i], start + k)
                for j in range(k):
                    weight = weight - lower[k, j] * weights[j]
                weights.append(weight * root[k])
                block = block - weights[k] * tops[k]
            blocks[i] = block


def factor_kernel(gram_ref, got_ref, inverse_ref):
    inverse_factor(unpack(gram_ref[...] + got_ref[...]), inverse_ref)


def factor_call(gram, got):
    return pl.pallas_call(
        factor_kernel,
        in_specs=[pl.BlockSpec(memory_space=pltpu.VMEM)] * 2,
        out_specs=pl.BlockSpec(memory_space=pltpu.VMEM),
        out_shape=jax.ShapeDtypeStruct((gram.shape[1], gram.shape[1]), jnp.float32),
        compiler_params=pltpu.CompilerParams(vmem_limit_bytes=VMEM_LIMIT),
        cost_estimate=pl.CostEstimate(
            flops=4000000000, bytes_accessed=gram.size * 8, transcendentals=gram.shape[0]
        ),
        name="factor",
    )(gram, got)


def two_parts(array):
    high = array.astype(jnp.bfloat16)
    return high, (array - high.astype(jnp.float32)).astype(jnp.bfloat16)


def finish_kernel(basis_factor, factor, inverse_ref, first_ref, sums_ref, *refs):
    basis_ref, out_ref = refs[-2:]
    inverse = inverse_ref[...]
    high, low = two_parts(first_ref[...])
    inverse_high, inverse_low = two_parts(inverse.T * basis_factor)
    basis_ref[...] = jnp.dot(
        jnp.concatenate([high, high, low, low], axis=1),
        jnp.concatenate([inverse_high, inverse_low, inverse_high, inverse_low], axis=0),
        preferred_element_type=jnp.float32,
    )
    sums = sums_ref[...]
    for got_ref in refs[:-2]:
        sums = sums + got_ref[...]
    result = jnp.dot(inverse, sums, precision=HIGHEST, preferred_element_type=jnp.float32)
    out_ref[...] = (result.T * factor).astype(out_ref.dtype)


def finish_call(inverse, first, total_rows, factor, sums):
    rows, rank = first.shape
    own = sums[0].shape[1]
    return pl.pallas_call(
        functools.partial(finish_kernel, float(total_rows) ** 0.5, factor),
        in_specs=[pl.BlockSpec(memory_space=pltpu.VMEM)] * (2 + len(sums)),
        out_shape=[
            jax.ShapeDtypeStruct((rows, rank), jnp.float32),
            jax.ShapeDtypeStruct((own, rank), jnp.bfloat16),
        ],
        compiler_params=pltpu.CompilerParams(vmem_limit_bytes=VMEM_LIMIT),
        cost_estimate=pl.CostEstimate(
            flops=12 * rows * rank * rank, bytes_accessed=rows * rank * 8, transcendentals=0
        ),
        name="finish",
    )(inverse, first, *sums)


def local(slab, sketch):
    rows_loc, width = slab.shape
    devices_all = lax.axis_size(AXES)
    own = width // devices_all
    bits = devices_all.bit_length() - 1
    low_bits = bits - ((width // LANES).bit_length() - 1)
    total_rows = rows_loc * devices_all
    me = lax.axis_index(AXES)

    core, x, y, z, zz = [1 << bit for bit in range(low_bits, low_bits + 5)]
    tie = lax.optimization_barrier

    def exchange(array, away, away_odd=None):
        odd = away if away_odd is None else away_odd
        pairs = [(i, i ^ (odd if i & core else away)) for i in range(devices_all)]
        return lax.ppermute(array, AXES, pairs)

    owner = lax.shift_right_logical(me, low_bits).astype(jnp.int32).reshape(1)
    near, first, gram, split, send = rows_call(owner, slab, sketch)
    got = exchange(send, core)
    keep, = project_call(owner, split, near, ((0, 8),), "project_first")
    got, gram = tie((got, gram + exchange(gram, core)))
    far, split = tie((keep + got, split))
    got = exchange(far, x, y)
    send, sums = project_call(owner, split, near, ((1, 0), (0, 0)), "project_rest")
    sums = sums + exchange(send, core)
    over_z = [exchange(gram, away) for away in (z | zz, zz, z)]
    got, over_z[0] = tie((got, over_z[0]))
    sums, gram = tie((sums + got, gram))
    got = exchange(sums[4:], y, x)
    gram = (gram + over_z[2]) + (over_z[1] + over_z[0])
    gram = gram + exchange(gram, x, y)
    got, _ = tie((got, gram))
    got_gram = exchange(gram, y, x)
    sums, gram = tie((sums[:4] + got, gram))
    over_z = [exchange(sums[i], away) for i, away in ((1, z), (2, zz), (3, z | zz))]
    for bit in range(low_bits):
        gram = gram + got_gram
        got_gram = exchange(gram, 1 << bit)
    sums, gram = tie((sums, gram))
    inverse = factor_call(gram, got_gram)
    sums = [sums[0], *over_z]
    if low_bits > 0:
        sums = sum(sums)
        for bit in reversed(range(low_bits)):
            half = sums.shape[1] // 2
            mine = lax.rem(lax.shift_right_logical(me, bit), 2) == 1
            left, right = sums[:, :half], sums[:, half:]
            sums = jnp.where(mine, right, left) + exchange(jnp.where(mine, left, right), 1 << bit)
        sums = [sums]
    factor = (float(width) / float(total_rows)) ** 0.5
    return tuple(finish_call(inverse, first, total_rows, factor, sums))


def solution(mesh):
    return jax.shard_map(
        local,
        mesh=mesh,
        in_specs=(P(AXES, None), P()),
        out_specs=(P(AXES, None), P(AXES, None)),
        check_vma=False,
    )
```

```python
import functools

import jax
import jax.numpy as jnp
from jax import lax
from jax.experimental import pallas as pl
from jax.experimental.pallas import tpu as pltpu
from jax.sharding import PartitionSpec as P

AXES = ("rows", "grp")
HIGHEST = lax.Precision.HIGHEST
LANES = 128
VMEM_LIMIT = 24 * 1024 * 1024
AHEAD = 2
ROWS = 256


def project(out_ref, split_ref, slab_ref, owner, sibling, first_place):
    rank = out_ref.shape[1]
    wanted = lax.bitwise_xor(lax.bitwise_and(owner, 1), sibling)
    mine = lax.shift_right_logical(owner, 1)

    def columns(place):
        one, two = place // 8, place // 4 % 2
        away = jnp.where(wanted == 0, one + 2 * two, two + 2 * one) + 4 * (place % 4)
        at = pl.multiple_of((2 * lax.bitwise_xor(mine, away) + wanted) * LANES, LANES)
        return slab_ref[:, pl.ds(at, LANES)]

    for i in range(0, out_ref.shape[0], 2):
        place = first_place + i
        both = jnp.dot(
            split_ref[...], jnp.concatenate([columns(place), columns(place + 1)], axis=1),
            preferred_element_type=jnp.float32,
        )
        sums = both[:rank] + both[rank:]
        out_ref[i] = sums[:, :LANES]
        out_ref[i + 1] = sums[:, LANES:]


def pack(gram):
    half = gram.shape[0] // 2
    top, bottom = gram[:half], gram[half:]
    row = lax.broadcasted_iota(jnp.int32, top.shape, 0)
    column = lax.broadcasted_iota(jnp.int32, top.shape, 1)
    body = jnp.where(column - half < row, jnp.where(column < half, bottom, pltpu.roll(top, half, 1)), bottom)
    diagonal = jnp.sum(jnp.where(row == column, top, 0.0), axis=0, keepdims=True)
    tail = jnp.where(row[:8] == 0, jnp.broadcast_to(diagonal, (8, diagonal.shape[1])), 0.0)
    return jnp.concatenate([body, tail], axis=0)


def unpack(packed):
    half = packed.shape[0] - 8
    body = packed[:half]
    row = lax.broadcasted_iota(jnp.int32, body.shape, 0)
    column = lax.broadcasted_iota(jnp.int32, body.shape, 1)
    diagonal = jnp.broadcast_to(packed[half : half + 1], body.shape)
    top = jnp.where(column < row, pltpu.roll(body, half, 1), jnp.where(column == row, diagonal, 0.0))
    bottom = jnp.where(column - half < row, jnp.where(column < half, body, 0.0), body)
    parts = jnp.concatenate([top, bottom], axis=0)
    row = lax.broadcasted_iota(jnp.int32, parts.shape, 0)
    column = lax.broadcasted_iota(jnp.int32, parts.shape, 1)
    return parts + jnp.where(row == column, 0.0, parts.T)


def rows_kernel(
    owner_ref, slab_hbm, sketch_hbm, slab_ref, first_ref, gram_ref, split_ref, send_ref,
    sketch_ref, sum_ref, slab_sem, sketch_sem,
):
    rows, width = slab_ref.shape
    rank = sketch_ref.shape[1]
    starts = list(range(0, rows, ROWS))
    copies = [
        pltpu.make_async_copy(
            slab_hbm.at[pl.ds(r, min(ROWS, rows - r)), :],
            slab_ref.at[pl.ds(r, min(ROWS, rows - r)), :],
            slab_sem.at[k],
        )
        for k, r in enumerate(starts)
    ]
    sketch_copy = pltpu.make_async_copy(sketch_hbm, sketch_ref, sketch_sem)
    sketch_copy.start()
    for copy in copies[:AHEAD]:
        copy.start()
    sketch_copy.wait()
    for k, r in enumerate(starts):
        copies[k].wait()
        if k + AHEAD < len(starts):
            copies[k + AHEAD].start()
        at = pl.ds(r, min(ROWS, rows - r))
        first = jnp.dot(slab_ref[at, :], sketch_ref[...], preferred_element_type=jnp.float32)
        first_ref[at, :] = first
        turned = first.T
        high = turned.astype(jnp.bfloat16)
        split_ref[:rank, at] = high
        split_ref[rank:, at] = (turned - high.astype(jnp.float32)).astype(jnp.bfloat16)
        gram = jnp.dot(turned, first, precision=HIGHEST, preferred_element_type=jnp.float32)
        if k == 0:
            sum_ref[...] = gram
        else:
            sum_ref[...] += gram
    gram_ref[...] = pack(sum_ref[...])

    project(send_ref, split_ref, slab_ref, owner_ref[0], 1, 8)


def project_kernel(parts, owner_ref, split_ref, slab_ref, *out_refs):
    for (sibling, first_place), out_ref in zip(parts, out_refs):
        project(out_ref, split_ref, slab_ref, owner_ref[0], sibling, first_place)


def project_call(owner, split, slab, parts, name):
    rows, width = slab.shape
    rank = split.shape[0] // 2
    vmem = pl.BlockSpec(memory_space=pltpu.VMEM)
    chunks = jax.ShapeDtypeStruct((width // (4 * LANES), rank, LANES), jnp.float32)
    return pl.pallas_call(
        functools.partial(project_kernel, parts),
        in_specs=[pl.BlockSpec(memory_space=pltpu.SMEM), vmem, vmem],
        out_specs=[vmem] * len(parts),
        out_shape=[chunks] * len(parts),
        compiler_params=pltpu.CompilerParams(vmem_limit_bytes=VMEM_LIMIT),
        cost_estimate=pl.CostEstimate(
            flops=len(parts) * rows * width * rank, bytes_accessed=rows * width, transcendentals=0
        ),
        name=name,
    )(owner, split, slab)


def rows_call(owner, slab, sketch):
    rows, width = slab.shape
    rank = sketch.shape[1]
    vmem = pl.BlockSpec(memory_space=pltpu.VMEM)
    chunks = (width // (4 * LANES), rank, LANES)
    return pl.pallas_call(
        rows_kernel,
        in_specs=[
            pl.BlockSpec(memory_space=pltpu.SMEM),
            pl.BlockSpec(memory_space=pltpu.HBM),
            pl.BlockSpec(memory_space=pltpu.HBM),
        ],
        out_specs=[vmem] * 5,
        out_shape=[
            jax.ShapeDtypeStruct((rows, width), jnp.bfloat16),
            jax.ShapeDtypeStruct((rows, rank), jnp.float32),
            jax.ShapeDtypeStruct((rank // 2 + 8, rank), jnp.float32),
            jax.ShapeDtypeStruct((2 * rank, rows), jnp.bfloat16),
            jax.ShapeDtypeStruct(chunks, jnp.float32),
        ],
        scratch_shapes=[
            pltpu.VMEM((width, rank), jnp.bfloat16),
            pltpu.VMEM((rank, rank), jnp.float32),
            pltpu.SemaphoreType.DMA((-(-rows // ROWS),)),
            pltpu.SemaphoreType.DMA,
        ],
        compiler_params=pltpu.CompilerParams(vmem_limit_bytes=VMEM_LIMIT),
        cost_estimate=pl.CostEstimate(
            flops=3 * rows * width * rank, bytes_accessed=rows * width * 2, transcendentals=0
        ),
        name="sketch_rows",
    )(
        owner,
        pltpu.with_memory_space_constraint(slab, pltpu.HBM),
        pltpu.with_memory_space_constraint(sketch, pltpu.HBM),
    )


def lane(block, at):
    return jnp.broadcast_to(block[:, at : at + 1], block.shape)


def sublane(block, at):
    return jnp.broadcast_to(block[at : at + 1, :], block.shape)


def inverse_factor(gram, inverse_ref):
    size = gram.shape[0]
    blocks = [gram[i : i + 8, :] for i in range(0, size, 8)]
    row_at = lax.broadcasted_iota(jnp.int32, (8, size), 0)
    lane_at = lax.broadcasted_iota(jnp.int32, (8, size), 1)
    for p in range(len(blocks)):
        start = 8 * p
        column = [lane(blocks[p], start + k) for k in range(8)]
        entry = {(r, c): sublane(column[c], r) for c in range(8) for r in range(c, 8)}
        root, lower = [], {}
        for k in range(0, 8, 2):
            first, side, second = entry[k, k], entry[k + 1, k], entry[k + 1, k + 1]
            one = lax.rsqrt(first)
            two = lax.rsqrt(first * second - side * side) * (first * one)
            root += [one, two]
            lower[k + 1, k] = side * one
            for r in range(k + 2, 8):
                lower[r, k] = entry[r, k] * one
                lower[r, k + 1] = (entry[r, k + 1] - lower[r, k] * lower[k + 1, k]) * two
            for c in range(k + 2, 8):
                for r in range(c, 8):
                    pair = lower[r, k] * lower[c, k] + lower[r, k + 1] * lower[c, k + 1]
                    entry[r, c] = entry[r, c] - pair
        in_panel = (lane_at >= start) & (lane_at < start + 8)
        unit = jnp.where(lane_at - start == row_at, 1.0, 0.0)
        panel = jnp.where(in_panel, unit, blocks[p])
        tops = []
        for k in range(8):
            top = sublane(panel, k)
            for j in range(k):
                top = top - lower[k, j] * tops[j]
            tops.append(top * root[k])
        result = tops[0]
        for k in range(1, 8):
            result = jnp.where(row_at == k, tops[k], result)
        inverse_ref[start : start + 8, :] = jnp.where(lane_at < start + 8, result, 0.0)
        for i in range(p + 1, len(blocks)):
            block = jnp.where(in_panel, 0.0, blocks[i])
            weights = []
            for k in range(8):
                weight = lane(blocks[i], start + k)
                for j in range(k):
                    weight = weight - lower[k, j] * weights[j]
                weights.append(weight * root[k])
                block = block - weights[k] * tops[k]
            blocks[i] = block


def factor_kernel(gram_ref, got_ref, inverse_ref):
    inverse_factor(unpack(gram_ref[...] + got_ref[...]), inverse_ref)


def factor_call(gram, got):
    return pl.pallas_call(
        factor_kernel,
        in_specs=[pl.BlockSpec(memory_space=pltpu.VMEM)] * 2,
        out_specs=pl.BlockSpec(memory_space=pltpu.VMEM),
        out_shape=jax.ShapeDtypeStruct((gram.shape[1], gram.shape[1]), jnp.float32),
        compiler_params=pltpu.CompilerParams(vmem_limit_bytes=VMEM_LIMIT),
        cost_estimate=pl.CostEstimate(
            flops=4000000000, bytes_accessed=gram.size * 8, transcendentals=gram.shape[0]
        ),
        name="factor",
    )(gram, got)


def two_parts(array):
    high = array.astype(jnp.bfloat16)
    return high, (array - high.astype(jnp.float32)).astype(jnp.bfloat16)


def finish_kernel(basis_factor, factor, inverse_ref, first_ref, sums_ref, *refs):
    basis_ref, out_ref = refs[-2:]
    inverse = inverse_ref[...]
    high, low = two_parts(first_ref[...])
    inverse_high, inverse_low = two_parts(inverse.T * basis_factor)
    basis_ref[...] = jnp.dot(
        jnp.concatenate([high, high, low, low], axis=1),
        jnp.concatenate([inverse_high, inverse_low, inverse_high, inverse_low], axis=0),
        preferred_element_type=jnp.float32,
    )
    sums = sums_ref[...]
    for got_ref in refs[:-2]:
        sums = sums + got_ref[...]
    result = jnp.dot(inverse, sums, precision=HIGHEST, preferred_element_type=jnp.float32)
    out_ref[...] = (result.T * factor).astype(out_ref.dtype)


def finish_call(inverse, first, total_rows, factor, sums):
    rows, rank = first.shape
    own = sums[0].shape[1]
    return pl.pallas_call(
        functools.partial(finish_kernel, float(total_rows) ** 0.5, factor),
        in_specs=[pl.BlockSpec(memory_space=pltpu.VMEM)] * (2 + len(sums)),
        out_shape=[
            jax.ShapeDtypeStruct((rows, rank), jnp.float32),
            jax.ShapeDtypeStruct((own, rank), jnp.bfloat16),
        ],
        compiler_params=pltpu.CompilerParams(vmem_limit_bytes=VMEM_LIMIT),
        cost_estimate=pl.CostEstimate(
            flops=12 * rows * rank * rank, bytes_accessed=rows * rank * 8, transcendentals=0
        ),
        name="finish",
    )(inverse, first, *sums)


def local(slab, sketch):
    rows_loc, width = slab.shape
    devices_all = lax.axis_size(AXES)
    own = width // devices_all
    bits = devices_all.bit_length() - 1
    low_bits = bits - ((width // LANES).bit_length() - 1)
    total_rows = rows_loc * devices_all
    me = lax.axis_index(AXES)

    core, x, y, z, zz = [1 << bit for bit in range(low_bits, low_bits + 5)]
    tie = lax.optimization_barrier

    def exchange(array, away, away_odd=None):
        odd = away if away_odd is None else away_odd
        pairs = [(i, i ^ (odd if i & core else away)) for i in range(devices_all)]
        return lax.ppermute(array, AXES, pairs)

    owner = lax.shift_right_logical(me, low_bits).astype(jnp.int32).reshape(1)
    near, first, gram, split, send = rows_call(owner, slab, sketch)
    got = exchange(send, core)
    keep, = project_call(owner, split, near, ((0, 8),), "project_first")
    got, gram = tie((got, gram + exchange(gram, core)))
    far, split = tie((keep + got, split))
    got = exchange(far, x, y)
    send, sums = project_call(owner, split, near, ((1, 0), (0, 0)), "project_rest")
    sums = sums + exchange(send, core)
    over_z = [exchange(gram, away) for away in (z | zz, zz, z)]
    got, over_z[0] = tie((got, over_z[0]))
    sums, gram = tie((sums + got, gram))
    got = exchange(sums[4:], y, x)
    gram = (gram + over_z[2]) + (over_z[1] + over_z[0])
    gram = gram + exchange(gram, x, y)
    got, _ = tie((got, gram))
    got_gram = exchange(gram, y, x)
    sums, gram = tie((sums[:4] + got, gram))
    over_z = [exchange(sums[i], away) for i, away in ((2, zz), (1, z), (3, z | zz))]
    for bit in range(low_bits):
        gram = gram + got_gram
        got_gram = exchange(gram, 1 << bit)
    sums, gram = tie((sums, gram))
    inverse = factor_call(gram, got_gram)
    sums = [sums[0], *over_z]
    if low_bits > 0:
        sums = sum(sums)
        for bit in reversed(range(low_bits)):
            half = sums.shape[1] // 2
            mine = lax.rem(lax.shift_right_logical(me, bit), 2) == 1
            left, right = sums[:, :half], sums[:, half:]
            sums = jnp.where(mine, right, left) + exchange(jnp.where(mine, left, right), 1 << bit)
        sums = [sums]
    factor = (float(width) / float(total_rows)) ** 0.5
    return tuple(finish_call(inverse, first, total_rows, factor, sums))


def solution(mesh):
    return jax.shard_map(
        local,
        mesh=mesh,
        in_specs=(P(AXES, None), P()),
        out_specs=(P(AXES, None), P(AXES, None)),
        check_vma=False,
    )
```

```python
import functools

import jax
import jax.numpy as jnp
from jax import lax
from jax.experimental import pallas as pl
from jax.experimental.pallas import tpu as pltpu
from jax.sharding import PartitionSpec as P

AXES = ("rows", "grp")
HIGHEST = lax.Precision.HIGHEST
LANES = 128
VMEM_LIMIT = 24 * 1024 * 1024
AHEAD = 2
ROWS = 256


def project(out_ref, split_ref, slab_ref, owner, sibling, first_place):
    rank = out_ref.shape[1]
    wanted = lax.bitwise_xor(lax.bitwise_and(owner, 1), sibling)
    mine = lax.shift_right_logical(owner, 1)

    def columns(place):
        one, two = place // 8, place // 4 % 2
        away = jnp.where(wanted == 0, one + 2 * two, two + 2 * one) + 4 * (place % 4)
        at = pl.multiple_of((2 * lax.bitwise_xor(mine, away) + wanted) * LANES, LANES)
        return slab_ref[:, pl.ds(at, LANES)]

    for i in range(0, out_ref.shape[0], 2):
        place = first_place + i
        both = jnp.dot(
            split_ref[...], jnp.concatenate([columns(place), columns(place + 1)], axis=1),
            preferred_element_type=jnp.float32,
        )
        sums = both[:rank] + both[rank:]
        out_ref[i] = sums[:, :LANES]
        out_ref[i + 1] = sums[:, LANES:]


def pack(gram):
    half = gram.shape[0] // 2
    top, bottom = gram[:half], gram[half:]
    row = lax.broadcasted_iota(jnp.int32, top.shape, 0)
    column = lax.broadcasted_iota(jnp.int32, top.shape, 1)
    body = jnp.where(column - half < row, jnp.where(column < half, bottom, pltpu.roll(top, half, 1)), bottom)
    diagonal = jnp.sum(jnp.where(row == column, top, 0.0), axis=0, keepdims=True)
    tail = jnp.where(row[:8] == 0, jnp.broadcast_to(diagonal, (8, diagonal.shape[1])), 0.0)
    return jnp.concatenate([body, tail], axis=0)


def unpack(packed):
    half = packed.shape[0] - 8
    body = packed[:half]
    row = lax.broadcasted_iota(jnp.int32, body.shape, 0)
    column = lax.broadcasted_iota(jnp.int32, body.shape, 1)
    diagonal = jnp.broadcast_to(packed[half : half + 1], body.shape)
    top = jnp.where(column < row, pltpu.roll(body, half, 1), jnp.where(column == row, diagonal, 0.0))
    bottom = jnp.where(column - half < row, jnp.where(column < half, body, 0.0), body)
    parts = jnp.concatenate([top, bottom], axis=0)
    row = lax.broadcasted_iota(jnp.int32, parts.shape, 0)
    column = lax.broadcasted_iota(jnp.int32, parts.shape, 1)
    return parts + jnp.where(row == column, 0.0, parts.T)


def rows_kernel(
    owner_ref, slab_hbm, sketch_hbm, slab_ref, first_ref, gram_ref, split_ref, send_ref,
    sketch_ref, sum_ref, slab_sem, sketch_sem,
):
    rows, width = slab_ref.shape
    rank = sketch_ref.shape[1]
    starts = list(range(0, rows, ROWS))
    copies = [
        pltpu.make_async_copy(
            slab_hbm.at[pl.ds(r, min(ROWS, rows - r)), :],
            slab_ref.at[pl.ds(r, min(ROWS, rows - r)), :],
            slab_sem.at[k],
        )
        for k, r in enumerate(starts)
    ]
    sketch_copy = pltpu.make_async_copy(sketch_hbm, sketch_ref, sketch_sem)
    sketch_copy.start()
    for copy in copies[:AHEAD]:
        copy.start()
    sketch_copy.wait()
    for k, r in enumerate(starts):
        copies[k].wait()
        if k + AHEAD < len(starts):
            copies[k + AHEAD].start()
        at = pl.ds(r, min(ROWS, rows - r))
        first = jnp.dot(slab_ref[at, :], sketch_ref[...], preferred_element_type=jnp.float32)
        first_ref[at, :] = first
        turned = first.T
        high = turned.astype(jnp.bfloat16)
        split_ref[:rank, at] = high
        split_ref[rank:, at] = (turned - high.astype(jnp.float32)).astype(jnp.bfloat16)
        gram = jnp.dot(turned, first, precision=HIGHEST, preferred_element_type=jnp.float32)
        if k == 0:
            sum_ref[...] = gram
        else:
            sum_ref[...] += gram
    gram_ref[...] = pack(sum_ref[...])

    project(send_ref, split_ref, slab_ref, owner_ref[0], 1, 8)


def project_kernel(parts, owner_ref, split_ref, slab_ref, *out_refs):
    for (sibling, first_place), out_ref in zip(parts, out_refs):
        project(out_ref, split_ref, slab_ref, owner_ref[0], sibling, first_place)


def project_call(owner, split, slab, parts, name):
    rows, width = slab.shape
    rank = split.shape[0] // 2
    vmem = pl.BlockSpec(memory_space=pltpu.VMEM)
    chunks = jax.ShapeDtypeStruct((width // (4 * LANES), rank, LANES), jnp.float32)
    return pl.pallas_call(
        functools.partial(project_kernel, parts),
        in_specs=[pl.BlockSpec(memory_space=pltpu.SMEM), vmem, vmem],
        out_specs=[vmem] * len(parts),
        out_shape=[chunks] * len(parts),
        compiler_params=pltpu.CompilerParams(vmem_limit_bytes=VMEM_LIMIT),
        cost_estimate=pl.CostEstimate(
            flops=len(parts) * rows * width * rank, bytes_accessed=rows * width, transcendentals=0
        ),
        name=name,
    )(owner, split, slab)


def rows_call(owner, slab, sketch):
    rows, width = slab.shape
    rank = sketch.shape[1]
    vmem = pl.BlockSpec(memory_space=pltpu.VMEM)
    chunks = (width // (4 * LANES), rank, LANES)
    return pl.pallas_call(
        rows_kernel,
        in_specs=[
            pl.BlockSpec(memory_space=pltpu.SMEM),
            pl.BlockSpec(memory_space=pltpu.HBM),
            pl.BlockSpec(memory_space=pltpu.HBM),
        ],
        out_specs=[vmem] * 5,
        out_shape=[
            jax.ShapeDtypeStruct((rows, width), jnp.bfloat16),
            jax.ShapeDtypeStruct((rows, rank), jnp.float32),
            jax.ShapeDtypeStruct((rank // 2 + 8, rank), jnp.float32),
            jax.ShapeDtypeStruct((2 * rank, rows), jnp.bfloat16),
            jax.ShapeDtypeStruct(chunks, jnp.float32),
        ],
        scratch_shapes=[
            pltpu.VMEM((width, rank), jnp.bfloat16),
            pltpu.VMEM((rank, rank), jnp.float32),
            pltpu.SemaphoreType.DMA((-(-rows // ROWS),)),
            pltpu.SemaphoreType.DMA,
        ],
        compiler_params=pltpu.CompilerParams(vmem_limit_bytes=VMEM_LIMIT),
        cost_estimate=pl.CostEstimate(
            flops=3 * rows * width * rank, bytes_accessed=rows * width * 2, transcendentals=0
        ),
        name="sketch_rows",
    )(
        owner,
        pltpu.with_memory_space_constraint(slab, pltpu.HBM),
        pltpu.with_memory_space_constraint(sketch, pltpu.HBM),
    )


def lane(block, at):
    return jnp.broadcast_to(block[:, at : at + 1], block.shape)


def sublane(block, at):
    return jnp.broadcast_to(block[at : at + 1, :], block.shape)


def inverse_factor(gram, inverse_ref):
    size = gram.shape[0]
    blocks = [gram[i : i + 8, :] for i in range(0, size, 8)]
    row_at = lax.broadcasted_iota(jnp.int32, (8, size), 0)
    lane_at = lax.broadcasted_iota(jnp.int32, (8, size), 1)
    for p in range(len(blocks)):
        start = 8 * p
        column = [lane(blocks[p], start + k) for k in range(8)]
        entry = {(r, c): sublane(column[c], r) for c in range(8) for r in range(c, 8)}
        root, lower = [], {}
        for k in range(0, 8, 2):
            first, side, second = entry[k, k], entry[k + 1, k], entry[k + 1, k + 1]
            one = lax.rsqrt(first)
            two = lax.rsqrt(first * second - side * side) * (first * one)
            root += [one, two]
            lower[k + 1, k] = side * one
            for r in range(k + 2, 8):
                lower[r, k] = entry[r, k] * one
                lower[r, k + 1] = (entry[r, k + 1] - lower[r, k] * lower[k + 1, k]) * two
            for c in range(k + 2, 8):
                for r in range(c, 8):
                    pair = lower[r, k] * lower[c, k] + lower[r, k + 1] * lower[c, k + 1]
                    entry[r, c] = entry[r, c] - pair
        in_panel = (lane_at >= start) & (lane_at < start + 8)
        unit = jnp.where(lane_at - start == row_at, 1.0, 0.0)
        panel = jnp.where(in_panel, unit, blocks[p])
        tops = []
        for k in range(8):
            top = sublane(panel, k)
            for j in range(k):
                top = top - lower[k, j] * tops[j]
            tops.append(top * root[k])
        result = tops[0]
        for k in range(1, 8):
            result = jnp.where(row_at == k, tops[k], result)
        inverse_ref[start : start + 8, :] = jnp.where(lane_at < start + 8, result, 0.0)
        for i in range(p + 1, len(blocks)):
            block = jnp.where(in_panel, 0.0, blocks[i])
            weights = []
            for k in range(8):
                weight = lane(blocks[i], start + k)
                for j in range(k):
                    weight = weight - lower[k, j] * weights[j]
                weights.append(weight * root[k])
                block = block - weights[k] * tops[k]
            blocks[i] = block


def factor_kernel(gram_ref, got_ref, inverse_ref):
    inverse_factor(unpack(gram_ref[...] + got_ref[...]), inverse_ref)


def factor_call(gram, got):
    return pl.pallas_call(
        factor_kernel,
        in_specs=[pl.BlockSpec(memory_space=pltpu.VMEM)] * 2,
        out_specs=pl.BlockSpec(memory_space=pltpu.VMEM),
        out_shape=jax.ShapeDtypeStruct((gram.shape[1], gram.shape[1]), jnp.float32),
        compiler_params=pltpu.CompilerParams(vmem_limit_bytes=VMEM_LIMIT),
        cost_estimate=pl.CostEstimate(
            flops=4000000000, bytes_accessed=gram.size * 8, transcendentals=gram.shape[0]
        ),
        name="factor",
    )(gram, got)


def two_parts(array):
    high = array.astype(jnp.bfloat16)
    return high, (array - high.astype(jnp.float32)).astype(jnp.bfloat16)


def finish_kernel(basis_factor, factor, inverse_ref, first_ref, sums_ref, *refs):
    basis_ref, out_ref = refs[-2:]
    sums = sums_ref[...]
    for got_ref in refs[:-2]:
        sums = sums + got_ref[...]
    inverse_high, inverse_low = two_parts(inverse_ref[...].T * basis_factor)
    factors = jnp.concatenate([inverse_high, inverse_low, inverse_high, inverse_low], axis=0)

    def product(rows):
        high, low = two_parts(rows)
        return jnp.dot(
            jnp.concatenate([high, high, low, low], axis=1), factors,
            preferred_element_type=jnp.float32,
        )

    out_ref[...] = (product(sums.T) * (factor / basis_factor)).astype(out_ref.dtype)
    basis_ref[...] = product(first_ref[...])


def finish_call(inverse, first, total_rows, factor, sums):
    rows, rank = first.shape
    own = sums[0].shape[1]
    return pl.pallas_call(
        functools.partial(finish_kernel, float(total_rows) ** 0.5, factor),
        in_specs=[pl.BlockSpec(memory_space=pltpu.VMEM)] * (2 + len(sums)),
        out_shape=[
            jax.ShapeDtypeStruct((rows, rank), jnp.float32),
            jax.ShapeDtypeStruct((own, rank), jnp.bfloat16),
        ],
        compiler_params=pltpu.CompilerParams(vmem_limit_bytes=VMEM_LIMIT),
        cost_estimate=pl.CostEstimate(
            flops=12 * rows * rank * rank, bytes_accessed=rows * rank * 8, transcendentals=0
        ),
        name="finish",
    )(inverse, first, *sums)


def local(slab, sketch):
    rows_loc, width = slab.shape
    devices_all = lax.axis_size(AXES)
    own = width // devices_all
    bits = devices_all.bit_length() - 1
    low_bits = bits - ((width // LANES).bit_length() - 1)
    total_rows = rows_loc * devices_all
    me = lax.axis_index(AXES)

    core, x, y, z, zz = [1 << bit for bit in range(low_bits, low_bits + 5)]
    tie = lax.optimization_barrier

    def exchange(array, away, away_odd=None):
        odd = away if away_odd is None else away_odd
        pairs = [(i, i ^ (odd if i & core else away)) for i in range(devices_all)]
        return lax.ppermute(array, AXES, pairs)

    owner = lax.shift_right_logical(me, low_bits).astype(jnp.int32).reshape(1)
    near, first, gram, split, send = rows_call(owner, slab, sketch)
    got = exchange(send, core)
    keep, = project_call(owner, split, near, ((0, 8),), "project_first")
    got, gram = tie((got, gram + exchange(gram, core)))
    far, split = tie((keep + got, split))
    got = exchange(far, x, y)
    send, sums = project_call(owner, split, near, ((1, 0), (0, 0)), "project_rest")
    sums = sums + exchange(send, core)
    over_z = [exchange(gram, away) for away in (z | zz, zz, z)]
    got, over_z[0] = tie((got, over_z[0]))
    sums, gram = tie((sums + got, gram))
    got = exchange(sums[4:], y, x)
    gram = (gram + over_z[2]) + (over_z[1] + over_z[0])
    gram = gram + exchange(gram, x, y)
    got, _ = tie((got, gram))
    got_gram = exchange(gram, y, x)
    sums, gram = tie((sums[:4] + got, gram))
    over_z = [exchange(sums[i], away) for i, away in ((1, z), (2, zz), (3, z | zz))]
    for bit in range(low_bits):
        gram = gram + got_gram
        got_gram = exchange(gram, 1 << bit)
    sums, gram = tie((sums, gram))
    inverse = factor_call(gram, got_gram)
    sums = [sums[0], *over_z]
    if low_bits > 0:
        sums = sum(sums)
        for bit in reversed(range(low_bits)):
            half = sums.shape[1] // 2
            mine = lax.rem(lax.shift_right_logical(me, bit), 2) == 1
            left, right = sums[:, :half], sums[:, half:]
            sums = jnp.where(mine, right, left) + exchange(jnp.where(mine, left, right), 1 << bit)
        sums = [sums]
    factor = (float(width) / float(total_rows)) ** 0.5
    return tuple(finish_call(inverse, first, total_rows, factor, sums))


def solution(mesh):
    return jax.shard_map(
        local,
        mesh=mesh,
        in_specs=(P(AXES, None), P()),
        out_specs=(P(AXES, None), P(AXES, None)),
        check_vma=False,
    )
```

```python
import functools

import jax
import jax.numpy as jnp
from jax import lax
from jax.experimental import pallas as pl
from jax.experimental.pallas import tpu as pltpu
from jax.sharding import PartitionSpec as P

AXES = ("rows", "grp")
HIGHEST = lax.Precision.HIGHEST
LANES = 128
VMEM_LIMIT = 24 * 1024 * 1024
AHEAD = 3
ROWS = 256


def project(out_ref, split_ref, slab_ref, owner, sibling, first_place):
    rank = out_ref.shape[1]
    wanted = lax.bitwise_xor(lax.bitwise_and(owner, 1), sibling)
    mine = lax.shift_right_logical(owner, 1)

    def columns(place):
        one, two = place // 8, place // 4 % 2
        away = jnp.where(wanted == 0, one + 2 * two, two + 2 * one) + 4 * (place % 4)
        at = pl.multiple_of((2 * lax.bitwise_xor(mine, away) + wanted) * LANES, LANES)
        return slab_ref[:, pl.ds(at, LANES)]

    for i in range(0, out_ref.shape[0], 2):
        place = first_place + i
        both = jnp.dot(
            split_ref[...], jnp.concatenate([columns(place), columns(place + 1)], axis=1),
            preferred_element_type=jnp.float32,
        )
        sums = both[:rank] + both[rank:]
        out_ref[i] = sums[:, :LANES]
        out_ref[i + 1] = sums[:, LANES:]


def pack(gram):
    half = gram.shape[0] // 2
    top, bottom = gram[:half], gram[half:]
    row = lax.broadcasted_iota(jnp.int32, top.shape, 0)
    column = lax.broadcasted_iota(jnp.int32, top.shape, 1)
    body = jnp.where(column - half < row, jnp.where(column < half, bottom, pltpu.roll(top, half, 1)), bottom)
    diagonal = jnp.sum(jnp.where(row == column, top, 0.0), axis=0, keepdims=True)
    tail = jnp.where(row[:8] == 0, jnp.broadcast_to(diagonal, (8, diagonal.shape[1])), 0.0)
    return jnp.concatenate([body, tail], axis=0)


def unpack(packed):
    half = packed.shape[0] - 8
    body = packed[:half]
    row = lax.broadcasted_iota(jnp.int32, body.shape, 0)
    column = lax.broadcasted_iota(jnp.int32, body.shape, 1)
    diagonal = jnp.broadcast_to(packed[half : half + 1], body.shape)
    top = jnp.where(column < row, pltpu.roll(body, half, 1), jnp.where(column == row, diagonal, 0.0))
    bottom = jnp.where(column - half < row, jnp.where(column < half, body, 0.0), body)
    parts = jnp.concatenate([top, bottom], axis=0)
    row = lax.broadcasted_iota(jnp.int32, parts.shape, 0)
    column = lax.broadcasted_iota(jnp.int32, parts.shape, 1)
    return parts + jnp.where(row == column, 0.0, parts.T)


def rows_kernel(
    owner_ref, slab_hbm, sketch_hbm, slab_ref, first_ref, gram_ref, split_ref, send_ref,
    sketch_ref, sum_ref, slab_sem, sketch_sem,
):
    rows, width = slab_ref.shape
    rank = sketch_ref.shape[1]
    starts = list(range(0, rows, ROWS))
    copies = [
        pltpu.make_async_copy(
            slab_hbm.at[pl.ds(r, min(ROWS, rows - r)), :],
            slab_ref.at[pl.ds(r, min(ROWS, rows - r)), :],
            slab_sem.at[k],
        )
        for k, r in enumerate(starts)
    ]
    sketch_copy = pltpu.make_async_copy(sketch_hbm, sketch_ref, sketch_sem)
    sketch_copy.start()
    for copy in copies[:AHEAD]:
        copy.start()
    sketch_copy.wait()
    for k, r in enumerate(starts):
        copies[k].wait()
        if k + AHEAD < len(starts):
            copies[k + AHEAD].start()
        at = pl.ds(r, min(ROWS, rows - r))
        first = jnp.dot(slab_ref[at, :], sketch_ref[...], preferred_element_type=jnp.float32)
        first_ref[at, :] = first
        turned = first.T
        high = turned.astype(jnp.bfloat16)
        split_ref[:rank, at] = high
        split_ref[rank:, at] = (turned - high.astype(jnp.float32)).astype(jnp.bfloat16)
        gram = jnp.dot(turned, first, precision=HIGHEST, preferred_element_type=jnp.float32)
        if k == 0:
            sum_ref[...] = gram
        else:
            sum_ref[...] += gram
    gram_ref[...] = pack(sum_ref[...])

    project(send_ref, split_ref, slab_ref, owner_ref[0], 1, 8)


def project_kernel(parts, owner_ref, split_ref, slab_ref, *out_refs):
    for (sibling, first_place), out_ref in zip(parts, out_refs):
        project(out_ref, split_ref, slab_ref, owner_ref[0], sibling, first_place)


def project_call(owner, split, slab, parts, name):
    rows, width = slab.shape
    rank = split.shape[0] // 2
    vmem = pl.BlockSpec(memory_space=pltpu.VMEM)
    chunks = jax.ShapeDtypeStruct((width // (4 * LANES), rank, LANES), jnp.float32)
    return pl.pallas_call(
        functools.partial(project_kernel, parts),
        in_specs=[pl.BlockSpec(memory_space=pltpu.SMEM), vmem, vmem],
        out_specs=[vmem] * len(parts),
        out_shape=[chunks] * len(parts),
        compiler_params=pltpu.CompilerParams(vmem_limit_bytes=VMEM_LIMIT),
        cost_estimate=pl.CostEstimate(
            flops=len(parts) * rows * width * rank, bytes_accessed=rows * width, transcendentals=0
        ),
        name=name,
    )(owner, split, slab)


def rows_call(owner, slab, sketch):
    rows, width = slab.shape
    rank = sketch.shape[1]
    vmem = pl.BlockSpec(memory_space=pltpu.VMEM)
    chunks = (width // (4 * LANES), rank, LANES)
    return pl.pallas_call(
        rows_kernel,
        in_specs=[
            pl.BlockSpec(memory_space=pltpu.SMEM),
            pl.BlockSpec(memory_space=pltpu.HBM),
            pl.BlockSpec(memory_space=pltpu.HBM),
        ],
        out_specs=[vmem] * 5,
        out_shape=[
            jax.ShapeDtypeStruct((rows, width), jnp.bfloat16),
            jax.ShapeDtypeStruct((rows, rank), jnp.float32),
            jax.ShapeDtypeStruct((rank // 2 + 8, rank), jnp.float32),
            jax.ShapeDtypeStruct((2 * rank, rows), jnp.bfloat16),
            jax.ShapeDtypeStruct(chunks, jnp.float32),
        ],
        scratch_shapes=[
            pltpu.VMEM((width, rank), jnp.bfloat16),
            pltpu.VMEM((rank, rank), jnp.float32),
            pltpu.SemaphoreType.DMA((-(-rows // ROWS),)),
            pltpu.SemaphoreType.DMA,
        ],
        compiler_params=pltpu.CompilerParams(vmem_limit_bytes=VMEM_LIMIT),
        cost_estimate=pl.CostEstimate(
            flops=3 * rows * width * rank, bytes_accessed=rows * width * 2, transcendentals=0
        ),
        name="sketch_rows",
    )(
        owner,
        pltpu.with_memory_space_constraint(slab, pltpu.HBM),
        pltpu.with_memory_space_constraint(sketch, pltpu.HBM),
    )


def lane(block, at):
    return jnp.broadcast_to(block[:, at : at + 1], block.shape)


def sublane(block, at):
    return jnp.broadcast_to(block[at : at + 1, :], block.shape)


def inverse_factor(gram, inverse_ref):
    size = gram.shape[0]
    blocks = [gram[i : i + 8, :] for i in range(0, size, 8)]
    row_at = lax.broadcasted_iota(jnp.int32, (8, size), 0)
    lane_at = lax.broadcasted_iota(jnp.int32, (8, size), 1)
    for p in range(len(blocks)):
        start = 8 * p
        column = [lane(blocks[p], start + k) for k in range(8)]
        entry = {(r, c): sublane(column[c], r) for c in range(8) for r in range(c, 8)}
        root, lower = [], {}
        for k in range(0, 8, 2):
            first, side, second = entry[k, k], entry[k + 1, k], entry[k + 1, k + 1]
            one = lax.rsqrt(first)
            two = lax.rsqrt(first * second - side * side) * (first * one)
            root += [one, two]
            lower[k + 1, k] = side * one
            for r in range(k + 2, 8):
                lower[r, k] = entry[r, k] * one
                lower[r, k + 1] = (entry[r, k + 1] - lower[r, k] * lower[k + 1, k]) * two
            for c in range(k + 2, 8):
                for r in range(c, 8):
                    pair = lower[r, k] * lower[c, k] + lower[r, k + 1] * lower[c, k + 1]
                    entry[r, c] = entry[r, c] - pair
        in_panel = (lane_at >= start) & (lane_at < start + 8)
        unit = jnp.where(lane_at - start == row_at, 1.0, 0.0)
        panel = jnp.where(in_panel, unit, blocks[p])
        tops = []
        for k in range(8):
            top = sublane(panel, k)
            for j in range(k):
                top = top - lower[k, j] * tops[j]
            tops.append(top * root[k])
        result = tops[0]
        for k in range(1, 8):
            result = jnp.where(row_at == k, tops[k], result)
        inverse_ref[start : start + 8, :] = jnp.where(lane_at < start + 8, result, 0.0)
        for i in range(p + 1, len(blocks)):
            block = jnp.where(in_panel, 0.0, blocks[i])
            weights = []
            for k in range(8):
                weight = lane(blocks[i], start + k)
                for j in range(k):
                    weight = weight - lower[k, j] * weights[j]
                weights.append(weight * root[k])
                block = block - weights[k] * tops[k]
            blocks[i] = block


def factor_kernel(gram_ref, got_ref, inverse_ref):
    inverse_factor(unpack(gram_ref[...] + got_ref[...]), inverse_ref)


def factor_call(gram, got):
    return pl.pallas_call(
        factor_kernel,
        in_specs=[pl.BlockSpec(memory_space=pltpu.VMEM)] * 2,
        out_specs=pl.BlockSpec(memory_space=pltpu.VMEM),
        out_shape=jax.ShapeDtypeStruct((gram.shape[1], gram.shape[1]), jnp.float32),
        compiler_params=pltpu.CompilerParams(vmem_limit_bytes=VMEM_LIMIT),
        cost_estimate=pl.CostEstimate(
            flops=4000000000, bytes_accessed=gram.size * 8, transcendentals=gram.shape[0]
        ),
        name="factor",
    )(gram, got)


def two_parts(array):
    high = array.astype(jnp.bfloat16)
    return high, (array - high.astype(jnp.float32)).astype(jnp.bfloat16)


def finish_kernel(basis_factor, factor, inverse_ref, first_ref, sums_ref, *refs):
    basis_ref, out_ref = refs[-2:]
    sums = sums_ref[...]
    for got_ref in refs[:-2]:
        sums = sums + got_ref[...]
    inverse_high, inverse_low = two_parts(inverse_ref[...].T * basis_factor)
    factors = jnp.concatenate([inverse_high, inverse_low, inverse_high, inverse_low], axis=0)

    def product(rows):
        high, low = two_parts(rows)
        return jnp.dot(
            jnp.concatenate([high, high, low, low], axis=1), factors,
            preferred_element_type=jnp.float32,
        )

    out_ref[...] = (product(sums.T) * (factor / basis_factor)).astype(out_ref.dtype)
    basis_ref[...] = product(first_ref[...])


def finish_call(inverse, first, total_rows, factor, sums):
    rows, rank = first.shape
    own = sums[0].shape[1]
    return pl.pallas_call(
        functools.partial(finish_kernel, float(total_rows) ** 0.5, factor),
        in_specs=[pl.BlockSpec(memory_space=pltpu.VMEM)] * (2 + len(sums)),
        out_shape=[
            jax.ShapeDtypeStruct((rows, rank), jnp.float32),
            jax.ShapeDtypeStruct((own, rank), jnp.bfloat16),
        ],
        compiler_params=pltpu.CompilerParams(vmem_limit_bytes=VMEM_LIMIT),
        cost_estimate=pl.CostEstimate(
            flops=12 * rows * rank * rank, bytes_accessed=rows * rank * 8, transcendentals=0
        ),
        name="finish",
    )(inverse, first, *sums)


def local(slab, sketch):
    rows_loc, width = slab.shape
    devices_all = lax.axis_size(AXES)
    own = width // devices_all
    bits = devices_all.bit_length() - 1
    low_bits = bits - ((width // LANES).bit_length() - 1)
    total_rows = rows_loc * devices_all
    me = lax.axis_index(AXES)

    core, x, y, z, zz = [1 << bit for bit in range(low_bits, low_bits + 5)]
    tie = lax.optimization_barrier

    def exchange(array, away, away_odd=None):
        odd = away if away_odd is None else away_odd
        pairs = [(i, i ^ (odd if i & core else away)) for i in range(devices_all)]
        return lax.ppermute(array, AXES, pairs)

    owner = lax.shift_right_logical(me, low_bits).astype(jnp.int32).reshape(1)
    near, first, gram, split, send = rows_call(owner, slab, sketch)
    got = exchange(send, core)
    keep, = project_call(owner, split, near, ((0, 8),), "project_first")
    got, gram = tie((got, gram + exchange(gram, core)))
    far, split = tie((keep + got, split))
    got = exchange(far, x, y)
    send, sums = project_call(owner, split, near, ((1, 0), (0, 0)), "project_rest")
    sums = sums + exchange(send, core)
    over_z = [exchange(gram, away) for away in (z | zz, zz, z)]
    got, over_z[0] = tie((got, over_z[0]))
    sums, gram = tie((sums + got, gram))
    got = exchange(sums[4:], y, x)
    gram = (gram + over_z[2]) + (over_z[1] + over_z[0])
    gram = gram + exchange(gram, x, y)
    got, _ = tie((got, gram))
    got_gram = exchange(gram, y, x)
    sums, gram = tie((sums[:4] + got, gram))
    over_z = [exchange(sums[i], away) for i, away in ((1, z), (2, zz), (3, z | zz))]
    for bit in range(low_bits):
        gram = gram + got_gram
        got_gram = exchange(gram, 1 << bit)
    sums, gram = tie((sums, gram))
    inverse = factor_call(gram, got_gram)
    sums = [sums[0], *over_z]
    if low_bits > 0:
        sums = sum(sums)
        for bit in reversed(range(low_bits)):
            half = sums.shape[1] // 2
            mine = lax.rem(lax.shift_right_logical(me, bit), 2) == 1
            left, right = sums[:, :half], sums[:, half:]
            sums = jnp.where(mine, right, left) + exchange(jnp.where(mine, left, right), 1 << bit)
        sums = [sums]
    factor = (float(width) / float(total_rows)) ** 0.5
    return tuple(finish_call(inverse, first, total_rows, factor, sums))


def solution(mesh):
    return jax.shard_map(
        local,
        mesh=mesh,
        in_specs=(P(AXES, None), P()),
        out_specs=(P(AXES, None), P(AXES, None)),
        check_vma=False,
    )
```

```python
import functools

import jax
import jax.numpy as jnp
from jax import lax
from jax.experimental import pallas as pl
from jax.experimental.pallas import tpu as pltpu
from jax.sharding import PartitionSpec as P

AXES = ("rows", "grp")
HIGHEST = lax.Precision.HIGHEST
LANES = 128
VMEM_LIMIT = 24 * 1024 * 1024
AHEAD = 2
ROWS = 256


def project(out_ref, split_ref, slab_ref, owner, sibling, first_place):
    rank = out_ref.shape[1]
    wanted = lax.bitwise_xor(lax.bitwise_and(owner, 1), sibling)
    mine = lax.shift_right_logical(owner, 1)

    def columns(place):
        one, two = place // 8, place // 4 % 2
        away = jnp.where(wanted == 0, one + 2 * two, two + 2 * one) + 4 * (place % 4)
        at = pl.multiple_of((2 * lax.bitwise_xor(mine, away) + wanted) * LANES, LANES)
        return slab_ref[:, pl.ds(at, LANES)]

    for i in range(0, out_ref.shape[0], 2):
        place = first_place + i
        both = jnp.dot(
            split_ref[...], jnp.concatenate([columns(place), columns(place + 1)], axis=1),
            preferred_element_type=jnp.float32,
        )
        sums = both[:rank] + both[rank:]
        out_ref[i] = sums[:, :LANES]
        out_ref[i + 1] = sums[:, LANES:]


def pack(gram):
    half = gram.shape[0] // 2
    top, bottom = gram[:half], gram[half:]
    row = lax.broadcasted_iota(jnp.int32, top.shape, 0)
    column = lax.broadcasted_iota(jnp.int32, top.shape, 1)
    body = jnp.where(column - half < row, jnp.where(column < half, bottom, pltpu.roll(top, half, 1)), bottom)
    diagonal = jnp.sum(jnp.where(row == column, top, 0.0), axis=0, keepdims=True)
    tail = jnp.where(row[:8] == 0, jnp.broadcast_to(diagonal, (8, diagonal.shape[1])), 0.0)
    return jnp.concatenate([body, tail], axis=0)


def unpack(packed):
    half = packed.shape[0] - 8
    body = packed[:half]
    row = lax.broadcasted_iota(jnp.int32, body.shape, 0)
    column = lax.broadcasted_iota(jnp.int32, body.shape, 1)
    diagonal = jnp.broadcast_to(packed[half : half + 1], body.shape)
    top = jnp.where(column < row, pltpu.roll(body, half, 1), jnp.where(column == row, diagonal, 0.0))
    bottom = jnp.where(column - half < row, jnp.where(column < half, body, 0.0), body)
    parts = jnp.concatenate([top, bottom], axis=0)
    row = lax.broadcasted_iota(jnp.int32, parts.shape, 0)
    column = lax.broadcasted_iota(jnp.int32, parts.shape, 1)
    return parts + jnp.where(row == column, 0.0, parts.T)


def rows_kernel(
    owner_ref, slab_hbm, sketch_hbm, slab_ref, first_ref, gram_ref, split_ref, send_ref,
    sketch_ref, sum_ref, slab_sem, sketch_sem,
):
    rows, width = slab_ref.shape
    rank = sketch_ref.shape[1]
    starts = list(range(0, rows, ROWS))
    copies = [
        pltpu.make_async_copy(
            slab_hbm.at[pl.ds(r, min(ROWS, rows - r)), :],
            slab_ref.at[pl.ds(r, min(ROWS, rows - r)), :],
            slab_sem.at[k],
        )
        for k, r in enumerate(starts)
    ]
    sketch_copy = pltpu.make_async_copy(sketch_hbm, sketch_ref, sketch_sem)
    sketch_copy.start()
    copies[0].start()
    sketch_copy.wait()
    for copy in copies[1:AHEAD]:
        copy.start()
    for k, r in enumerate(starts):
        copies[k].wait()
        if k + AHEAD < len(starts):
            copies[k + AHEAD].start()
        at = pl.ds(r, min(ROWS, rows - r))
        first = jnp.dot(slab_ref[at, :], sketch_ref[...], preferred_element_type=jnp.float32)
        first_ref[at, :] = first
        turned = first.T
        high = turned.astype(jnp.bfloat16)
        split_ref[:rank, at] = high
        split_ref[rank:, at] = (turned - high.astype(jnp.float32)).astype(jnp.bfloat16)
        gram = jnp.dot(turned, first, precision=HIGHEST, preferred_element_type=jnp.float32)
        if k == 0:
            sum_ref[...] = gram
        else:
            sum_ref[...] += gram
    gram_ref[...] = pack(sum_ref[...])

    project(send_ref, split_ref, slab_ref, owner_ref[0], 1, 8)


def project_kernel(parts, owner_ref, split_ref, slab_ref, *out_refs):
    for (sibling, first_place), out_ref in zip(parts, out_refs):
        project(out_ref, split_ref, slab_ref, owner_ref[0], sibling, first_place)


def project_call(owner, split, slab, parts, name):
    rows, width = slab.shape
    rank = split.shape[0] // 2
    vmem = pl.BlockSpec(memory_space=pltpu.VMEM)
    chunks = jax.ShapeDtypeStruct((width // (4 * LANES), rank, LANES), jnp.float32)
    return pl.pallas_call(
        functools.partial(project_kernel, parts),
        in_specs=[pl.BlockSpec(memory_space=pltpu.SMEM), vmem, vmem],
        out_specs=[vmem] * len(parts),
        out_shape=[chunks] * len(parts),
        compiler_params=pltpu.CompilerParams(vmem_limit_bytes=VMEM_LIMIT),
        cost_estimate=pl.CostEstimate(
            flops=len(parts) * rows * width * rank, bytes_accessed=rows * width, transcendentals=0
        ),
        name=name,
    )(owner, split, slab)


def rows_call(owner, slab, sketch):
    rows, width = slab.shape
    rank = sketch.shape[1]
    vmem = pl.BlockSpec(memory_space=pltpu.VMEM)
    chunks = (width // (4 * LANES), rank, LANES)
    return pl.pallas_call(
        rows_kernel,
        in_specs=[
            pl.BlockSpec(memory_space=pltpu.SMEM),
            pl.BlockSpec(memory_space=pltpu.HBM),
            pl.BlockSpec(memory_space=pltpu.HBM),
        ],
        out_specs=[vmem] * 5,
        out_shape=[
            jax.ShapeDtypeStruct((rows, width), jnp.bfloat16),
            jax.ShapeDtypeStruct((rows, rank), jnp.float32),
            jax.ShapeDtypeStruct((rank // 2 + 8, rank), jnp.float32),
            jax.ShapeDtypeStruct((2 * rank, rows), jnp.bfloat16),
            jax.ShapeDtypeStruct(chunks, jnp.float32),
        ],
        scratch_shapes=[
            pltpu.VMEM((width, rank), jnp.bfloat16),
            pltpu.VMEM((rank, rank), jnp.float32),
            pltpu.SemaphoreType.DMA((-(-rows // ROWS),)),
            pltpu.SemaphoreType.DMA,
        ],
        compiler_params=pltpu.CompilerParams(vmem_limit_bytes=VMEM_LIMIT),
        cost_estimate=pl.CostEstimate(
            flops=3 * rows * width * rank, bytes_accessed=rows * width * 2, transcendentals=0
        ),
        name="sketch_rows",
    )(
        owner,
        pltpu.with_memory_space_constraint(slab, pltpu.HBM),
        pltpu.with_memory_space_constraint(sketch, pltpu.HBM),
    )


def lane(block, at):
    return jnp.broadcast_to(block[:, at : at + 1], block.shape)


def sublane(block, at):
    return jnp.broadcast_to(block[at : at + 1, :], block.shape)


def inverse_factor(gram, inverse_ref):
    size = gram.shape[0]
    blocks = [gram[i : i + 8, :] for i in range(0, size, 8)]
    row_at = lax.broadcasted_iota(jnp.int32, (8, size), 0)
    lane_at = lax.broadcasted_iota(jnp.int32, (8, size), 1)
    for p in range(len(blocks)):
        start = 8 * p
        column = [lane(blocks[p], start + k) for k in range(8)]
        entry = {(r, c): sublane(column[c], r) for c in range(8) for r in range(c, 8)}
        root, lower = [], {}
        for k in range(0, 8, 2):
            first, side, second = entry[k, k], entry[k + 1, k], entry[k + 1, k + 1]
            one = lax.rsqrt(first)
            two = lax.rsqrt(first * second - side * side) * (first * one)
            root += [one, two]
            lower[k + 1, k] = side * one
            for r in range(k + 2, 8):
                lower[r, k] = entry[r, k] * one
                lower[r, k + 1] = (entry[r, k + 1] - lower[r, k] * lower[k + 1, k]) * two
            for c in range(k + 2, 8):
                for r in range(c, 8):
                    pair = lower[r, k] * lower[c, k] + lower[r, k + 1] * lower[c, k + 1]
                    entry[r, c] = entry[r, c] - pair
        in_panel = (lane_at >= start) & (lane_at < start + 8)
        unit = jnp.where(lane_at - start == row_at, 1.0, 0.0)
        panel = jnp.where(in_panel, unit, blocks[p])
        tops = []
        for k in range(8):
            top = sublane(panel, k)
            for j in range(k):
                top = top - lower[k, j] * tops[j]
            tops.append(top * root[k])
        result = tops[0]
        for k in range(1, 8):
            result = jnp.where(row_at == k, tops[k], result)
        inverse_ref[start : start + 8, :] = jnp.where(lane_at < start + 8, result, 0.0)
        for i in range(p + 1, len(blocks)):
            block = jnp.where(in_panel, 0.0, blocks[i])
            weights = []
            for k in range(8):
                weight = lane(blocks[i], start + k)
                for j in range(k):
                    weight = weight - lower[k, j] * weights[j]
                weights.append(weight * root[k])
                block = block - weights[k] * tops[k]
            blocks[i] = block


def factor_kernel(gram_ref, got_ref, inverse_ref):
    inverse_factor(unpack(gram_ref[...] + got_ref[...]), inverse_ref)


def factor_call(gram, got):
    return pl.pallas_call(
        factor_kernel,
        in_specs=[pl.BlockSpec(memory_space=pltpu.VMEM)] * 2,
        out_specs=pl.BlockSpec(memory_space=pltpu.VMEM),
        out_shape=jax.ShapeDtypeStruct((gram.shape[1], gram.shape[1]), jnp.float32),
        compiler_params=pltpu.CompilerParams(vmem_limit_bytes=VMEM_LIMIT),
        cost_estimate=pl.CostEstimate(
            flops=4000000000, bytes_accessed=gram.size * 8, transcendentals=gram.shape[0]
        ),
        name="factor",
    )(gram, got)


def two_parts(array):
    high = array.astype(jnp.bfloat16)
    return high, (array - high.astype(jnp.float32)).astype(jnp.bfloat16)


def finish_kernel(basis_factor, factor, inverse_ref, first_ref, sums_ref, *refs):
    basis_ref, out_ref = refs[-2:]
    sums = sums_ref[...]
    for got_ref in refs[:-2]:
        sums = sums + got_ref[...]
    inverse_high, inverse_low = two_parts(inverse_ref[...].T * basis_factor)
    factors = jnp.concatenate([inverse_high, inverse_low, inverse_high, inverse_low], axis=0)

    def product(rows):
        high, low = two_parts(rows)
        return jnp.dot(
            jnp.concatenate([high, high, low, low], axis=1), factors,
            preferred_element_type=jnp.float32,
        )

    out_ref[...] = (product(sums.T) * (factor / basis_factor)).astype(out_ref.dtype)
    basis_ref[...] = product(first_ref[...])


def finish_call(inverse, first, total_rows, factor, sums):
    rows, rank = first.shape
    own = sums[0].shape[1]
    return pl.pallas_call(
        functools.partial(finish_kernel, float(total_rows) ** 0.5, factor),
        in_specs=[pl.BlockSpec(memory_space=pltpu.VMEM)] * (2 + len(sums)),
        out_shape=[
            jax.ShapeDtypeStruct((rows, rank), jnp.float32),
            jax.ShapeDtypeStruct((own, rank), jnp.bfloat16),
        ],
        compiler_params=pltpu.CompilerParams(vmem_limit_bytes=VMEM_LIMIT),
        cost_estimate=pl.CostEstimate(
            flops=12 * rows * rank * rank, bytes_accessed=rows * rank * 8, transcendentals=0
        ),
        name="finish",
    )(inverse, first, *sums)


def local(slab, sketch):
    rows_loc, width = slab.shape
    devices_all = lax.axis_size(AXES)
    own = width // devices_all
    bits = devices_all.bit_length() - 1
    low_bits = bits - ((width // LANES).bit_length() - 1)
    total_rows = rows_loc * devices_all
    me = lax.axis_index(AXES)

    core, x, y, z, zz = [1 << bit for bit in range(low_bits, low_bits + 5)]
    tie = lax.optimization_barrier

    def exchange(array, away, away_odd=None):
        odd = away if away_odd is None else away_odd
        pairs = [(i, i ^ (odd if i & core else away)) for i in range(devices_all)]
        return lax.ppermute(array, AXES, pairs)

    owner = lax.shift_right_logical(me, low_bits).astype(jnp.int32).reshape(1)
    near, first, gram, split, send = rows_call(owner, slab, sketch)
    got = exchange(send, core)
    keep, = project_call(owner, split, near, ((0, 8),), "project_first")
    got, gram = tie((got, gram + exchange(gram, core)))
    far, split = tie((keep + got, split))
    got = exchange(far, x, y)
    send, sums = project_call(owner, split, near, ((1, 0), (0, 0)), "project_rest")
    sums = sums + exchange(send, core)
    over_z = [exchange(gram, away) for away in (z | zz, zz, z)]
    got, over_z[0] = tie((got, over_z[0]))
    sums, gram = tie((sums + got, gram))
    got = exchange(sums[4:], y, x)
    gram = (gram + over_z[2]) + (over_z[1] + over_z[0])
    gram = gram + exchange(gram, x, y)
    got, _ = tie((got, gram))
    got_gram = exchange(gram, y, x)
    sums, gram = tie((sums[:4] + got, gram))
    over_z = [exchange(sums[i], away) for i, away in ((1, z), (2, zz), (3, z | zz))]
    for bit in range(low_bits):
        gram = gram + got_gram
        got_gram = exchange(gram, 1 << bit)
    sums, gram = tie((sums, gram))
    inverse = factor_call(gram, got_gram)
    sums = [sums[0], *over_z]
    if low_bits > 0:
        sums = sum(sums)
        for bit in reversed(range(low_bits)):
            half = sums.shape[1] // 2
            mine = lax.rem(lax.shift_right_logical(me, bit), 2) == 1
            left, right = sums[:, :half], sums[:, half:]
            sums = jnp.where(mine, right, left) + exchange(jnp.where(mine, left, right), 1 << bit)
        sums = [sums]
    factor = (float(width) / float(total_rows)) ** 0.5
    return tuple(finish_call(inverse, first, total_rows, factor, sums))


def solution(mesh):
    return jax.shard_map(
        local,
        mesh=mesh,
        in_specs=(P(AXES, None), P()),
        out_specs=(P(AXES, None), P(AXES, None)),
        check_vma=False,
    )
```
